256 devices in a mesh: lon: 16 (over x_lo, y, core), lev: 8 (over z), lat: 2 (over x_hi).
Axes of the slice: x: 4 (x_hi: 2, x_lo: 2; x = x_hi * 2 + x_lo), y: 4, z: 8, core: 2. Of those that a mesh axis runs over, the one named last changes fastest.
Arguments:
- tokens: bfloat16 [8, 12, 384, 1024], P('lev', 'lat', 'lon'), may hold values from -60 to 60
- norm_gain: float32 [2, 1024], replicated, may hold values from 0.1 to 1.9
- qkv_weight: bfloat16 [2, 1024, 3, 1024], P(None, None, None, 'lev'), may hold values from -0.1875 to 0.1875
- out_weight: bfloat16 [2, 1024, 1024], P(None, 'lev'), may hold values from -0.1875 to 0.1875
- bias_table: float32 [2, 16, 759], P(None, 'lev'), may hold values from -3 to 320
- rel_index: int32 [144, 144], replicated, may hold values from 0 to 758, as said below
- region_ids: int32 [12, 384], P('lat', 'lon'), may hold values from 0 to 2
- row_valid: int32 [12], P('lat'), may hold values from 0 to 1, as said below
- grad_out: bfloat16 [8, 12, 384, 1024], P('lev', 'lat', 'lon'), may hold values from -6 to 6
Outputs:
- output: bfloat16 [8, 12, 384, 1024], P('lev', 'lat', 'lon')
- grad_tokens: bfloat16 [8, 12, 384, 1024], P('lev', 'lat', 'lon')
- grad_qkv: float32 [2, 1024, 3, 1024], P(None, None, None, 'lev')
- grad_out_weight: float32 [2, 1024, 1024], P(None, 'lev')
- grad_bias: float32 [2, 16, 759], P(None, 'lev')
The draws below stay inside these ranges and needn't reach their ends.
Inputs may be any that keep to these rules, and one draw needn't show every extreme that they name: `rel_index`: entry (p, k) names the bias slot of the offset between window positions p and k: equal offsets share a slot and different offsets have different slots. `row_valid`: 1 marks a latitude row inside the grid, 0 a padding row; the padding rows are the last 1 to 3 rows of the slab.
All inputs are finite; a program needn't handle non-finite values.
Results may differ from the reference program's by a relative error of at most 0.035.
Values may be sent and summed in bfloat16 or wider, within the bound.
No kernel may reach another device: no remote copies, remote signals or barrier semaphores. Data moves between devices by JAX's collectives and lax.ppermute only.
A program may use at most 128 MiB of HBM per device.

```python
import jax
import jax.numpy as jnp
from jax import lax

C = 1024
HEADS = 16
WL = 2
WH = 6
WW = 12
BLOCKS = 2
LEVELS = 8
ROWS = 12
LON = 384
SLOTS = 759
N_LEV = 8


def slot_order(key):
    return jax.random.permutation(key, SLOTS)


def standard_offsets():
    position = jnp.arange(WL * WH * WW)
    level_pos = position // (WH * WW)
    row_pos = position // WW % WH
    column_pos = position % WW
    level_step = level_pos[:, None] - level_pos[None, :] + WL - 1
    row_step = row_pos[:, None] - row_pos[None, :] + WH - 1
    column_step = column_pos[:, None] - column_pos[None, :] + WW - 1
    return (level_step * (2 * WH - 1) + row_step) * (2 * WW - 1) + column_step


def draw_rel_index(key, part):
    order = slot_order(key)
    return order[standard_offsets()].astype(jnp.int32)


def draw_bias_table(key, part):
    key = jax.random.fold_in(key, 13)
    table = jax.random.uniform(key, (BLOCKS, HEADS, SLOTS), jnp.float32, -3.0, 3.0)
    return table


def draw_tokens(key, part):
    key = jax.random.fold_in(key, 7)
    first_key = jax.random.fold_in(key, 0)
    base = jax.random.normal(first_key, (LEVELS, ROWS, LON, C), jnp.float32)
    return jnp.clip(base, -6.0, 6.0).astype(jnp.bfloat16)


def draw_row_valid(key, part):
    key = jax.random.fold_in(key, 5)
    padding = jax.random.randint(key, (), 1, 4)
    return (jnp.arange(ROWS) < ROWS - padding).astype(jnp.int32)


def place_ends(drawn, key, least, largest):
    shape = drawn.shape
    spot = [jax.random.randint(jax.random.fold_in(key, axis), (), 0, shape[axis]) for axis in range(len(shape))]
    drawn = drawn.at[tuple(spot)].set(least)
    longest = shape.index(max(shape))
    spot[longest] = (spot[longest] + 1) % shape[longest]
    return drawn.at[tuple(spot)].set(largest)


def shard_levels(key, extent, cuts, low, largest):
    gain, own = 1.0, jax.random.fold_in(key, 6)
    for dim, blocks in cuts:
        heights = jnp.exp(jax.random.uniform(jax.random.fold_in(own, dim), (blocks,), jnp.float32, low / len(cuts), largest / len(cuts)))
        gain = gain * jnp.repeat(heights, extent[dim] // blocks).reshape([-1 if axis == dim else 1 for axis in range(len(extent))])
    return gain


def noise(rng, extent, deviation, most, shards=(), kind=jnp.bfloat16):
    factor_of = shard_levels(rng, extent, shards, -0.22, 0.18) if shards else 1.0
    entries = jax.random.normal(rng, extent, jnp.float32) * deviation * factor_of
    return jnp.minimum(jnp.maximum(entries, -most), most).astype(kind)


def setup_inputs(seed: int = 0) -> dict:
    streams_of = jax.random.split(jax.random.key(seed), 10)
    return {
        "tokens": draw_tokens(jax.random.fold_in(streams_of[9], 71), 0),
        "norm_gain": jnp.clip(1.0 + 0.18 * jax.random.normal(streams_of[1], (BLOCKS, C), jnp.float32), 0.1, 1.9),
        "qkv_weight": noise(streams_of[2], (BLOCKS, C, 3, C), C ** -0.5, 0.1875, ((3, 8),)),
        "out_weight": noise(streams_of[3], (BLOCKS, C, C), C ** -0.5, 0.1875, ((1, 8),)),
        "bias_table": draw_bias_table(jax.random.fold_in(streams_of[9], 71), 0),
        "rel_index": draw_rel_index(jax.random.fold_in(streams_of[9], 71), 0),
        "region_ids": place_ends(jax.random.randint(streams_of[6], (ROWS, LON), 0, 3), jax.random.fold_in(streams_of[6], 1), 0, 2).astype(jnp.int32),
        "row_valid": draw_row_valid(jax.random.fold_in(streams_of[9], 71), 0),
        "grad_out": noise(streams_of[8], (LEVELS, ROWS, LON, C), 1.0, 6.0, ((0, 8), (1, 2), (2, 16))),
    }


EPSILON = 1e-05
MASKED = -1e+30

def layer_norm(field, scale):
    values = field.astype(jnp.float32)
    centre = lax.optimization_barrier(jnp.mean(values, axis=-1, keepdims=True))
    spread = lax.optimization_barrier(jnp.mean((values - centre) ** 2, axis=-1, keepdims=True))
    inv_spread = lax.rsqrt(spread + EPSILON)
    normed = (values - centre) * inv_spread
    return ((normed * scale).astype(jnp.bfloat16), normed, inv_spread)

def norm_adjoint(cotan, normed, inv_spread, scale):
    scaled = cotan * scale
    first = lax.optimization_barrier(jnp.mean(scaled, axis=-1, keepdims=True))
    second = lax.optimization_barrier(jnp.mean(scaled * normed, axis=-1, keepdims=True))
    return inv_spread * (scaled - first - normed * second)

def to_windows(field):
    levels, rows, columns = field.shape[:3]
    rest = field.shape[3:]
    split = field.reshape((levels // WL, WL, rows // WH, WH, columns // WW, WW) + rest)
    order = (0, 2, 4, 1, 3, 5) + tuple(range(6, 6 + len(rest)))
    return split.transpose(order).reshape((-1, WL * WH * WW) + rest)

def from_windows(windows, levels, rows, columns):
    rest = windows.shape[2:]
    split = windows.reshape((levels // WL, rows // WH, columns // WW, WL, WH, WW) + rest)
    order = (0, 3, 1, 4, 2, 5) + tuple(range(6, 6 + len(rest)))
    return split.transpose(order).reshape((levels, rows, columns) + rest)

def allowed_pairs(labels, row_valid, levels):
    rows, columns = labels.shape
    marks = to_windows(jnp.broadcast_to(labels[None], (levels, rows, columns)))
    living = to_windows(jnp.broadcast_to(row_valid[None, :, None], (levels, rows, columns))) > 0
    same = marks[:, :, None] == marks[:, None, :]
    diagonal = jnp.eye(marks.shape[1], dtype=bool)
    return same & (living[:, None, :] | diagonal[None])

def unpack(packed, levels, rows, columns, heads_local):
    local = packed.shape[-1] // 3
    head_dim = local // heads_local
    windows = to_windows(packed.reshape(levels, rows, columns, 3 * local))
    parts = windows.reshape(windows.shape[0], windows.shape[1], 3, heads_local, head_dim)
    return tuple((parts[:, :, index].transpose(0, 2, 1, 3) for index in range(3)))

def pack_heads(mixed, levels, rows, columns):
    count, heads_local, span, head_dim = mixed.shape
    joined = mixed.transpose(0, 2, 1, 3).reshape(count, span, heads_local * head_dim)
    return from_windows(joined, levels, rows, columns)

def repack(grad_query, grad_key, grad_value, levels, rows, columns):
    pieces = [pack_heads(item, levels, rows, columns) for item in (grad_query, grad_key, grad_value)]
    joined = jnp.concatenate(pieces, axis=-1)
    return joined.reshape(-1, joined.shape[-1])

def attend_probs(query, key_rows, bias, allowed):
    scale = query.shape[-1] ** (-0.5)
    scores = jnp.einsum('nhqd,nhkd->nhqk', query.astype(jnp.float32), key_rows.astype(jnp.float32)) * scale + bias[None]
    scores = jnp.where(allowed[:, None], scores, MASKED)
    top = lax.optimization_barrier(jnp.max(scores, axis=-1, keepdims=True))
    weights = jnp.exp(scores - top)
    return weights / lax.optimization_barrier(jnp.sum(weights, axis=-1, keepdims=True))

def mix_values(probs, value):
    low = probs.astype(jnp.bfloat16).astype(jnp.float32)
    return jnp.einsum('nhqk,nhkd->nhqd', low, value.astype(jnp.float32)).astype(jnp.bfloat16)

def attend_backward(query, key_rows, value, probs, cotan):
    scale = query.shape[-1] ** (-0.5)
    probs_low = probs.astype(jnp.bfloat16).astype(jnp.float32)
    cotan_f = cotan.astype(jnp.float32)
    grad_probs = jnp.einsum('nhqd,nhkd->nhqk', cotan_f, value.astype(jnp.float32))
    grad_value = jnp.einsum('nhqk,nhqd->nhkd', probs_low, cotan_f).astype(jnp.bfloat16)
    inner = lax.optimization_barrier(jnp.sum(grad_probs * probs, axis=-1, keepdims=True))
    grad_scores = probs * (grad_probs - inner)
    grad_low = grad_scores.astype(jnp.bfloat16).astype(jnp.float32)
    grad_query = (jnp.einsum('nhqk,nhkd->nhqd', grad_low, key_rows.astype(jnp.float32)) * scale).astype(jnp.bfloat16)
    grad_key = (jnp.einsum('nhqk,nhqd->nhkd', grad_low, query.astype(jnp.float32)) * scale).astype(jnp.bfloat16)
    return (grad_query, grad_key, grad_value, lax.optimization_barrier(jnp.sum(grad_scores, axis=0)))

def slot_sums(grad_scores, rel_index, slots):
    flat = grad_scores.reshape(grad_scores.shape[0], -1).T
    return jax.ops.segment_sum(flat, rel_index.reshape(-1), num_segments=slots).T

def reference(tokens, norm_gain, qkv_weight, out_weight, bias_table, rel_index, region_ids, row_valid, grad_out):
    levels, rows, columns, width = tokens.shape
    groups = N_LEV
    local = width // groups
    heads_local = HEADS // groups
    reach = WW // 2
    saved = []
    field = tokens
    for block in range(BLOCKS):
        normed_low, normed, inv_spread = layer_norm(field, norm_gain[block])
        labels = region_ids
        if block % 2 == 1:
            normed_low = jnp.roll(normed_low, -reach, axis=2)
            labels = jnp.roll(region_ids, -reach, axis=1)
        allowed = allowed_pairs(labels, row_valid, levels)
        flat = normed_low.reshape(-1, width)
        total = jnp.zeros((flat.shape[0], width), jnp.float32)
        for group in range(groups):
            in_matrix = qkv_weight[block, :, :, group * local:(group + 1) * local].reshape(width, 3 * local)
            packed = jnp.dot(flat, in_matrix, preferred_element_type=jnp.float32).astype(jnp.bfloat16)
            query, key_rows, value = unpack(packed, levels, rows, columns, heads_local)
            bias = jnp.take(bias_table[block, group * heads_local:(group + 1) * heads_local], rel_index, axis=1)
            probs = attend_probs(query, key_rows, bias, allowed)
            mixed = pack_heads(mix_values(probs, value), levels, rows, columns).reshape(-1, local)
            part_sum = jnp.dot(mixed, out_weight[block, group * local:(group + 1) * local], preferred_element_type=jnp.float32)
            total = total + part_sum.astype(jnp.bfloat16).astype(jnp.float32)
        branch = total.astype(jnp.bfloat16).reshape(levels, rows, columns, width)
        if block % 2 == 1:
            branch = jnp.roll(branch, reach, axis=2)
        saved.append((normed, inv_spread, normed_low, labels))
        field = (field.astype(jnp.float32) + branch.astype(jnp.float32)).astype(jnp.bfloat16)
    output = field
    carry = grad_out.astype(jnp.float32)
    qkv_list, out_list, bias_list = ([], [], [])
    for block in reversed(range(BLOCKS)):
        normed, inv_spread, normed_low, labels = saved[block]
        upstream = carry.astype(jnp.bfloat16)
        if block % 2 == 1:
            upstream = jnp.roll(upstream, -reach, axis=2)
        allowed = allowed_pairs(labels, row_valid, levels)
        flat = normed_low.reshape(-1, width)
        up_flat = upstream.reshape(-1, width)
        total = jnp.zeros((flat.shape[0], width), jnp.float32)
        block_in, block_out, block_bias = ([], [], [])
        for group in range(groups):
            in_matrix = qkv_weight[block, :, :, group * local:(group + 1) * local].reshape(width, 3 * local)
            packed = jnp.dot(flat, in_matrix, preferred_element_type=jnp.float32).astype(jnp.bfloat16)
            query, key_rows, value = unpack(packed, levels, rows, columns, heads_local)
            bias = jnp.take(bias_table[block, group * heads_local:(group + 1) * heads_local], rel_index, axis=1)
            probs = attend_probs(query, key_rows, bias, allowed)
            mixed = pack_heads(mix_values(probs, value), levels, rows, columns).reshape(-1, local)
            out_rows = out_weight[block, group * local:(group + 1) * local]
            block_out.append(jnp.dot(mixed.T, up_flat, preferred_element_type=jnp.float32))
            grad_mixed = jnp.dot(up_flat, out_rows.T, preferred_element_type=jnp.float32).astype(jnp.bfloat16)
            cotan = unpack(jnp.concatenate([grad_mixed, grad_mixed, grad_mixed], axis=-1), levels, rows, columns, heads_local)[0]
            grad_query, grad_key, grad_value, grad_scores = attend_backward(query, key_rows, value, probs, cotan)
            grad_packed = repack(grad_query, grad_key, grad_value, levels, rows, columns)
            block_in.append(jnp.dot(flat.T, grad_packed, preferred_element_type=jnp.float32).reshape(width, 3, local))
            block_bias.append(slot_sums(grad_scores, rel_index, SLOTS))
            part_sum = jnp.dot(grad_packed, in_matrix.T, preferred_element_type=jnp.float32)
            total = total + part_sum.astype(jnp.bfloat16).astype(jnp.float32)
        grad_normed = total.astype(jnp.bfloat16).reshape(levels, rows, columns, width)
        if block % 2 == 1:
            grad_normed = jnp.roll(grad_normed, reach, axis=2)
        carry = carry + norm_adjoint(grad_normed.astype(jnp.float32), normed, inv_spread, norm_gain[block])
        qkv_list.insert(0, jnp.concatenate(block_in, axis=2))
        out_list.insert(0, jnp.concatenate(block_out, axis=0))
        bias_list.insert(0, jnp.concatenate(block_bias, axis=0))
    return (output, carry.astype(jnp.bfloat16), jnp.stack(qkv_list), jnp.stack(out_list), jnp.stack(bias_list))
```

```python
import functools

import jax
import jax.numpy as jnp
import numpy as np
from jax import lax
from jax.experimental import pallas as pl
from jax.experimental.pallas import tpu as pltpu
from jax.sharding import PartitionSpec as P

WL = 2
WH = 6
WW = 12
SPAN = WL * WH * WW
REACH = WW // 2
BLOCKS = 2
EPSILON = 1e-05
MASKED = -1e30
F32 = jnp.float32
BF16 = jnp.bfloat16

AXES = ("lon", "lev", "lat")
LEV = 8
RING = 4
OFFSETS = (0, 1, -1, 2)
PIECES = 2 * RING * RING
BIAS_ROWS = 16
VMEM = 56 * 1024 * 1024


def decode(device):
    lat, lev, lon = device % 2, device // 2 % LEV, device // (2 * LEV)
    return (2 * lat + lon // 8, lon // 2 % 4, lon % 2, lev)


def encode(x, y, core, lev):
    x, y, lev = x % RING, y % RING, lev % LEV
    return (((x % 2) * 8 + y * 2 + core) * LEV + lev) * 2 + x // 2


def send(value, target):
    pairs = [(i, encode(*target(*decode(i)))) for i in range(2 * RING * RING * LEV)]
    return lax.ppermute(value, AXES, pairs)


def along(value, ring, step):
    def target(x, y, core, lev):
        if (core == 0) == (ring == 1):
            return (x + step, y, core, lev)
        return (x, y + step, core, lev)

    return send(value, target)


def along_levels(value, step):
    return send(value, lambda x, y, core, lev: (x, y, core, lev + step))


def swap_cores(value):
    return send(value, lambda x, y, core, lev: (x, y, 1 - core, lev))


def swap_levels(value):
    return send(value, lambda x, y, core, lev: (x, y, core, lev ^ 1))


def to_window(value, step):
    def target(x, y, core, lev):
        lon = (x % 2) * 8 + y * 2 + core
        index = (2 * lon + lev % 2 + step) % 32
        lon, side = index // 2, index % 2
        return (2 * (x // 2) + lon // 8, lon // 2 % 4, lon % 2, lev - lev % 2 + side)

    return send(value, target)


def from_next_lon(value):
    def target(x, y, core, lev):
        lon = ((x % 2) * 8 + y * 2 + core - 1) % 16
        return (2 * (x // 2) + lon // 8, lon // 2 % 4, lon % 2, lev)

    return send(value, target)


def after(values, *others):
    tied = lax.optimization_barrier((values, others))
    return tied[0]


def piece_order():
    lon, lat = lax.axis_index("lon"), lax.axis_index("lat")
    x, y, core = 2 * lat + lon // 8, lon // 2 % 4, lon % 2
    offsets = jnp.array(OFFSETS, jnp.int32)
    side = jnp.arange(2, dtype=jnp.int32)[:, None, None]
    second = offsets[None, :, None]
    first = offsets[None, None, :]
    which = (core + side) % 2
    at_x = (x + jnp.where(which == 0, first, second)) % RING
    at_y = (y + jnp.where(which == 0, second, first)) % RING
    return ((which * RING + at_x) * RING + at_y).reshape(-1).astype(jnp.int32)


def own_rows(qkv_weight, out_weight, piece):
    width = qkv_weight.shape[1]
    rows = width // PIECES
    start = piece * rows
    into = lax.dynamic_slice_in_dim(qkv_weight, start, rows, axis=1).reshape(BLOCKS, rows, -1)
    outof = lax.dynamic_slice_in_dim(out_weight, start, rows, axis=2).transpose(0, 2, 1)
    return jnp.concatenate([into, outof], axis=2)


def table_rows(bias_table, columns):
    high = lax.reduce_precision(bias_table, 8, 7)
    middle = lax.reduce_precision(bias_table - high, 8, 7)
    low = bias_table - high - middle
    flat = jnp.stack([high, middle, low]).reshape(-1)
    rows = -(-flat.shape[0] // columns // BIAS_ROWS) * BIAS_ROWS
    return jnp.pad(flat, (0, rows * columns - flat.shape[0])).reshape(rows, columns).astype(BF16)


def gather_levels(own):
    up, down = [own], [own]
    for _ in range(3):
        up.append(along_levels(up[-1], -1))
        down.append(along_levels(down[-1], 1))
    up.append(along_levels(up[-1], -1))
    return up + down[:0:-1]


def scatter_levels(messages):
    up, down = messages[LEV // 2], messages[LEV // 2 + 1]
    for step in range(LEV // 2 - 1, 0, -1):
        up = add_low(messages[step], along_levels(up, 1))
        if step > 1:
            down = add_low(messages[LEV + 1 - step], along_levels(down, -1))
    return add_low(messages[0], along_levels(up, 1), along_levels(down, -1))


def pack_kernel(*refs):
    parts, outs = refs[:LEV], refs[LEV:]
    for index, part in enumerate(parts):
        start = 0
        for out in outs:
            out[index] = part[start : start + out.shape[1]]
            start += out.shape[1]


def pack_levels(parts, rows):
    height, columns = parts[0].shape
    return pl.pallas_call(
        pack_kernel,
        out_shape=[
            jax.ShapeDtypeStruct((LEV, item, columns), BF16) for item in (rows, height - rows)
        ],
        compiler_params=pltpu.CompilerParams(vmem_limit_bytes=VMEM),
    )(*parts)


def first_ring(part):
    ahead = along(part, 1, -1)
    behind = along(part, 1, 1)
    far = along(part, 1, -2)
    return (jnp.stack([part, ahead]), jnp.stack([behind, far]))


def second_ring(own_a, own_b):
    ahead_a = along(own_a, 2, -1)
    behind_b = along(own_b, 2, 1)
    ahead_b = along(own_b, 2, -1)
    behind_a = along(own_a, 2, 1)
    far_a = along(ahead_a, 2, -1)
    far_b = along(behind_b, 2, 1)
    return (own_a, own_b, ahead_a, ahead_b, behind_a, behind_b, far_a, far_b)


def add_low(*terms):
    return functools.reduce(jnp.add, [term.astype(F32) for term in terms]).astype(BF16)


def end_kernel(*refs):
    ins, outs = refs[:6], refs[6:]
    for pair in range(2):
        value = ins[3 * pair][...].astype(F32)
        for item in ins[3 * pair + 1 : 3 * pair + 3]:
            value += item[...].astype(F32)
        outs[2 * pair][...] = value[0].astype(BF16)
        outs[2 * pair + 1][...] = value[1].astype(BF16)


def second_ring_end(*parts):
    rows, columns = parts[0].shape[2:]
    return pl.pallas_call(
        end_kernel,
        grid=(LEV // 2,),
        in_specs=[pl.BlockSpec((2, 2, rows, columns), lambda g: (0, g, 0, 0))] * 6,
        out_specs=[pl.BlockSpec((2, rows, columns), lambda g: (g, 0, 0))] * 4,
        out_shape=[jax.ShapeDtypeStruct((LEV, rows, columns), BF16)] * 4,
        compiler_params=pltpu.CompilerParams(vmem_limit_bytes=VMEM),
    )(*parts)


def scatter_start(grads):
    return (
        along(grads[6], 2, 1),
        along(grads[7], 2, -1),
        along(grads[3], 2, 1),
        along(grads[4], 2, -1),
    )


def scatter_middle(grads, far_a, far_b):
    return (
        along(add_low(grads[2], far_a), 2, 1),
        along(add_low(grads[5], far_b), 2, -1),
    )


def scatter_end(grads, ahead_a, behind_a, ahead_b, behind_b):
    mine, ahead, behind, far = second_ring_end(
        grads[0], ahead_a, behind_a, grads[1], ahead_b, behind_b
    )
    return (mine, along(ahead, 1, 1), along(behind, 1, -1), along(far, 1, 2))


def levels_kernel(*refs):
    parts, bias, outs = refs[: 4 * BLOCKS], refs[4 * BLOCKS], refs[4 * BLOCKS + 1 :]
    rows = parts[0].shape[1]
    for level, out in enumerate(outs):
        for block in range(BLOCKS):
            value = parts[4 * block][level].astype(F32)
            for item in parts[4 * block + 1 : 4 * block + 4]:
                value += item[level].astype(F32)
            out[pl.ds(block * rows, rows), :] = value.astype(BF16)
        out[pl.ds(BLOCKS * rows, BIAS_ROWS), :] = bias[level]


def finish_sums(parts, bias_rows):
    rows, columns = parts[0][0].shape[1:]
    height = BLOCKS * rows + BIAS_ROWS
    messages = pl.pallas_call(
        levels_kernel,
        out_shape=[jax.ShapeDtypeStruct((height, columns), BF16)] * LEV,
        compiler_params=pltpu.CompilerParams(vmem_limit_bytes=VMEM),
    )(*parts[0], *parts[1], bias_rows)
    total = scatter_levels(messages)
    first = jnp.stack([total, along(total, 1, -1), along(total, 1, 1), along(total, 1, -2)])
    mine = [first, along(first, 2, -1), along(first, 2, 1), along(first, 2, -2)]
    return mine + [swap_cores(item) for item in mine]


def pick(first, own, other):
    return jnp.where(first, own, other)


def enter_windows(field, even):
    left, right = field[..., :WW, :], field[..., WW:, :]
    keep = pick(even, left, right)
    got = swap_levels(pick(even, right, left))
    window = jnp.stack([pick(even, keep, got), pick(even, got, keep)], axis=-4)
    shape = window.shape[:-4] + (SPAN // 2, window.shape[-1])
    return window[..., :REACH, :].reshape(shape), window[..., REACH:, :].reshape(shape)


def leave_windows(halves, even):
    shape = (WL, WH, REACH, halves[0].shape[-1])
    window = jnp.concatenate([item.reshape(shape) for item in halves], axis=2)
    own = pick(even, window[0], window[1])
    got = swap_levels(pick(even, window[1], window[0]))
    return jnp.concatenate([pick(even, own, got), pick(even, got, own)], axis=1)


def wrap_left(halves):
    return (halves[1], to_window(halves[0], -1))


def wrap_right(halves):
    return (to_window(halves[1], 1), halves[0])


def by_half(values):
    halves = values.reshape(WH, 2, REACH).transpose(1, 0, 2)
    return jnp.broadcast_to(halves[:, None], (2, WL, WH, REACH)).reshape(1, SPAN)


ROW_GROUPS = WL * WH
LINES = (2 * WL - 1) * (2 * WH - 1)
STEPS = 2 * WW - 1


CORNERS = [p * WH * WW + q * WW + r for p in (0, WL - 1) for q in (0, WH - 1) for r in (0, WW - 1)]


def offset_places():
    table = np.zeros((len(CORNERS) * SPAN, LINES * STEPS), np.float32)
    offset = 0
    for a in range(1 - WL, WL):
        for b in range(1 - WH, WH):
            for c in range(1 - WW, WW):
                p = [(size - 1) * (step > 0) for size, step in ((WL, a), (WH, b), (WW, c))]
                k = [at - step for at, step in zip(p, (a, b, c))]
                row = CORNERS.index((p[0] * WH + p[1]) * WW + p[2])
                table[row * SPAN + (k[0] * WH + k[1]) * WW + k[2], offset] = 1
                offset += 1
    return table


def line_table():
    table = np.zeros((LINES, ROW_GROUPS * ROW_GROUPS), np.float32)
    for p in range(ROW_GROUPS):
        for k in range(ROW_GROUPS):
            a, b = p // WH - k // WH + WL - 1, p % WH - k % WH + WH - 1
            table[a * (2 * WH - 1) + b, p * ROW_GROUPS + k] = 1
    return table


def column_table():
    table = np.zeros((ROW_GROUPS, STEPS, WW, 2, ROW_GROUPS, REACH), np.float32)
    for group in range(ROW_GROUPS):
        for p in range(WW):
            for k in range(WW):
                table[group, p - k + WW - 1, p, k // REACH, group, k % REACH] = 1
    return table.reshape(ROW_GROUPS * STEPS, WW * SPAN)


def slot_table(rel_index):
    rows = jnp.concatenate([rel_index[at : at + 1] for at in CORNERS], axis=1)
    digits = jnp.concatenate([rows // 32, rows % 32]).astype(BF16)
    places = dot(digits, offset_places().astype(BF16))
    slots = (places[0] * 32 + places[1]).astype(jnp.int32)
    return (slots[:, None] == jnp.arange(LINES * STEPS)[None, :]).astype(BF16)


def expand_bias(tables, by_slot):
    count = tables.shape[1]
    flat = tables.reshape(3 * count, LINES * STEPS)
    steps = dot_nt(flat, by_slot).astype(BF16).reshape(3 * count, LINES, STEPS)
    lines = jnp.einsum(
        "hoj,oq->hqj", steps, line_table().astype(BF16), preferred_element_type=F32
    ).astype(BF16)
    rows = lines.reshape(3, count * ROW_GROUPS, ROW_GROUPS * STEPS)
    rows = jnp.concatenate([rows[part] for part in range(3)], axis=1)
    table = np.concatenate([column_table()] * 3).astype(BF16)
    bias = dot(rows, table)
    bias = bias.reshape(count, ROW_GROUPS, 2, REACH, SPAN).transpose(0, 2, 1, 3, 4)
    return bias.reshape(count, SPAN, SPAN)


def slot_sums(grad_scores, by_slot):
    count = grad_scores.shape[0]
    rows = grad_scores.reshape(count, 2, ROW_GROUPS, REACH, SPAN).transpose(0, 2, 1, 3, 4)
    lines = lax.dot_general(
        rows.reshape(count * ROW_GROUPS, WW * SPAN),
        column_table().astype(BF16),
        (((1,), (1,)), ((), ())),
        preferred_element_type=F32,
    )
    lines = lines.astype(BF16).reshape(count, ROW_GROUPS * ROW_GROUPS, STEPS)
    steps = jnp.einsum(
        "hqj,oq->hoj", lines, line_table().astype(BF16), preferred_element_type=F32
    )
    return dot(steps.astype(BF16).reshape(count, LINES * STEPS), by_slot)


def dot(a, b):
    return jnp.dot(a, b, preferred_element_type=F32)


def dot_nt(a, b):
    return lax.dot_general(a, b, (((1,), (1,)), ((), ())), preferred_element_type=F32)


def dot_tn(a, b):
    return lax.dot_general(a, b, (((0,), (0,)), ((), ())), preferred_element_type=F32)


def standardise(field):
    values = field.astype(F32)
    centre = jnp.mean(values, axis=-1, keepdims=True)
    spread = jnp.mean((values - centre) ** 2, axis=-1, keepdims=True)
    inv_spread = lax.rsqrt(spread + EPSILON)
    return (values - centre) * inv_spread, inv_spread


def norm_adjoint(cotan, field, gain):
    normed, inv_spread = standardise(field)
    scaled = cotan.astype(F32) * gain
    first = jnp.mean(scaled, axis=-1, keepdims=True)
    second = jnp.mean(scaled * normed, axis=-1, keepdims=True)
    return inv_spread * (scaled - first - normed * second)


def piece_slots():
    for index in range(PIECES):
        side, place = index // (RING * RING), index % (RING * RING)
        yield index, side, place


def collect_rows(order, pieces, weights):
    rows = weights.shape[0] // PIECES
    for index, side, place in piece_slots():
        start = pl.multiple_of(order[index] * rows, rows)
        weights[pl.ds(start, rows), :] = pieces[side * 8 + place // 2][place % 2, 0]


def join(halves):
    return jnp.concatenate([item[...].astype(F32) for item in halves], axis=0)


def split(values, halves):
    halves[0][...] = values[: SPAN // 2].astype(BF16)
    halves[1][...] = values[SPAN // 2 :].astype(BF16)


def head_masks(width):
    lane = lax.broadcasted_iota(jnp.int32, (1, width), 1)
    return [(lane // (width // 2) == head).astype(F32).astype(BF16) for head in range(2)]


def forward_kernel(order, *refs):
    halves, (gain, marks, bias), pieces = refs[:2], refs[2:5], refs[5:21]
    after, (packed_out, mixed_out, probs_out) = refs[21:23], refs[23:26]
    weights, normed, total, allowed = refs[26:]
    group = pl.program_id(0)
    local = mixed_out.shape[-1]

    @pl.when(group == 0)
    def _():
        values, _ = standardise(join(halves))
        normed[...] = (values * gain[...]).astype(BF16)
        total[...] = jnp.zeros_like(total)
        here = lax.broadcasted_iota(jnp.int32, (SPAN, SPAN), 0)
        there = lax.broadcasted_iota(jnp.int32, (SPAN, SPAN), 1)
        labels = jnp.broadcast_to(marks[0:1].astype(F32), (SPAN, SPAN))
        living = jnp.broadcast_to(marks[1:2], (SPAN, SPAN))
        seen = (labels == labels.T) & ((living > 0) | (here == there))
        allowed[...] = jnp.where(seen, 1.0, 0.0)

    collect_rows(order, pieces, weights)
    packed = dot(normed[...], weights[:, : 3 * local]).astype(BF16)
    packed_out[0] = packed
    query, keys, value = (packed[:, i * local : (i + 1) * local] for i in range(3))
    scale = (local // 2) ** (-0.5)
    mixed = jnp.zeros((SPAN, local), F32)
    for head, mask in enumerate(head_masks(local)):
        scores = dot_nt(query, keys * mask) * scale + bias[head]
        scores = jnp.where(allowed[...] > 0, scores, MASKED)
        grown = jnp.exp(scores - jnp.max(scores, axis=-1, keepdims=True))
        probs = grown / jnp.sum(grown, axis=-1, keepdims=True)
        probs_out[head] = probs
        mixed += dot(probs.astype(BF16), value * mask)
    mixed = mixed.astype(BF16)
    mixed_out[0] = mixed
    total[...] += dot_nt(mixed, weights[:, 3 * local :]).astype(BF16).astype(F32)

    @pl.when(group == LEV - 1)
    def _():
        split(join(halves) + total[...].astype(BF16).astype(F32), after)


def backward_kernel(last, order, *refs):
    refs = list(refs)

    def take(count):
        taken, refs[:] = refs[:count], refs[count:]
        return taken

    grad_out = take(2)
    later_grad, later_field = (take(2), take(2)) if last else (None, None)
    later_gain = take(1)[0] if last else None
    field, (gain, packed_in, mixed_in, probs_in), pieces = take(2), take(4), take(16)
    outs, (scores_out, operands) = take(2), take(2)
    weights, normed, up, total = take(4)
    carried = take(1)[0] if last else None
    step = pl.program_id(0)
    local = mixed_in.shape[-1]

    @pl.when(step == 0)
    def _():
        values, _ = standardise(join(field))
        normed[...] = (values * gain[...]).astype(BF16)
        upstream = join(grad_out)
        if last:
            upstream = upstream + norm_adjoint(join(later_grad), join(later_field), later_gain[...])
            carried[...] = upstream
        up[...] = upstream.astype(BF16)
        total[...] = jnp.zeros_like(total)

    collect_rows(order, pieces, weights)
    packed, mixed = packed_in[0], mixed_in[0]
    query, keys, value = (packed[:, i * local : (i + 1) * local] for i in range(3))
    cotan = dot(up[...], weights[:, 3 * local :]).astype(BF16)
    scale = (local // 2) ** (-0.5)
    grad_query = grad_keys = grad_value = jnp.zeros((SPAN, local), F32)
    for head, mask in enumerate(head_masks(local)):
        probs = probs_in[head]
        grad_probs = dot_nt(cotan, value * mask)
        grad_value += dot_tn(probs.astype(BF16), cotan * mask)
        inner = jnp.sum(grad_probs * probs, axis=-1, keepdims=True)
        grad_scores = (probs * (grad_probs - inner)).astype(BF16)
        scores_out[head] = grad_scores
        grad_query += dot(grad_scores, keys * mask)
        grad_keys += dot_tn(grad_scores, query * mask)
    grad_packed = jnp.concatenate(
        [
            (grad_query * scale).astype(BF16),
            (grad_keys * scale).astype(BF16),
            grad_value.astype(BF16),
        ],
        axis=1,
    )
    total[...] += dot_nt(grad_packed, weights[:, : 3 * local]).astype(BF16).astype(F32)
    here = pl.ds(pl.multiple_of(step * local, local), local)
    operands[0, :, : 3 * local] = grad_packed
    operands[0, :, 3 * local : 4 * local] = mixed
    operands[0, :, 4 * local : 5 * local] = normed[:, here]
    operands[0, :, 5 * local :] = up[:, here]

    @pl.when(step == LEV - 1)
    def _():
        if last:
            grad_normed = total[...].astype(BF16)
            split(carried[...] + norm_adjoint(grad_normed, join(field), gain[...]), outs)
        else:
            split(total[...], outs)


def weights_kernel(order, mine, other, *refs):
    outs, (turned, normed, up) = refs[:8], refs[8:]
    step = pl.program_id(0)
    local = mine.shape[-1] // 6
    rows = normed.shape[1] // (PIECES // 2)

    @pl.when(step == 0)
    def _():
        for side, source in enumerate((mine, other)):
            for target, column in ((normed, 4 * local), (up, 5 * local)):
                for level in range(LEV):
                    part = source[level, :, column : column + local]
                    turned[level * local : (level + 1) * local] = part.T
                for place in range(PIECES // 2):
                    start = pl.multiple_of(order[place] * rows, rows)
                    target[side, place * rows : (place + 1) * rows] = turned[pl.ds(start, rows), :]

    packed = [item[step, :, : 3 * local] for item in (mine, other)]
    mixed = [item[step, :, 3 * local : 4 * local] for item in (mine, other)]
    into = (dot(normed[0], packed[0]) + dot(normed[1], packed[1])).astype(BF16)
    outof = (dot(up[0], mixed[0]) + dot(up[1], mixed[1])).astype(BF16)
    for place in range(PIECES // 2):
        out = outs[place // 2]
        out[place % 2, 0, :, : 3 * local] = into[place * rows : (place + 1) * rows]
        out[place % 2, 0, :, 3 * local :] = outof[place * rows : (place + 1) * rows]


def finish_kernel(order, *refs):
    inputs, (into, outof, bias, turned) = refs[:8], refs[8:]
    rows = into.shape[2] // PIECES
    local = outof.shape[1]
    bias_total = jnp.zeros(bias.shape, F32)
    for index, side, place in piece_slots():
        source = inputs[side * RING + place // RING]
        bias_total += source[place % RING, BLOCKS * rows :].astype(F32)
    bias[...] = bias_total
    for block in range(BLOCKS):
        for index, side, place in piece_slots():
            start = pl.multiple_of(order[index] * rows, rows)
            source = inputs[side * RING + place // RING]
            values = source[place % RING, pl.ds(block * rows, rows), :].astype(F32)
            for part in range(3):
                into[block, part, pl.ds(start, rows), :] = values[:, part * local : (part + 1) * local]
            turned[pl.ds(start, rows), :] = values[:, 3 * local :]
        outof[block] = turned[...].T


def whole(*shape):
    return pl.BlockSpec(shape, lambda g, order: (0,) * len(shape))


def by_group(*shape):
    return pl.BlockSpec((1,) + shape, lambda g, order: (g,) + (0,) * len(shape))


def by_head(base):
    return pl.BlockSpec((2, SPAN, SPAN), lambda g, order: (g + base, 0, 0))


def by_piece(block, rows, columns):
    return pl.BlockSpec((2, 1, rows, columns), lambda g, order: (0, g, block, 0))


def cost(flops, bytes_accessed):
    return pl.CostEstimate(flops=flops, bytes_accessed=bytes_accessed, transcendentals=0)


def run_forward(order, halves, gain, marks, bias, block, pieces):
    width = halves[0].shape[1]
    rows, columns = pieces[0].shape[2] // BLOCKS, pieces[0].shape[3]
    local = columns // 4
    shape = jax.ShapeDtypeStruct
    first, second, *saved = pl.pallas_call(
        forward_kernel,
        grid_spec=pltpu.PrefetchScalarGridSpec(
            num_scalar_prefetch=1,
            grid=(LEV,),
            in_specs=[
                whole(SPAN // 2, width),
                whole(SPAN // 2, width),
                whole(1, width),
                whole(2, SPAN),
                by_head(block * LEV),
                *[by_piece(block, rows, columns)] * 16,
            ],
            out_specs=[
                whole(SPAN // 2, width),
                whole(SPAN // 2, width),
                by_group(SPAN, 3 * local),
                by_group(SPAN, local),
                by_head(0),
            ],
            scratch_shapes=[
                pltpu.VMEM((width, columns), BF16),
                pltpu.VMEM((SPAN, width), BF16),
                pltpu.VMEM((SPAN, width), F32),
                pltpu.VMEM((SPAN, SPAN), F32),
            ],
        ),
        out_shape=[
            shape((SPAN // 2, width), BF16),
            shape((SPAN // 2, width), BF16),
            shape((LEV, SPAN, 3 * local), BF16),
            shape((LEV, SPAN, local), BF16),
            shape((2 * LEV, SPAN, SPAN), F32),
        ],
        compiler_params=pltpu.CompilerParams(vmem_limit_bytes=VMEM),
        cost_estimate=cost(14 * 10**9, 2 * 10**7),
    )(order, *halves, gain, marks, bias, *pieces)
    return (first, second), saved


def run_backward(order, last, upstream, halves, gain, block, saved, pieces):
    width = halves[0].shape[1]
    rows, columns = pieces[0].shape[2] // BLOCKS, pieces[0].shape[3]
    local = columns // 4
    shape = jax.ShapeDtypeStruct
    half = whole(SPAN // 2, width)
    above = [half] * 2
    scratch = [
        pltpu.VMEM((width, columns), BF16),
        pltpu.VMEM((SPAN, width), BF16),
        pltpu.VMEM((SPAN, width), BF16),
        pltpu.VMEM((SPAN, width), F32),
    ]
    if last:
        above += [half] * 4 + [whole(1, width)]
        scratch.append(pltpu.VMEM((SPAN, width), F32))
    first, second, scores, operands = pl.pallas_call(
        functools.partial(backward_kernel, last),
        grid_spec=pltpu.PrefetchScalarGridSpec(
            num_scalar_prefetch=1,
            grid=(LEV,),
            in_specs=[
                *above,
                half,
                half,
                whole(1, width),
                by_group(SPAN, 3 * local),
                by_group(SPAN, local),
                by_head(0),
                *[by_piece(block, rows, columns)] * 16,
            ],
            out_specs=[half, half, by_head(0), by_group(SPAN, 6 * local)],
            scratch_shapes=scratch,
        ),
        out_shape=[
            shape((SPAN // 2, width), BF16),
            shape((SPAN // 2, width), BF16),
            shape((2 * LEV, SPAN, SPAN), BF16),
            shape((LEV, SPAN, 6 * local), BF16),
        ],
        compiler_params=pltpu.CompilerParams(vmem_limit_bytes=VMEM),
        cost_estimate=cost(14 * 10**9, 2 * 10**7),
    )(order, *upstream, *halves, gain, *saved, *pieces)
    return (first, second), scores, operands


def run_weights(order, mine, other, rows):
    local = mine.shape[-1] // 6
    width, columns = LEV * local, 4 * local
    return pl.pallas_call(
        weights_kernel,
        grid_spec=pltpu.PrefetchScalarGridSpec(
            num_scalar_prefetch=1,
            grid=(LEV,),
            in_specs=[whole(*mine.shape), whole(*other.shape)],
            out_specs=[pl.BlockSpec((2, 1, rows, columns), lambda g, order: (0, g, 0, 0))] * 8,
            scratch_shapes=[
                pltpu.VMEM((width, SPAN), BF16),
                pltpu.VMEM((2, width // 2, SPAN), BF16),
                pltpu.VMEM((2, width // 2, SPAN), BF16),
            ],
        ),
        out_shape=[jax.ShapeDtypeStruct((2, LEV, rows, columns), BF16)] * 8,
        compiler_params=pltpu.CompilerParams(vmem_limit_bytes=VMEM),
        cost_estimate=cost(5 * 10**9, 10**7),
    )(order, mine, other)


def run_finish(order, parts, width, local):
    shape = jax.ShapeDtypeStruct

    def whole_of(*extent):
        return pl.BlockSpec(extent, lambda order: (0,) * len(extent))

    shapes = [
        (BLOCKS, 3, width, local),
        (BLOCKS, local, width),
        (BIAS_ROWS, 4 * local),
    ]
    return pl.pallas_call(
        finish_kernel,
        grid_spec=pltpu.PrefetchScalarGridSpec(
            num_scalar_prefetch=1,
            grid=(),
            in_specs=[whole_of(*item.shape) for item in parts],
            out_specs=[whole_of(*extent) for extent in shapes],
            scratch_shapes=[pltpu.VMEM((width, local), F32)],
        ),
        out_shape=[shape(extent, F32) for extent in shapes],
        compiler_params=pltpu.CompilerParams(vmem_limit_bytes=VMEM),
    )(order, *parts)


def bias_message(grad_scores, by_slot, columns):
    sums = slot_sums(grad_scores, by_slot)
    slots = sums.shape[-1]
    flat = sums.reshape(BLOCKS, LEV, 2 * slots).transpose(1, 0, 2).reshape(LEV, -1)
    flat = jnp.pad(flat, ((0, 0), (0, BIAS_ROWS * columns - flat.shape[1])))
    return flat.reshape(LEV, BIAS_ROWS, columns).astype(BF16)


def on_device(
    tokens,
    norm_gain,
    qkv_weight,
    out_weight,
    bias_table,
    rel_index,
    region_ids,
    row_valid,
    grad_out,
):
    width = tokens.shape[-1]
    local = qkv_weight.shape[-1]
    slots = bias_table.shape[-1]
    columns = 4 * local
    rows = width // PIECES
    even = lax.axis_index("lev") % 2 == 0
    order = piece_order()
    gains = [norm_gain[block : block + 1] for block in range(BLOCKS)]

    own = own_rows(qkv_weight, out_weight, order[0]).reshape(BLOCKS * rows, columns)
    own = jnp.concatenate([own, table_rows(bias_table, columns)])
    part, tables = pack_levels(gather_levels(own), BLOCKS * rows)
    pieces = second_ring(*first_ring(part))
    pieces = pieces + tuple(swap_cores(item) for item in pieces)

    both = enter_windows(jnp.concatenate([tokens, grad_out]), even)
    start = tuple(item[0] for item in both)
    grad_start = tuple(item[1] for item in both)
    grad_shifted = wrap_left(grad_start)

    following = from_next_lon(region_ids[:, :REACH])
    shifted = jnp.concatenate([region_ids[:, REACH:], following], axis=1)
    living = by_half(jnp.broadcast_to(row_valid[:, None], (WH, WW)))
    marks = [
        jnp.concatenate([by_half(pick(even, item[:, :WW], item[:, WW:])), living])
        for item in (region_ids, shifted)
    ]

    by_slot = slot_table(rel_index)
    parts = tables.reshape(LEV, -1)[:, : 3 * bias_table.size]
    parts = parts.reshape(LEV, 3, BLOCKS, 2, slots).transpose(1, 2, 0, 3, 4)
    bias = expand_bias(parts.reshape(3, BLOCKS * 2 * LEV, slots), by_slot)

    middle, saved_0 = run_forward(order, start, gains[0], marks[0], bias, 0, pieces)
    second = wrap_left(middle)
    ended, saved_1 = run_forward(order, second, gains[1], marks[1], bias, 1, pieces)

    grad_normed, scores_1, operands = run_backward(
        order, False, grad_shifted, second, gains[1], 1, saved_1, pieces
    )
    later_grad = wrap_right(grad_normed)
    grads_1 = run_weights(order, operands, swap_cores(operands), rows)
    far_a, far_b, ahead_b, behind_a = scatter_start(grads_1)

    upstream = after([*grad_start, *later_grad, *middle, gains[1]], *grads_1)
    grad_first, scores_0, operands = run_backward(
        order, True, upstream, start, gains[0], 0, saved_0, pieces
    )
    operands, far_a, far_b, ahead_b, behind_a = after(
        (operands, far_a, far_b, ahead_b, behind_a)
    )
    ahead_a, behind_b = scatter_middle(grads_1, far_a, far_b)
    grads_0 = run_weights(order, operands, swap_cores(operands), rows)
    rest = after((ahead_a, behind_a, ahead_b, behind_b), *grads_0)
    sums_1 = scatter_end(grads_1, *rest)
    far_a, far_b, ahead_b, behind_a = scatter_start(grads_0)
    ahead_a, behind_b = scatter_middle(grads_0, far_a, far_b)
    sums_0 = scatter_end(grads_0, ahead_a, behind_a, ahead_b, behind_b)

    scores = jnp.concatenate([scores_0, scores_1])
    finished = finish_sums((sums_0, sums_1), bias_message(scores, by_slot, columns))
    grad_tokens = leave_windows(grad_first, even)
    ended = after(ended, grad_first)
    output = leave_windows(wrap_right(ended), even)

    grad_qkv, grad_out_weight, bias_rows = run_finish(order, finished, width, local)
    grad_qkv = grad_qkv.transpose(0, 2, 1, 3)
    grad_bias = bias_rows.reshape(-1)[: BLOCKS * 2 * slots].reshape(BLOCKS, 2, slots)
    return (output[None], grad_tokens[None], grad_qkv, grad_out_weight, grad_bias)


def solution(mesh):
    placed = (
        P("lev", "lat", "lon", None),
        P(),
        P(None, None, None, "lev"),
        P(None, "lev", None),
        P(None, "lev", None),
        P(),
        P("lat", "lon"),
        P("lat"),
        P("lev", "lat", "lon", None),
    )
    return jax.shard_map(
        on_device,
        mesh=mesh,
        in_specs=placed,
        out_specs=(
            P("lev", "lat", "lon", None),
            P("lev", "lat", "lon", None),
            P(None, None, None, "lev"),
            P(None, "lev", None),
            P(None, "lev", None),
        ),
        check_vma=False,
    )
```

```python
import functools

import jax
import jax.numpy as jnp
import numpy as np
from jax import lax
from jax.experimental import pallas as pl
from jax.experimental.pallas import tpu as pltpu
from jax.sharding import PartitionSpec as P

WL = 2
WH = 6
WW = 12
SPAN = WL * WH * WW
REACH = WW // 2
BLOCKS = 2
EPSILON = 1e-05
MASKED = -1e30
F32 = jnp.float32
BF16 = jnp.bfloat16

AXES = ("lon", "lev", "lat")
LEV = 8
RING = 4
OFFSETS = (0, 1, -1, 2)
PIECES = 2 * RING * RING
BIAS_ROWS = 16
VMEM = 56 * 1024 * 1024


def decode(device):
    lat, lev, lon = device % 2, device // 2 % LEV, device // (2 * LEV)
    return (2 * lat + lon // 8, lon // 2 % 4, lon % 2, lev)


def encode(x, y, core, lev):
    x, y, lev = x % RING, y % RING, lev % LEV
    return (((x % 2) * 8 + y * 2 + core) * LEV + lev) * 2 + x // 2


def send(value, target):
    pairs = [(i, encode(*target(*decode(i)))) for i in range(2 * RING * RING * LEV)]
    return lax.ppermute(value, AXES, pairs)


def along(value, ring, step):
    def target(x, y, core, lev):
        if (core == 0) == (ring == 1):
            return (x + step, y, core, lev)
        return (x, y + step, core, lev)

    return send(value, target)


def along_levels(value, step):
    return send(value, lambda x, y, core, lev: (x, y, core, lev + step))


def swap_cores(value):
    return send(value, lambda x, y, core, lev: (x, y, 1 - core, lev))


def swap_levels(value):
    return send(value, lambda x, y, core, lev: (x, y, core, lev ^ 1))


def to_window(value, step):
    def target(x, y, core, lev):
        lon = (x % 2) * 8 + y * 2 + core
        index = (2 * lon + lev % 2 + step) % 32
        lon, side = index // 2, index % 2
        return (2 * (x // 2) + lon // 8, lon // 2 % 4, lon % 2, lev - lev % 2 + side)

    return send(value, target)


def from_next_lon(value):
    def target(x, y, core, lev):
        lon = ((x % 2) * 8 + y * 2 + core - 1) % 16
        return (2 * (x // 2) + lon // 8, lon // 2 % 4, lon % 2, lev)

    return send(value, target)


def after(values, *others):
    tied = lax.optimization_barrier((values, others))
    return tied[0]


def piece_order():
    lon, lat = lax.axis_index("lon"), lax.axis_index("lat")
    x, y, core = 2 * lat + lon // 8, lon // 2 % 4, lon % 2
    offsets = jnp.array(OFFSETS, jnp.int32)
    side = jnp.arange(2, dtype=jnp.int32)[:, None, None]
    second = offsets[None, :, None]
    first = offsets[None, None, :]
    which = (core + side) % 2
    at_x = (x + jnp.where(which == 0, first, second)) % RING
    at_y = (y + jnp.where(which == 0, second, first)) % RING
    return ((which * RING + at_x) * RING + at_y).reshape(-1).astype(jnp.int32)


def own_rows(qkv_weight, out_weight, piece):
    width = qkv_weight.shape[1]
    rows = width // PIECES
    start = piece * rows
    into = lax.dynamic_slice_in_dim(qkv_weight, start, rows, axis=1).reshape(BLOCKS, rows, -1)
    outof = lax.dynamic_slice_in_dim(out_weight, start, rows, axis=2).transpose(0, 2, 1)
    return jnp.concatenate([into, outof], axis=2)


def table_rows(bias_table, columns):
    high = lax.reduce_precision(bias_table, 8, 7)
    middle = lax.reduce_precision(bias_table - high, 8, 7)
    low = bias_table - high - middle
    flat = jnp.stack([high, middle, low]).reshape(-1)
    rows = -(-flat.shape[0] // columns // BIAS_ROWS) * BIAS_ROWS
    return jnp.pad(flat, (0, rows * columns - flat.shape[0])).reshape(rows, columns).astype(BF16)


def gather_levels(own):
    up, down = [own], [own]
    for _ in range(3):
        up.append(along_levels(up[-1], -1))
        down.append(along_levels(down[-1], 1))
    up.append(along_levels(up[-1], -1))
    return up + down[:0:-1]


def pack_kernel(*refs):
    parts, outs = refs[:LEV], refs[LEV:]
    for index, part in enumerate(parts):
        start = 0
        for out in outs:
            out[index] = part[start : start + out.shape[1]]
            start += out.shape[1]


def pack_levels(parts, rows):
    height, columns = parts[0].shape
    return pl.pallas_call(
        pack_kernel,
        out_shape=[
            jax.ShapeDtypeStruct((LEV, item, columns), BF16) for item in (rows, height - rows)
        ],
        compiler_params=pltpu.CompilerParams(vmem_limit_bytes=VMEM),
    )(*parts)


def first_ring(part):
    ahead = along(part, 1, -1)
    behind = along(part, 1, 1)
    far = along(part, 1, -2)
    return (jnp.stack([part, ahead]), jnp.stack([behind, far]))


def second_ring(own_a, own_b):
    ahead_a = along(own_a, 2, -1)
    behind_b = along(own_b, 2, 1)
    ahead_b = along(own_b, 2, -1)
    behind_a = along(own_a, 2, 1)
    far_a = along(ahead_a, 2, -1)
    far_b = along(behind_b, 2, 1)
    return (own_a, own_b, ahead_a, ahead_b, behind_a, behind_b, far_a, far_b)


def add_low(*terms):
    return functools.reduce(jnp.add, [term.astype(F32) for term in terms]).astype(BF16)


def end_kernel(*refs):
    ins, outs = refs[:6], refs[6:]
    for pair in range(2):
        value = ins[3 * pair][...] + (ins[3 * pair + 1][...] + ins[3 * pair + 2][...])
        outs[2 * pair][...] = value[0]
        outs[2 * pair + 1][...] = value[1]


def second_ring_end(*parts):
    rows, columns = parts[0].shape[2:]
    return pl.pallas_call(
        end_kernel,
        grid=(LEV // 2,),
        in_specs=[pl.BlockSpec((2, 2, rows, columns), lambda g: (0, g, 0, 0))] * 6,
        out_specs=[pl.BlockSpec((2, rows, columns), lambda g: (g, 0, 0))] * 4,
        out_shape=[jax.ShapeDtypeStruct((LEV, rows, columns), BF16)] * 4,
        compiler_params=pltpu.CompilerParams(vmem_limit_bytes=VMEM),
    )(*parts)


def scatter_start(grads):
    return (
        along(grads[6], 2, 1),
        along(grads[7], 2, -1),
        along(grads[3], 2, 1),
        along(grads[4], 2, -1),
    )


def scatter_middle(grads, far_a, far_b):
    return (
        along(add_low(grads[2], far_a), 2, 1),
        along(add_low(grads[5], far_b), 2, -1),
    )


def scatter_end(grads, ahead_a, behind_a, ahead_b, behind_b):
    mine, ahead, behind, far = second_ring_end(
        grads[0], ahead_a, behind_a, grads[1], ahead_b, behind_b
    )
    return (mine, along(ahead, 1, 1), along(behind, 1, -1), along(far, 1, 2))


def levels_kernel(lev, *refs):
    parts, bias, out = refs[: 4 * BLOCKS], refs[4 * BLOCKS], refs[4 * BLOCKS + 1]
    rows = parts[0].shape[1]
    for level in range(LEV):
        owner = lax.rem(lev[0] + level, LEV)
        for block in range(BLOCKS):
            value = parts[4 * block][level].astype(F32)
            for item in parts[4 * block + 1 : 4 * block + 4]:
                value += item[level].astype(F32)
            out[owner, pl.ds(block * rows, rows), :] = value.astype(BF16)
        out[owner, pl.ds(BLOCKS * rows, BIAS_ROWS), :] = bias[level]


def whole_of(*extent):
    return pl.BlockSpec(extent, lambda order: (0,) * len(extent))


def finish_sums(parts, bias_rows):
    rows, columns = parts[0][0].shape[1:]
    height = BLOCKS * rows + BIAS_ROWS
    operands = [*parts[0], *parts[1], bias_rows]
    messages = pl.pallas_call(
        levels_kernel,
        grid_spec=pltpu.PrefetchScalarGridSpec(
            num_scalar_prefetch=1,
            grid=(),
            in_specs=[whole_of(*item.shape) for item in operands],
            out_specs=whole_of(LEV, height, columns),
        ),
        out_shape=jax.ShapeDtypeStruct((LEV, height, columns), BF16),
        compiler_params=pltpu.CompilerParams(vmem_limit_bytes=VMEM),
    )(lax.axis_index("lev").reshape(1), *operands)
    total = lax.psum_scatter(messages, "lev", scatter_dimension=0, tiled=False)
    first = jnp.stack([total, along(total, 1, -1), along(total, 1, 1), along(total, 1, -2)])
    mine = [first, along(first, 2, -1), along(first, 2, 1), along(first, 2, -2)]
    return mine + [swap_cores(item) for item in mine]


def pick(first, own, other):
    return jnp.where(first, own, other)


def enter_windows(field, even):
    left, right = field[..., :WW, :], field[..., WW:, :]
    keep = pick(even, left, right)
    got = swap_levels(pick(even, right, left))
    window = jnp.stack([pick(even, keep, got), pick(even, got, keep)], axis=-4)
    window = jnp.moveaxis(window, -2, -4)
    flat = window.reshape(window.shape[:-4] + (SPAN, window.shape[-1]))
    return flat[..., : SPAN // 2, :], flat[..., SPAN // 2 :, :]


def leave_windows(halves, even):
    shape = (REACH, WL, WH, halves[0].shape[-1])
    window = jnp.concatenate([item.reshape(shape) for item in halves]).transpose(1, 2, 0, 3)
    own = pick(even, window[0], window[1])
    got = swap_levels(pick(even, window[1], window[0]))
    return jnp.concatenate([pick(even, own, got), pick(even, got, own)], axis=1)


def wrap_left(halves):
    return (halves[1], to_window(halves[0], -1))


def wrap_right(halves):
    return (to_window(halves[1], 1), halves[0])


def by_half(values):
    return jnp.broadcast_to(values.T[:, None], (WW, WL, WH)).reshape(1, SPAN)


ROW_GROUPS = WL * WH
LINES = (2 * WL - 1) * (2 * WH - 1)
STEPS = 2 * WW - 1


CORNERS = [p * WH * WW + q * WW + r for p in (0, WL - 1) for q in (0, WH - 1) for r in (0, WW - 1)]


def offset_places():
    table = np.zeros((len(CORNERS) * SPAN, LINES * STEPS), np.float32)
    offset = 0
    for a in range(1 - WL, WL):
        for b in range(1 - WH, WH):
            for c in range(1 - WW, WW):
                p = [(size - 1) * (step > 0) for size, step in ((WL, a), (WH, b), (WW, c))]
                k = [at - step for at, step in zip(p, (a, b, c))]
                row = CORNERS.index((p[0] * WH + p[1]) * WW + p[2])
                table[row * SPAN + (k[0] * WH + k[1]) * WW + k[2], offset] = 1
                offset += 1
    return table


LANES = 32
WIDE = 256


def line_table():
    table = np.zeros((LINES, STEPS, ROW_GROUPS, ROW_GROUPS, LANES), np.float32)
    for p in range(ROW_GROUPS):
        for k in range(ROW_GROUPS):
            a, b = p // WH - k // WH + WL - 1, p % WH - k % WH + WH - 1
            for step in range(STEPS):
                table[a * (2 * WH - 1) + b, step, p, k, step] = 1
    return table.reshape(LINES * STEPS, ROW_GROUPS * ROW_GROUPS * LANES).astype(BF16)


def column_table():
    table = np.zeros((ROW_GROUPS, LANES, WW, WIDE), np.float32)
    for line in range(ROW_GROUPS):
        for p in range(WW):
            for k in range(WW):
                table[line, p - k + WW - 1, p, k * ROW_GROUPS + line] = 1
    return table.reshape(ROW_GROUPS * LANES, WW * WIDE).astype(BF16)


def slot_table(rel_index):
    rows = jnp.concatenate([rel_index[at : at + 1] for at in CORNERS], axis=1)
    digits = jnp.concatenate([rows // 32, rows % 32]).astype(BF16)
    places = dot(digits, offset_places().astype(BF16))
    slots = (places[0] * 32 + places[1]).astype(jnp.int32)
    return (slots[:, None] == jnp.arange(LINES * STEPS)[None, :]).astype(BF16)


def expand_bias(tables, by_slot):
    count = tables.shape[1]
    flat = tables.reshape(3 * count, LINES * STEPS)
    steps = dot_nt(flat, by_slot).astype(BF16)
    lines = dot(steps, line_table()).astype(BF16)
    rows = lines.reshape(3, count * ROW_GROUPS, ROW_GROUPS * LANES)
    rows = jnp.concatenate([rows[part] for part in range(3)], axis=1)
    return dot(rows, np.concatenate([column_table()] * 3))


def slot_sums(grad_scores, by_slot):
    rows = dot_nt(grad_scores.astype(BF16), column_table()).astype(BF16)
    lines = rows.reshape(-1, ROW_GROUPS * ROW_GROUPS * LANES)
    return dot(dot_nt(lines, line_table()).astype(BF16), by_slot)


def dot(a, b):
    return jnp.dot(a, b, preferred_element_type=F32)


def dot_nt(a, b):
    return lax.dot_general(a, b, (((1,), (1,)), ((), ())), preferred_element_type=F32)


def dot_tn(a, b):
    return lax.dot_general(a, b, (((0,), (0,)), ((), ())), preferred_element_type=F32)


def standardise(field):
    values = field.astype(F32)
    centre = jnp.mean(values, axis=-1, keepdims=True)
    spread = jnp.mean((values - centre) ** 2, axis=-1, keepdims=True)
    inv_spread = lax.rsqrt(spread + EPSILON)
    return (values - centre) * inv_spread, inv_spread


def norm_adjoint(cotan, field, gain):
    normed, inv_spread = standardise(field)
    scaled = cotan.astype(F32) * gain
    first = jnp.mean(scaled, axis=-1, keepdims=True)
    second = jnp.mean(scaled * normed, axis=-1, keepdims=True)
    return inv_spread * (scaled - first - normed * second)


def piece_slots():
    for index in range(PIECES):
        side, place = index // (RING * RING), index % (RING * RING)
        yield index, side, place


def collect_rows(order, pieces, weights):
    rows = weights.shape[0] // PIECES
    for index, side, place in piece_slots():
        start = pl.multiple_of(order[index] * rows, rows)
        weights[pl.ds(start, rows), :] = pieces[side * 8 + place // 2][place % 2, 0]


def join(halves):
    return jnp.concatenate([item[...].astype(F32) for item in halves], axis=0)


def split(values, halves):
    halves[0][...] = values[: SPAN // 2].astype(BF16)
    halves[1][...] = values[SPAN // 2 :].astype(BF16)


def head_masks(width):
    lane = lax.broadcasted_iota(jnp.int32, (1, width), 1)
    return [(lane // (width // 2) == head).astype(F32).astype(BF16) for head in range(2)]


def forward_kernel(order, *refs):
    halves, (gain, marks, bias), pieces = refs[:2], refs[2:5], refs[5:21]
    after, (packed_out, mixed_out, probs_out) = refs[21:23], refs[23:26]
    weights, normed, total, allowed, added = refs[26:]
    group = pl.program_id(0)
    local = mixed_out.shape[-1]

    @pl.when(group == 0)
    def _():
        values, _ = standardise(join(halves))
        normed[...] = (values * gain[...]).astype(BF16)
        total[...] = jnp.zeros_like(total)
        here = lax.broadcasted_iota(jnp.int32, (SPAN, SPAN), 0)
        there = lax.broadcasted_iota(jnp.int32, (SPAN, SPAN), 1)
        labels = jnp.broadcast_to(marks[0:1].astype(F32), (SPAN, SPAN))
        living = jnp.broadcast_to(marks[1:2], (SPAN, SPAN))
        seen = (labels == labels.T) & ((living > 0) | (here == there))
        allowed[...] = jnp.where(seen, 1.0, 0.0)

    collect_rows(order, pieces, weights)
    for head in range(2):
        for column in range(WW):
            rows = pl.ds(head * ROW_GROUPS, ROW_GROUPS)
            lanes = pl.ds(column * WIDE, SPAN)
            added[head, pl.ds(column * ROW_GROUPS, ROW_GROUPS), :] = bias[rows, lanes]
    packed = dot(normed[...], weights[:, : 3 * local]).astype(BF16)
    packed_out[0] = packed
    query, keys, value = (packed[:, i * local : (i + 1) * local] for i in range(3))
    scale = (local // 2) ** (-0.5)
    mixed = jnp.zeros((SPAN, local), F32)
    for head, mask in enumerate(head_masks(local)):
        scores = dot_nt(query, keys * mask) * scale + added[head]
        scores = jnp.where(allowed[...] > 0, scores, MASKED)
        grown = jnp.exp(scores - jnp.max(scores, axis=-1, keepdims=True))
        probs = grown / jnp.sum(grown, axis=-1, keepdims=True)
        probs_out[head] = probs
        mixed += dot(probs.astype(BF16), value * mask)
    mixed = mixed.astype(BF16)
    mixed_out[0] = mixed
    total[...] += dot_nt(mixed, weights[:, 3 * local :]).astype(BF16).astype(F32)

    @pl.when(group == LEV - 1)
    def _():
        split(join(halves) + total[...].astype(BF16).astype(F32), after)


def backward_kernel(last, order, *refs):
    refs = list(refs)

    def take(count):
        taken, refs[:] = refs[:count], refs[count:]
        return taken

    grad_out = take(2)
    later_grad, later_field = (take(2), take(2)) if last else (None, None)
    later_gain = take(1)[0] if last else None
    field, (gain, packed_in, mixed_in, probs_in), pieces = take(2), take(4), take(16)
    outs, (scores_out, operands) = take(2), take(2)
    weights, normed, up, total = take(4)
    carried = take(1)[0] if last else None
    step = pl.program_id(0)
    local = mixed_in.shape[-1]

    @pl.when(step == 0)
    def _():
        values, _ = standardise(join(field))
        normed[...] = (values * gain[...]).astype(BF16)
        upstream = join(grad_out)
        if last:
            upstream = upstream + norm_adjoint(join(later_grad), join(later_field), later_gain[...])
            carried[...] = upstream
        up[...] = upstream.astype(BF16)
        total[...] = jnp.zeros_like(total)

    scores_out[...] = jnp.zeros_like(scores_out)
    collect_rows(order, pieces, weights)
    packed, mixed = packed_in[0], mixed_in[0]
    query, keys, value = (packed[:, i * local : (i + 1) * local] for i in range(3))
    cotan = dot(up[...], weights[:, 3 * local :]).astype(BF16)
    scale = (local // 2) ** (-0.5)
    grad_query = grad_keys = grad_value = jnp.zeros((SPAN, local), F32)
    for head, mask in enumerate(head_masks(local)):
        probs = probs_in[head]
        grad_probs = dot_nt(cotan, value * mask)
        grad_value += dot_tn(probs.astype(BF16), cotan * mask)
        inner = jnp.sum(grad_probs * probs, axis=-1, keepdims=True)
        grad_scores = probs * (grad_probs - inner)
        for column in range(WW):
            rows = pl.ds(head * ROW_GROUPS, ROW_GROUPS)
            lanes = pl.ds(column * WIDE, SPAN)
            scores_out[rows, lanes] = grad_scores[column * ROW_GROUPS : (column + 1) * ROW_GROUPS]
        grad_scores = grad_scores.astype(BF16)
        grad_query += dot(grad_scores, keys * mask)
        grad_keys += dot_tn(grad_scores, query * mask)
    grad_packed = jnp.concatenate(
        [
            (grad_query * scale).astype(BF16),
            (grad_keys * scale).astype(BF16),
            grad_value.astype(BF16),
        ],
        axis=1,
    )
    total[...] += dot_nt(grad_packed, weights[:, : 3 * local]).astype(BF16).astype(F32)
    here = pl.ds(pl.multiple_of(step * local, local), local)
    operands[0, :, : 3 * local] = grad_packed
    operands[0, :, 3 * local : 4 * local] = mixed
    operands[0, :, 4 * local : 5 * local] = normed[:, here]
    operands[0, :, 5 * local :] = up[:, here]

    @pl.when(step == LEV - 1)
    def _():
        if last:
            grad_normed = total[...].astype(BF16)
            split(carried[...] + norm_adjoint(grad_normed, join(field), gain[...]), outs)
        else:
            split(total[...], outs)


def weights_kernel(order, mine, other, *refs):
    outs, (turned, normed, up) = refs[:8], refs[8:]
    step = pl.program_id(0)
    local = mine.shape[-1] // 6
    half = PIECES // 2
    rows = normed.shape[0] // half
    core = order[0] // half

    @pl.when(step == 0)
    def _():
        for side, source in enumerate((mine, other)):
            for target, column in ((normed, 4 * local), (up, 5 * local)):
                for level in range(LEV // 2):
                    part = source[core * (LEV // 2) + level, :, column : column + local]
                    turned[level * local : (level + 1) * local] = part.T
                for place in range(half):
                    start = pl.multiple_of((order[place] - core * half) * rows, rows)
                    target[place * rows : (place + 1) * rows, side * SPAN : (side + 1) * SPAN] = (
                        turned[pl.ds(start, rows), :]
                    )

    packed = jnp.concatenate([item[step, :, : 3 * local] for item in (mine, other)])
    mixed = jnp.concatenate([item[step, :, 3 * local : 4 * local] for item in (mine, other)])
    into = dot(normed[...], packed).astype(BF16)
    outof = dot(up[...], mixed).astype(BF16)
    for place in range(half):
        out = outs[place // 2]
        out[place % 2, 0, :, : 3 * local] = into[place * rows : (place + 1) * rows]
        out[place % 2, 0, :, 3 * local :] = outof[place * rows : (place + 1) * rows]


def finish_kernel(order, *refs):
    inputs, (into, outof, bias, turned) = refs[:8], refs[8:]
    rows = into.shape[2] // PIECES
    local = outof.shape[1]
    bias_total = jnp.zeros(bias.shape, F32)
    for index, side, place in piece_slots():
        source = inputs[side * RING + place // RING]
        bias_total += source[place % RING, BLOCKS * rows :].astype(F32)
    bias[...] = bias_total
    for block in range(BLOCKS):
        for index, side, place in piece_slots():
            start = pl.multiple_of(order[index] * rows, rows)
            source = inputs[side * RING + place // RING]
            values = source[place % RING, pl.ds(block * rows, rows), :].astype(F32)
            for part in range(3):
                into[block, part, pl.ds(start, rows), :] = values[:, part * local : (part + 1) * local]
            turned[pl.ds(start, rows), :] = values[:, 3 * local :]
        outof[block] = turned[...].T


def whole(*shape):
    return pl.BlockSpec(shape, lambda g, order: (0,) * len(shape))


def by_group(*shape):
    return pl.BlockSpec((1,) + shape, lambda g, order: (g,) + (0,) * len(shape))


def by_head():
    return pl.BlockSpec((2, SPAN, SPAN), lambda g, order: (g, 0, 0))


def by_rows(base):
    return pl.BlockSpec((2 * ROW_GROUPS, WW * WIDE), lambda g, order: (g + base, 0))


def by_piece(block, rows, columns):
    return pl.BlockSpec((2, 1, rows, columns), lambda g, order: (0, g, block, 0))


def cost(flops, bytes_accessed):
    return pl.CostEstimate(flops=flops, bytes_accessed=bytes_accessed, transcendentals=0)


def run_forward(order, halves, gain, marks, bias, block, pieces):
    width = halves[0].shape[1]
    rows, columns = pieces[0].shape[2] // BLOCKS, pieces[0].shape[3]
    local = columns // 4
    shape = jax.ShapeDtypeStruct
    first, second, *saved = pl.pallas_call(
        forward_kernel,
        grid_spec=pltpu.PrefetchScalarGridSpec(
            num_scalar_prefetch=1,
            grid=(LEV,),
            in_specs=[
                whole(SPAN // 2, width),
                whole(SPAN // 2, width),
                whole(1, width),
                whole(2, SPAN),
                by_rows(block * LEV),
                *[by_piece(block, rows, columns)] * 16,
            ],
            out_specs=[
                whole(SPAN // 2, width),
                whole(SPAN // 2, width),
                by_group(SPAN, 3 * local),
                by_group(SPAN, local),
                by_head(),
            ],
            scratch_shapes=[
                pltpu.VMEM((width, columns), BF16),
                pltpu.VMEM((SPAN, width), BF16),
                pltpu.VMEM((SPAN, width), F32),
                pltpu.VMEM((SPAN, SPAN), F32),
                pltpu.VMEM((2, SPAN, SPAN), F32),
            ],
        ),
        out_shape=[
            shape((SPAN // 2, width), BF16),
            shape((SPAN // 2, width), BF16),
            shape((LEV, SPAN, 3 * local), BF16),
            shape((LEV, SPAN, local), BF16),
            shape((2 * LEV, SPAN, SPAN), F32),
        ],
        compiler_params=pltpu.CompilerParams(vmem_limit_bytes=VMEM),
        cost_estimate=cost(14 * 10**9, 2 * 10**7),
    )(order, *halves, gain, marks, bias, *pieces)
    return (first, second), saved


def run_backward(order, last, upstream, halves, gain, block, saved, pieces):
    width = halves[0].shape[1]
    rows, columns = pieces[0].shape[2] // BLOCKS, pieces[0].shape[3]
    local = columns // 4
    shape = jax.ShapeDtypeStruct
    half = whole(SPAN // 2, width)
    above = [half] * 2
    scratch = [
        pltpu.VMEM((width, columns), BF16),
        pltpu.VMEM((SPAN, width), BF16),
        pltpu.VMEM((SPAN, width), BF16),
        pltpu.VMEM((SPAN, width), F32),
    ]
    if last:
        above += [half] * 4 + [whole(1, width)]
        scratch.append(pltpu.VMEM((SPAN, width), F32))
    first, second, scores, operands = pl.pallas_call(
        functools.partial(backward_kernel, last),
        grid_spec=pltpu.PrefetchScalarGridSpec(
            num_scalar_prefetch=1,
            grid=(LEV,),
            in_specs=[
                *above,
                half,
                half,
                whole(1, width),
                by_group(SPAN, 3 * local),
                by_group(SPAN, local),
                by_head(),
                *[by_piece(block, rows, columns)] * 16,
            ],
            out_specs=[half, half, by_rows(0), by_group(SPAN, 6 * local)],
            scratch_shapes=scratch,
        ),
        out_shape=[
            shape((SPAN // 2, width), BF16),
            shape((SPAN // 2, width), BF16),
            shape((2 * LEV * ROW_GROUPS, WW * WIDE), F32),
            shape((LEV, SPAN, 6 * local), BF16),
        ],
        compiler_params=pltpu.CompilerParams(vmem_limit_bytes=VMEM),
        cost_estimate=cost(14 * 10**9, 2 * 10**7),
    )(order, *upstream, *halves, gain, *saved, *pieces)
    return (first, second), scores, operands


def run_weights(order, mine, other, rows):
    local = mine.shape[-1] // 6
    width, columns = LEV * local, 4 * local
    return pl.pallas_call(
        weights_kernel,
        grid_spec=pltpu.PrefetchScalarGridSpec(
            num_scalar_prefetch=1,
            grid=(LEV,),
            in_specs=[whole(*mine.shape), whole(*other.shape)],
            out_specs=[pl.BlockSpec((2, 1, rows, columns), lambda g, order: (0, g, 0, 0))] * 8,
            scratch_shapes=[
                pltpu.VMEM((width // 2, SPAN), BF16),
                pltpu.VMEM((width // 2, 2 * SPAN), BF16),
                pltpu.VMEM((width // 2, 2 * SPAN), BF16),
            ],
        ),
        out_shape=[jax.ShapeDtypeStruct((2, LEV, rows, columns), BF16)] * 8,
        compiler_params=pltpu.CompilerParams(vmem_limit_bytes=VMEM),
        cost_estimate=cost(5 * 10**9, 10**7),
    )(order, mine, other)


def run_finish(order, parts, width, local):
    shape = jax.ShapeDtypeStruct

    shapes = [
        (BLOCKS, 3, width, local),
        (BLOCKS, local, width),
        (BIAS_ROWS, 4 * local),
    ]
    return pl.pallas_call(
        finish_kernel,
        grid_spec=pltpu.PrefetchScalarGridSpec(
            num_scalar_prefetch=1,
            grid=(),
            in_specs=[whole_of(*item.shape) for item in parts],
            out_specs=[whole_of(*extent) for extent in shapes],
            scratch_shapes=[pltpu.VMEM((width, local), F32)],
        ),
        out_shape=[shape(extent, F32) for extent in shapes],
        compiler_params=pltpu.CompilerParams(vmem_limit_bytes=VMEM),
    )(order, *parts)


def bias_message(grad_scores, by_slot, columns):
    sums = slot_sums(grad_scores, by_slot)
    slots = sums.shape[-1]
    flat = sums.reshape(BLOCKS, LEV, 2 * slots).transpose(1, 0, 2).reshape(LEV, -1)
    flat = jnp.pad(flat, ((0, 0), (0, BIAS_ROWS * columns - flat.shape[1])))
    return flat.reshape(LEV, BIAS_ROWS, columns).astype(BF16)


def on_device(
    tokens,
    norm_gain,
    qkv_weight,
    out_weight,
    bias_table,
    rel_index,
    region_ids,
    row_valid,
    grad_out,
):
    width = tokens.shape[-1]
    local = qkv_weight.shape[-1]
    slots = bias_table.shape[-1]
    columns = 4 * local
    rows = width // PIECES
    even = lax.axis_index("lev") % 2 == 0
    order = piece_order()
    gains = [norm_gain[block : block + 1] for block in range(BLOCKS)]

    own = own_rows(qkv_weight, out_weight, order[0]).reshape(BLOCKS * rows, columns)
    own = jnp.concatenate([own, table_rows(bias_table, columns)])
    part, tables = pack_levels(gather_levels(own), BLOCKS * rows)
    pieces = second_ring(*first_ring(part))
    pieces = pieces + tuple(swap_cores(item) for item in pieces)

    both = enter_windows(jnp.concatenate([tokens, grad_out]), even)
    start = tuple(item[0] for item in both)
    grad_start = tuple(item[1] for item in both)
    grad_shifted = wrap_left(grad_start)

    following = from_next_lon(region_ids[:, :REACH])
    shifted = jnp.concatenate([region_ids[:, REACH:], following], axis=1)
    living = by_half(jnp.broadcast_to(row_valid[:, None], (WH, WW)))
    marks = [
        jnp.concatenate([by_half(pick(even, item[:, :WW], item[:, WW:])), living])
        for item in (region_ids, shifted)
    ]

    by_slot = slot_table(rel_index)
    parts = tables.reshape(LEV, -1)[:, : 3 * bias_table.size]
    parts = parts.reshape(LEV, 3, BLOCKS, 2, slots).transpose(1, 2, 0, 3, 4)
    bias = expand_bias(parts.reshape(3, BLOCKS * 2 * LEV, slots), by_slot)

    middle, saved_0 = run_forward(order, start, gains[0], marks[0], bias, 0, pieces)
    second = wrap_left(middle)
    ended, saved_1 = run_forward(order, second, gains[1], marks[1], bias, 1, pieces)

    grad_normed, scores_1, operands = run_backward(
        order, False, grad_shifted, second, gains[1], 1, saved_1, pieces
    )
    later_grad = wrap_right(grad_normed)
    grads_1 = run_weights(order, operands, swap_cores(operands), rows)
    far_a, far_b, ahead_b, behind_a = scatter_start(grads_1)

    upstream = after([*grad_start, *later_grad, *middle, gains[1]], *grads_1)
    grad_first, scores_0, operands = run_backward(
        order, True, upstream, start, gains[0], 0, saved_0, pieces
    )
    operands, far_a, far_b, ahead_b, behind_a = after(
        (operands, far_a, far_b, ahead_b, behind_a)
    )
    ahead_a, behind_b = scatter_middle(grads_1, far_a, far_b)
    grads_0 = run_weights(order, operands, swap_cores(operands), rows)
    rest = after((ahead_a, behind_a, ahead_b, behind_b), *grads_0)
    sums_1 = scatter_end(grads_1, *rest)
    far_a, far_b, ahead_b, behind_a = scatter_start(grads_0)
    ahead_a, behind_b = scatter_middle(grads_0, far_a, far_b)
    sums_0 = scatter_end(grads_0, ahead_a, behind_a, ahead_b, behind_b)

    scores = jnp.concatenate([scores_0, scores_1])
    finished = finish_sums((sums_0, sums_1), bias_message(scores, by_slot, columns))
    grad_tokens = leave_windows(grad_first, even)
    ended = after(ended, grad_first)
    output = leave_windows(wrap_right(ended), even)

    grad_qkv, grad_out_weight, bias_rows = run_finish(order, finished, width, local)
    grad_qkv = grad_qkv.transpose(0, 2, 1, 3)
    grad_bias = bias_rows.reshape(-1)[: BLOCKS * 2 * slots].reshape(BLOCKS, 2, slots)
    return (output[None], grad_tokens[None], grad_qkv, grad_out_weight, grad_bias)


def solution(mesh):
    placed = (
        P("lev", "lat", "lon", None),
        P(),
        P(None, None, None, "lev"),
        P(None, "lev", None),
        P(None, "lev", None),
        P(),
        P("lat", "lon"),
        P("lat"),
        P("lev", "lat", "lon", None),
    )
    return jax.shard_map(
        on_device,
        mesh=mesh,
        in_specs=placed,
        out_specs=(
            P("lev", "lat", "lon", None),
            P("lev", "lat", "lon", None),
            P(None, None, None, "lev"),
            P(None, "lev", None),
            P(None, "lev", None),
        ),
        check_vma=False,
    )
```

```python
import functools

import jax
import jax.numpy as jnp
import numpy as np
from jax import lax
from jax.experimental import pallas as pl
from jax.experimental.pallas import tpu as pltpu
from jax.sharding import PartitionSpec as P

WL = 2
WH = 6
WW = 12
SPAN = WL * WH * WW
REACH = WW // 2
BLOCKS = 2
EPSILON = 1e-05
MASKED = -1e30
F32 = jnp.float32
BF16 = jnp.bfloat16

AXES = ("lon", "lev", "lat")
LEV = 8
RING = 4
OFFSETS = (0, 1, -1, 2)
PIECES = 2 * RING * RING
SHARES = 2 * RING
STEP = 2
BIAS_ROWS = 16
VMEM = 56 * 1024 * 1024


def decode(device):
    lat, lev, lon = device % 2, device // 2 % LEV, device // (2 * LEV)
    return (2 * lat + lon // 8, lon // 2 % 4, lon % 2, lev)


def encode(x, y, core, lev):
    x, y, lev = x % RING, y % RING, lev % LEV
    return (((x % 2) * 8 + y * 2 + core) * LEV + lev) * 2 + x // 2


def send(value, target):
    pairs = [(i, encode(*target(*decode(i)))) for i in range(2 * RING * RING * LEV)]
    return lax.ppermute(value, AXES, pairs)


def along(value, ring, step):
    def target(x, y, core, lev):
        if (core == 0) == (ring == 1):
            return (x + step, y, core, lev)
        return (x, y + step, core, lev)

    return send(value, target)


def along_levels(value, step):
    return send(value, lambda x, y, core, lev: (x, y, core, lev + step))


def swap_cores(value):
    return send(value, lambda x, y, core, lev: (x, y, 1 - core, lev))


def swap_levels(value):
    return send(value, lambda x, y, core, lev: (x, y, core, lev ^ 1))


def to_window(value, step):
    def target(x, y, core, lev):
        lon = (x % 2) * 8 + y * 2 + core
        index = (2 * lon + lev % 2 + step) % 32
        lon, side = index // 2, index % 2
        return (2 * (x // 2) + lon // 8, lon // 2 % 4, lon % 2, lev - lev % 2 + side)

    return send(value, target)


def from_next_lon(value):
    def target(x, y, core, lev):
        lon = ((x % 2) * 8 + y * 2 + core - 1) % 16
        return (2 * (x // 2) + lon // 8, lon // 2 % 4, lon % 2, lev)

    return send(value, target)


def after(values, *others):
    tied = lax.optimization_barrier((values, others))
    return tied[0]


def piece_order():
    lon, lat = lax.axis_index("lon"), lax.axis_index("lat")
    x, y, core = 2 * lat + lon // 8, lon // 2 % 4, lon % 2
    offsets = jnp.array(OFFSETS, jnp.int32)
    side = jnp.arange(2, dtype=jnp.int32)[:, None, None]
    second = offsets[None, :, None]
    first = offsets[None, None, :]
    which = (core + side) % 2
    at_x = (x + jnp.where(which == 0, first, second)) % RING
    at_y = (y + jnp.where(which == 0, second, first)) % RING
    return ((which * RING + at_x) * RING + at_y).reshape(-1).astype(jnp.int32)


def share_order():
    lon, lat = lax.axis_index("lon"), lax.axis_index("lat")
    x, y, core = 2 * lat + lon // 8, lon // 2 % 4, lon % 2
    which = (core + jnp.arange(2, dtype=jnp.int32)[:, None]) % 2
    place = jnp.where(which == 0, y, x) + jnp.array(OFFSETS, jnp.int32)[None]
    return (which * RING + place % RING).reshape(-1).astype(jnp.int32)


def own_rows(qkv_weight, out_weight, block, share):
    width, parts, local = qkv_weight.shape[1:]
    rows = width // SHARES
    start = share * rows
    zero = jnp.zeros_like(start)
    into = lax.dynamic_slice(
        qkv_weight, (zero + block, start, zero, zero), (1, rows, parts, local)
    )[0]
    outof = lax.dynamic_slice(out_weight, (zero + block, zero, start), (1, local, rows))[0].T
    return jnp.concatenate([into[:, part] for part in range(parts)] + [outof], axis=1)


def table_rows(bias_table, columns):
    high = lax.reduce_precision(bias_table, 8, 7)
    middle = lax.reduce_precision(bias_table - high, 8, 7)
    low = bias_table - high - middle
    flat = jnp.stack([high, middle, low]).reshape(-1)
    rows = -(-flat.shape[0] // columns // BIAS_ROWS) * BIAS_ROWS
    return jnp.pad(flat, (0, rows * columns - flat.shape[0])).reshape(rows, columns).astype(BF16)


def gather_levels(own):
    up, down = [own], [own]
    for _ in range(3):
        up.append(along_levels(up[-1], -1))
        down.append(along_levels(down[-1], 1))
    up.append(along_levels(up[-1], -1))
    return up + down[:0:-1]


def pack_kernel(*refs):
    parts, outs = refs[:LEV], refs[LEV:]
    for index, part in enumerate(parts):
        start = 0
        for out in outs:
            out[index] = part[start : start + out.shape[1]]
            start += out.shape[1]


def scatter_levels(messages):
    up, down = messages[LEV // 2], messages[LEV // 2 + 1]
    for step in range(LEV // 2 - 1, 0, -1):
        up = add_low(messages[step], along_levels(up, 1))
        if step > 1:
            down = add_low(messages[LEV + 1 - step], along_levels(down, -1))
    return add_low(messages[0], along_levels(up, 1), along_levels(down, -1))


def pack_levels(parts, heights):
    columns = parts[0].shape[1]
    return pl.pallas_call(
        pack_kernel,
        out_shape=[jax.ShapeDtypeStruct((LEV, item, columns), BF16) for item in heights],
        compiler_params=pltpu.CompilerParams(vmem_limit_bytes=VMEM),
    )(*parts)


def second_ring(own_a, own_b):
    ahead_a = along(own_a, 2, -1)
    behind_b = along(own_b, 2, 1)
    ahead_b = along(own_b, 2, -1)
    behind_a = along(own_a, 2, 1)
    far_a = along(ahead_a, 2, -1)
    far_b = along(behind_b, 2, 1)
    return (own_a, own_b, ahead_a, ahead_b, behind_a, behind_b, far_a, far_b)


def add_low(*terms):
    return functools.reduce(jnp.add, [term.astype(F32) for term in terms]).astype(BF16)


def end_kernel(*refs):
    ins, outs = refs[:6], refs[6:]
    for pair in range(2):
        value = ins[3 * pair][...] + (ins[3 * pair + 1][...] + ins[3 * pair + 2][...])
        outs[2 * pair][...] = value[0]
        outs[2 * pair + 1][...] = value[1]


def second_ring_end(*parts):
    rows, columns = parts[0].shape[2:]
    return pl.pallas_call(
        end_kernel,
        grid=(LEV // 2,),
        in_specs=[pl.BlockSpec((2, 2, rows, columns), lambda g: (0, g, 0, 0))] * 6,
        out_specs=[pl.BlockSpec((2, rows, columns), lambda g: (g, 0, 0))] * 4,
        out_shape=[jax.ShapeDtypeStruct((LEV, rows, columns), BF16)] * 4,
        compiler_params=pltpu.CompilerParams(vmem_limit_bytes=VMEM),
    )(*parts)


def scatter_start(grads):
    return (
        along(grads[6], 2, 1),
        along(grads[7], 2, -1),
        along(grads[3], 2, 1),
        along(grads[4], 2, -1),
    )


def scatter_middle(grads, far_a, far_b):
    return (
        along(add_low(grads[2], far_a), 2, 1),
        along(add_low(grads[5], far_b), 2, -1),
    )


def scatter_end(grads, ahead_a, behind_a, ahead_b, behind_b):
    mine, ahead, behind, far = second_ring_end(
        grads[0], ahead_a, behind_a, grads[1], ahead_b, behind_b
    )
    return (mine, along(ahead, 1, 1), along(behind, 1, -1), along(far, 1, 2))


def levels_kernel(*refs):
    parts, bias, outs = refs[: 4 * BLOCKS], refs[4 * BLOCKS], refs[4 * BLOCKS + 1 :]
    rows = parts[0].shape[1]
    for level, out in enumerate(outs):
        for block in range(BLOCKS):
            value = parts[4 * block][level].astype(F32)
            for item in parts[4 * block + 1 : 4 * block + 4]:
                value += item[level].astype(F32)
            out[pl.ds(block * rows, rows), :] = value.astype(BF16)
        out[pl.ds(BLOCKS * rows, BIAS_ROWS), :] = bias[level]


def whole_of(*extent):
    return pl.BlockSpec(extent, lambda order: (0,) * len(extent))


def finish_sums(parts, bias_rows):
    rows, columns = parts[0][0].shape[1:]
    height = BLOCKS * rows + BIAS_ROWS
    messages = pl.pallas_call(
        levels_kernel,
        out_shape=[jax.ShapeDtypeStruct((height, columns), BF16)] * LEV,
        compiler_params=pltpu.CompilerParams(vmem_limit_bytes=VMEM),
    )(*parts[0], *parts[1], bias_rows)
    total = scatter_levels(messages)
    first = jnp.stack([total, along(total, 1, -1), along(total, 1, 1), along(total, 1, -2)])
    mine = [first, along(first, 2, -1), along(first, 2, 1), along(first, 2, -2)]
    return mine + [swap_cores(item) for item in mine]


def pick(first, own, other):
    return jnp.where(first, own, other)


def enter_windows(field, even):
    left, right = field[..., :WW, :], field[..., WW:, :]
    keep = pick(even, left, right)
    got = swap_levels(pick(even, right, left))
    window = jnp.stack([pick(even, keep, got), pick(even, got, keep)], axis=-4)
    window = jnp.moveaxis(window, -2, -4)
    flat = window.reshape(window.shape[:-4] + (SPAN, window.shape[-1]))
    return flat[..., : SPAN // 2, :], flat[..., SPAN // 2 :, :]


def leave_windows(halves, even):
    shape = (REACH, WL, WH, halves[0].shape[-1])
    window = jnp.concatenate([item.reshape(shape) for item in halves]).transpose(1, 2, 0, 3)
    own = pick(even, window[0], window[1])
    got = swap_levels(pick(even, window[1], window[0]))
    return jnp.concatenate([pick(even, own, got), pick(even, got, own)], axis=1)


def wrap_left(halves):
    return (halves[1], to_window(halves[0], -1))


def wrap_right(halves):
    return (to_window(halves[1], 1), halves[0])


def by_half(values):
    return jnp.broadcast_to(values.T[:, None], (WW, WL, WH)).reshape(1, SPAN)


ROW_GROUPS = WL * WH
LINES = (2 * WL - 1) * (2 * WH - 1)
STEPS = 2 * WW - 1


CORNERS = [p * WH * WW + q * WW + r for p in (0, WL - 1) for q in (0, WH - 1) for r in (0, WW - 1)]


def offset_places():
    table = np.zeros((len(CORNERS) * SPAN, LINES * STEPS), np.float32)
    offset = 0
    for a in range(1 - WL, WL):
        for b in range(1 - WH, WH):
            for c in range(1 - WW, WW):
                p = [(size - 1) * (step > 0) for size, step in ((WL, a), (WH, b), (WW, c))]
                k = [at - step for at, step in zip(p, (a, b, c))]
                row = CORNERS.index((p[0] * WH + p[1]) * WW + p[2])
                table[row * SPAN + (k[0] * WH + k[1]) * WW + k[2], offset] = 1
                offset += 1
    return table


LANES = 32
WIDE = 256


def line_table():
    table = np.zeros((LINES, STEPS, ROW_GROUPS, ROW_GROUPS, LANES), np.float32)
    for p in range(ROW_GROUPS):
        for k in range(ROW_GROUPS):
            a, b = p // WH - k // WH + WL - 1, p % WH - k % WH + WH - 1
            for step in range(STEPS):
                table[a * (2 * WH - 1) + b, step, p, k, step] = 1
    return table.reshape(LINES * STEPS, ROW_GROUPS * ROW_GROUPS * LANES).astype(BF16)


def column_table():
    table = np.zeros((ROW_GROUPS, LANES, WW, WIDE), np.float32)
    for line in range(ROW_GROUPS):
        for p in range(WW):
            for k in range(WW):
                table[line, p - k + WW - 1, p, k * ROW_GROUPS + line] = 1
    return table.reshape(ROW_GROUPS * LANES, WW * WIDE).astype(BF16)


def slot_table(rel_index):
    rows = jnp.concatenate([rel_index[at : at + 1] for at in CORNERS], axis=1)
    digits = jnp.concatenate([rows // 32, rows % 32]).astype(BF16)
    places = dot(digits, offset_places().astype(BF16))
    slots = (places[0] * 32 + places[1]).astype(jnp.int32)
    return (slots[:, None] == jnp.arange(LINES * STEPS)[None, :]).astype(BF16)


def expand_bias(tables, by_slot):
    count = tables.shape[1]
    flat = tables.reshape(3 * count, LINES * STEPS)
    steps = dot_nt(flat, by_slot).astype(BF16)
    lines = dot(steps, line_table()).astype(BF16)
    rows = lines.reshape(3, count * ROW_GROUPS, ROW_GROUPS * LANES)
    rows = jnp.concatenate([rows[part] for part in range(3)], axis=1)
    return dot(rows, np.concatenate([column_table()] * 3))


def slot_sums(grad_scores, by_slot):
    rows = dot_nt(grad_scores.astype(BF16), column_table()).astype(BF16)
    lines = rows.reshape(-1, ROW_GROUPS * ROW_GROUPS * LANES)
    return dot(dot_nt(lines, line_table()).astype(BF16), by_slot)


def dot(a, b):
    return jnp.dot(a, b, preferred_element_type=F32)


def dot_nt(a, b):
    return lax.dot_general(a, b, (((1,), (1,)), ((), ())), preferred_element_type=F32)


def dot_tn(a, b):
    return lax.dot_general(a, b, (((0,), (0,)), ((), ())), preferred_element_type=F32)


def standardise(field):
    values = field.astype(F32)
    centre = jnp.mean(values, axis=-1, keepdims=True)
    spread = jnp.mean((values - centre) ** 2, axis=-1, keepdims=True)
    inv_spread = lax.rsqrt(spread + EPSILON)
    return (values - centre) * inv_spread, inv_spread


def norm_adjoint(cotan, field, gain):
    normed, inv_spread = standardise(field)
    scaled = cotan.astype(F32) * gain
    first = jnp.mean(scaled, axis=-1, keepdims=True)
    second = jnp.mean(scaled * normed, axis=-1, keepdims=True)
    return inv_spread * (scaled - first - normed * second)


def piece_slots():
    for index in range(PIECES):
        side, place = index // (RING * RING), index % (RING * RING)
        yield index, side, place


def collect_rows(order, pieces, weights, sub):
    rows = pieces[0].shape[1]
    for index, item in enumerate(pieces):
        share, half = order[index // 2], index % 2
        start = pl.multiple_of((2 * share + half) * rows, rows)
        weights[sub, pl.ds(start, rows), :] = item[sub]


def join(halves):
    return jnp.concatenate([item[...].astype(F32) for item in halves], axis=0)


def split(values, halves):
    halves[0][...] = values[: SPAN // 2].astype(BF16)
    halves[1][...] = values[SPAN // 2 :].astype(BF16)


def head_masks(width):
    lane = lax.broadcasted_iota(jnp.int32, (1, width), 1)
    return [(lane // (width // 2) == head).astype(F32).astype(BF16) for head in range(2)]


def forward_kernel(order, *refs):
    halves, (gain, marks, bias), pieces = refs[:2], refs[2:5], refs[5:21]
    after, (packed_out, mixed_out, probs_out) = refs[21:23], refs[23:26]
    weights, normed, total, allowed, added = refs[26:]
    group = pl.program_id(0)
    local = mixed_out.shape[-1]

    @pl.when(group == 0)
    def _():
        values, _ = standardise(join(halves))
        normed[...] = (values * gain[...]).astype(BF16)
        total[...] = jnp.zeros_like(total)
        here = lax.broadcasted_iota(jnp.int32, (SPAN, SPAN), 0)
        there = lax.broadcasted_iota(jnp.int32, (SPAN, SPAN), 1)
        labels = jnp.broadcast_to(marks[0:1].astype(F32), (SPAN, SPAN))
        living = jnp.broadcast_to(marks[1:2], (SPAN, SPAN))
        seen = (labels == labels.T) & ((living > 0) | (here == there))
        allowed[...] = jnp.where(seen, 1.0, 0.0)

    scale = (local // 2) ** (-0.5)
    for sub in range(STEP):
        collect_rows(order, pieces, weights, sub)
        for head in range(2):
            for column in range(WW):
                rows = pl.ds((2 * sub + head) * ROW_GROUPS, ROW_GROUPS)
                lanes = pl.ds(column * WIDE, SPAN)
                place = pl.ds(column * ROW_GROUPS, ROW_GROUPS)
                added[2 * sub + head, place, :] = bias[rows, lanes]
    for sub in range(STEP):
        packed = dot(normed[...], weights[sub, :, : 3 * local]).astype(BF16)
        packed_out[sub] = packed
        query, keys, value = (packed[:, i * local : (i + 1) * local] for i in range(3))
        mixed = jnp.zeros((SPAN, local), F32)
        for head, mask in enumerate(head_masks(local)):
            scores = dot_nt(query, keys * mask) * scale + added[2 * sub + head]
            scores = jnp.where(allowed[...] > 0, scores, MASKED)
            grown = jnp.exp(scores - jnp.max(scores, axis=-1, keepdims=True))
            probs = grown / jnp.sum(grown, axis=-1, keepdims=True)
            probs_out[2 * sub + head] = probs
            mixed += dot(probs.astype(BF16), value * mask)
        mixed = mixed.astype(BF16)
        mixed_out[sub] = mixed
        total[...] += dot_nt(mixed, weights[sub, :, 3 * local :]).astype(BF16).astype(F32)

    @pl.when(group == LEV // STEP - 1)
    def _():
        split(join(halves) + total[...].astype(BF16).astype(F32), after)


def backward_kernel(last, order, *refs):
    refs = list(refs)

    def take(count):
        taken, refs[:] = refs[:count], refs[count:]
        return taken

    grad_out = take(2)
    later_grad, later_field = (take(2), take(2)) if last else (None, None)
    later_gain = take(1)[0] if last else None
    field, (gain, packed_in, mixed_in, probs_in), pieces = take(2), take(4), take(16)
    outs, (scores_out, operands) = take(2), take(2)
    weights, normed, up, total = take(4)
    carried = take(1)[0] if last else None
    step = pl.program_id(0)
    local = mixed_in.shape[-1]

    @pl.when(step == 0)
    def _():
        values, _ = standardise(join(field))
        normed[...] = (values * gain[...]).astype(BF16)
        upstream = join(grad_out)
        if last:
            upstream = upstream + norm_adjoint(join(later_grad), join(later_field), later_gain[...])
            carried[...] = upstream
        up[...] = upstream.astype(BF16)
        total[...] = jnp.zeros_like(total)

    scores_out[...] = jnp.zeros_like(scores_out)
    scale = (local // 2) ** (-0.5)
    for sub in range(STEP):
        collect_rows(order, pieces, weights, sub)
    for sub in range(STEP):
        packed, mixed = packed_in[sub], mixed_in[sub]
        query, keys, value = (packed[:, i * local : (i + 1) * local] for i in range(3))
        cotan = dot(up[...], weights[sub, :, 3 * local :]).astype(BF16)
        grad_query = grad_keys = grad_value = jnp.zeros((SPAN, local), F32)
        for head, mask in enumerate(head_masks(local)):
            probs = probs_in[2 * sub + head]
            grad_probs = dot_nt(cotan, value * mask)
            grad_value += dot_tn(probs.astype(BF16), cotan * mask)
            inner = jnp.sum(grad_probs * probs, axis=-1, keepdims=True)
            grad_scores = probs * (grad_probs - inner)
            for column in range(WW):
                rows = pl.ds((2 * sub + head) * ROW_GROUPS, ROW_GROUPS)
                lanes = pl.ds(column * WIDE, SPAN)
                place = slice(column * ROW_GROUPS, (column + 1) * ROW_GROUPS)
                scores_out[rows, lanes] = grad_scores[place]
            grad_scores = grad_scores.astype(BF16)
            grad_query += dot(grad_scores, keys * mask)
            grad_keys += dot_tn(grad_scores, query * mask)
        grad_packed = jnp.concatenate(
            [
                (grad_query * scale).astype(BF16),
                (grad_keys * scale).astype(BF16),
                grad_value.astype(BF16),
            ],
            axis=1,
        )
        total[...] += dot_nt(grad_packed, weights[sub, :, : 3 * local]).astype(BF16).astype(F32)
        here = pl.ds(pl.multiple_of((STEP * step + sub) * local, local), local)
        operands[sub, :, : 3 * local] = grad_packed
        operands[sub, :, 3 * local : 4 * local] = mixed
        operands[sub, :, 4 * local : 5 * local] = normed[:, here]
        operands[sub, :, 5 * local :] = up[:, here]

    @pl.when(step == LEV // STEP - 1)
    def _():
        if last:
            grad_normed = total[...].astype(BF16)
            split(carried[...] + norm_adjoint(grad_normed, join(field), gain[...]), outs)
        else:
            split(total[...], outs)


def weights_kernel(order, mine, other, *refs):
    outs, (turned, normed, up) = refs[:8], refs[8:]
    step = pl.program_id(0)
    local = mine.shape[-1] // 6
    half = PIECES // 2
    rows = normed.shape[0] // half
    core = order[0] // half

    @pl.when(step == 0)
    def _():
        for side, source in enumerate((mine, other)):
            for target, column in ((normed, 4 * local), (up, 5 * local)):
                for level in range(LEV // 2):
                    part = source[core * (LEV // 2) + level, :, column : column + local]
                    turned[level * local : (level + 1) * local] = part.T
                for place in range(half):
                    start = pl.multiple_of((order[place] - core * half) * rows, rows)
                    target[place * rows : (place + 1) * rows, side * SPAN : (side + 1) * SPAN] = (
                        turned[pl.ds(start, rows), :]
                    )

    packed = jnp.concatenate([item[step, :, : 3 * local] for item in (mine, other)])
    mixed = jnp.concatenate([item[step, :, 3 * local : 4 * local] for item in (mine, other)])
    into = dot(normed[...], packed).astype(BF16)
    outof = dot(up[...], mixed).astype(BF16)
    for place in range(half):
        out = outs[place // 2]
        out[place % 2, 0, :, : 3 * local] = into[place * rows : (place + 1) * rows]
        out[place % 2, 0, :, 3 * local :] = outof[place * rows : (place + 1) * rows]


def finish_kernel(order, *refs):
    inputs, (into, outof, bias, turned) = refs[:8], refs[8:]
    rows = into.shape[2] // PIECES
    local = outof.shape[1]
    bias_total = jnp.zeros(bias.shape, F32)
    for index, side, place in piece_slots():
        source = inputs[side * RING + place // RING]
        bias_total += source[place % RING, BLOCKS * rows :].astype(F32)
    bias[...] = bias_total
    for block in range(BLOCKS):
        for index, side, place in piece_slots():
            start = pl.multiple_of(order[index] * rows, rows)
            source = inputs[side * RING + place // RING]
            values = source[place % RING, pl.ds(block * rows, rows), :].astype(F32)
            for part in range(3):
                into[block, part, pl.ds(start, rows), :] = values[:, part * local : (part + 1) * local]
            turned[pl.ds(start, rows), :] = values[:, 3 * local :]
        outof[block] = turned[...].T


def whole(*shape):
    return pl.BlockSpec(shape, lambda g, order: (0,) * len(shape))


def by_group(*shape):
    return pl.BlockSpec((STEP,) + shape, lambda g, order: (g,) + (0,) * len(shape))


def by_head():
    return pl.BlockSpec((2 * STEP, SPAN, SPAN), lambda g, order: (g, 0, 0))


def by_rows(base):
    start = base // STEP
    return pl.BlockSpec((2 * STEP * ROW_GROUPS, WW * WIDE), lambda g, order: (g + start, 0))


def cost(flops, bytes_accessed):
    return pl.CostEstimate(flops=flops, bytes_accessed=bytes_accessed, transcendentals=0)


def run_forward(order, halves, gain, marks, bias, block, pieces):
    width = halves[0].shape[1]
    rows, columns = pieces[0].shape[1:]
    local = columns // 4
    shape = jax.ShapeDtypeStruct
    first, second, *saved = pl.pallas_call(
        forward_kernel,
        grid_spec=pltpu.PrefetchScalarGridSpec(
            num_scalar_prefetch=1,
            grid=(LEV // STEP,),
            in_specs=[
                whole(SPAN // 2, width),
                whole(SPAN // 2, width),
                whole(1, width),
                whole(2, SPAN),
                by_rows(block * LEV),
                *[by_group(rows, columns)] * 16,
            ],
            out_specs=[
                whole(SPAN // 2, width),
                whole(SPAN // 2, width),
                by_group(SPAN, 3 * local),
                by_group(SPAN, local),
                by_head(),
            ],
            scratch_shapes=[
                pltpu.VMEM((STEP, width, columns), BF16),
                pltpu.VMEM((SPAN, width), BF16),
                pltpu.VMEM((SPAN, width), F32),
                pltpu.VMEM((SPAN, SPAN), F32),
                pltpu.VMEM((2 * STEP, SPAN, SPAN), F32),
            ],
        ),
        out_shape=[
            shape((SPAN // 2, width), BF16),
            shape((SPAN // 2, width), BF16),
            shape((LEV, SPAN, 3 * local), BF16),
            shape((LEV, SPAN, local), BF16),
            shape((2 * LEV, SPAN, SPAN), F32),
        ],
        compiler_params=pltpu.CompilerParams(vmem_limit_bytes=VMEM),
        cost_estimate=cost(14 * 10**9, 2 * 10**7),
    )(order, *halves, gain, marks, bias, *pieces)
    return (first, second), saved


def run_backward(order, last, upstream, halves, gain, saved, pieces):
    width = halves[0].shape[1]
    rows, columns = pieces[0].shape[1:]
    local = columns // 4
    shape = jax.ShapeDtypeStruct
    half = whole(SPAN // 2, width)
    above = [half] * 2
    scratch = [
        pltpu.VMEM((STEP, width, columns), BF16),
        pltpu.VMEM((SPAN, width), BF16),
        pltpu.VMEM((SPAN, width), BF16),
        pltpu.VMEM((SPAN, width), F32),
    ]
    if last:
        above += [half] * 4 + [whole(1, width)]
        scratch.append(pltpu.VMEM((SPAN, width), F32))
    first, second, scores, operands = pl.pallas_call(
        functools.partial(backward_kernel, last),
        grid_spec=pltpu.PrefetchScalarGridSpec(
            num_scalar_prefetch=1,
            grid=(LEV // STEP,),
            in_specs=[
                *above,
                half,
                half,
                whole(1, width),
                by_group(SPAN, 3 * local),
                by_group(SPAN, local),
                by_head(),
                *[by_group(rows, columns)] * 16,
            ],
            out_specs=[half, half, by_rows(0), by_group(SPAN, 6 * local)],
            scratch_shapes=scratch,
        ),
        out_shape=[
            shape((SPAN // 2, width), BF16),
            shape((SPAN // 2, width), BF16),
            shape((2 * LEV * ROW_GROUPS, WW * WIDE), F32),
            shape((LEV, SPAN, 6 * local), BF16),
        ],
        compiler_params=pltpu.CompilerParams(vmem_limit_bytes=VMEM),
        cost_estimate=cost(14 * 10**9, 2 * 10**7),
    )(order, *upstream, *halves, gain, *saved, *pieces)
    return (first, second), scores, operands


def run_weights(order, mine, other, rows):
    local = mine.shape[-1] // 6
    width, columns = LEV * local, 4 * local
    return pl.pallas_call(
        weights_kernel,
        grid_spec=pltpu.PrefetchScalarGridSpec(
            num_scalar_prefetch=1,
            grid=(LEV,),
            in_specs=[whole(*mine.shape), whole(*other.shape)],
            out_specs=[pl.BlockSpec((2, 1, rows, columns), lambda g, order: (0, g, 0, 0))] * 8,
            scratch_shapes=[
                pltpu.VMEM((width // 2, SPAN), BF16),
                pltpu.VMEM((width // 2, 2 * SPAN), BF16),
                pltpu.VMEM((width // 2, 2 * SPAN), BF16),
            ],
        ),
        out_shape=[jax.ShapeDtypeStruct((2, LEV, rows, columns), BF16)] * 8,
        compiler_params=pltpu.CompilerParams(vmem_limit_bytes=VMEM),
        cost_estimate=cost(5 * 10**9, 10**7),
    )(order, mine, other)


def run_finish(order, parts, width, local):
    shape = jax.ShapeDtypeStruct

    shapes = [
        (BLOCKS, 3, width, local),
        (BLOCKS, local, width),
        (BIAS_ROWS, 4 * local),
    ]
    return pl.pallas_call(
        finish_kernel,
        grid_spec=pltpu.PrefetchScalarGridSpec(
            num_scalar_prefetch=1,
            grid=(),
            in_specs=[whole_of(*item.shape) for item in parts],
            out_specs=[whole_of(*extent) for extent in shapes],
            scratch_shapes=[pltpu.VMEM((width, local), F32)],
        ),
        out_shape=[shape(extent, F32) for extent in shapes],
        compiler_params=pltpu.CompilerParams(vmem_limit_bytes=VMEM),
    )(order, *parts)


def bias_message(grad_scores, by_slot, columns):
    sums = slot_sums(grad_scores, by_slot)
    slots = sums.shape[-1]
    flat = sums.reshape(BLOCKS, LEV, 2 * slots).transpose(1, 0, 2).reshape(LEV, -1)
    flat = jnp.pad(flat, ((0, 0), (0, BIAS_ROWS * columns - flat.shape[1])))
    return flat.reshape(LEV, BIAS_ROWS, columns).astype(BF16)


def on_device(
    tokens,
    norm_gain,
    qkv_weight,
    out_weight,
    bias_table,
    rel_index,
    region_ids,
    row_valid,
    grad_out,
):
    width = tokens.shape[-1]
    local = qkv_weight.shape[-1]
    slots = bias_table.shape[-1]
    columns = 4 * local
    rows = width // PIECES
    even = lax.axis_index("lev") % 2 == 0
    order, shares = piece_order(), share_order()
    gains = [norm_gain[block : block + 1] for block in range(BLOCKS)]

    half = width // SHARES // 2
    own = [own_rows(qkv_weight, out_weight, b, shares[0]) for b in range(BLOCKS)]
    own[0] = jnp.concatenate([own[0], table_rows(bias_table, columns)])
    table_height = own[0].shape[0] - 2 * half
    low, high, tables = pack_levels(gather_levels(own[0]), (half, half, table_height))
    pieces_0 = second_ring(low, high)
    own[1], tokens, grad_out = after((own[1], tokens, grad_out), low)
    low, high = pack_levels(gather_levels(own[1]), (half, half))
    pieces_1 = second_ring(*after((low, high), pieces_0[6], pieces_0[7]))
    pieces_0 = pieces_0 + tuple(swap_cores(item) for item in pieces_0)

    both = enter_windows(jnp.concatenate([tokens, grad_out]), even)
    start = tuple(item[0] for item in both)
    grad_start = tuple(item[1] for item in both)
    grad_shifted = wrap_left(grad_start)

    following = from_next_lon(region_ids[:, :REACH])
    shifted = jnp.concatenate([region_ids[:, REACH:], following], axis=1)
    living = by_half(jnp.broadcast_to(row_valid[:, None], (WH, WW)))
    marks = [
        jnp.concatenate([by_half(pick(even, item[:, :WW], item[:, WW:])), living])
        for item in (region_ids, shifted)
    ]

    by_slot = slot_table(rel_index)
    parts = tables.reshape(LEV, -1)[:, : 3 * bias_table.size]
    parts = parts.reshape(LEV, 3, BLOCKS, 2, slots).transpose(1, 2, 0, 3, 4)
    bias = expand_bias(parts.reshape(3, BLOCKS * 2 * LEV, slots), by_slot)

    middle, saved_0 = run_forward(shares, start, gains[0], marks[0], bias, 0, pieces_0)
    second = wrap_left(middle)
    pieces_1 = pieces_1[:2] + tuple(after(pieces_1[2:], middle[0]))
    pieces_1 = pieces_1 + tuple(swap_cores(item) for item in pieces_1)
    ended, saved_1 = run_forward(shares, second, gains[1], marks[1], bias, 1, pieces_1)

    grad_normed, scores_1, operands = run_backward(
        shares, False, grad_shifted, second, gains[1], saved_1, pieces_1
    )
    later_grad = wrap_right(grad_normed)
    grads_1 = run_weights(order, operands, swap_cores(operands), rows)
    far_a, far_b, ahead_b, behind_a = scatter_start(grads_1)

    upstream = after([*grad_start, *later_grad, *middle, gains[1]], *grads_1)
    grad_first, scores_0, operands = run_backward(
        shares, True, upstream, start, gains[0], saved_0, pieces_0
    )
    operands, far_a, far_b, ahead_b, behind_a = after(
        (operands, far_a, far_b, ahead_b, behind_a)
    )
    ahead_a, behind_b = scatter_middle(grads_1, far_a, far_b)
    grads_0 = run_weights(order, operands, swap_cores(operands), rows)
    rest = after((ahead_a, behind_a, ahead_b, behind_b), *grads_0)
    sums_1 = scatter_end(grads_1, *rest)
    far_a, far_b, ahead_b, behind_a = scatter_start(grads_0)
    ahead_a, behind_b = scatter_middle(grads_0, far_a, far_b)
    sums_0 = scatter_end(grads_0, ahead_a, behind_a, ahead_b, behind_b)

    scores = jnp.concatenate([scores_0, scores_1])
    finished = finish_sums((sums_0, sums_1), bias_message(scores, by_slot, columns))
    grad_tokens = leave_windows(grad_first, even)
    ended = after(ended, grad_first)
    output = leave_windows(wrap_right(ended), even)

    grad_qkv, grad_out_weight, bias_rows = run_finish(order, finished, width, local)
    grad_qkv = grad_qkv.transpose(0, 2, 1, 3)
    grad_bias = bias_rows.reshape(-1)[: BLOCKS * 2 * slots].reshape(BLOCKS, 2, slots)
    return (output[None], grad_tokens[None], grad_qkv, grad_out_weight, grad_bias)


def solution(mesh):
    placed = (
        P("lev", "lat", "lon", None),
        P(),
        P(None, None, None, "lev"),
        P(None, "lev", None),
        P(None, "lev", None),
        P(),
        P("lat", "lon"),
        P("lat"),
        P("lev", "lat", "lon", None),
    )
    return jax.shard_map(
        on_device,
        mesh=mesh,
        in_specs=placed,
        out_specs=(
            P("lev", "lat", "lon", None),
            P("lev", "lat", "lon", None),
            P(None, None, None, "lev"),
            P(None, "lev", None),
            P(None, "lev", None),
        ),
        check_vma=False,
    )
```

```python
import functools

import jax
import jax.numpy as jnp
import numpy as np
from jax import lax
from jax.experimental import pallas as pl
from jax.experimental.pallas import tpu as pltpu
from jax.sharding import PartitionSpec as P

WL = 2
WH = 6
WW = 12
SPAN = WL * WH * WW
REACH = WW // 2
BLOCKS = 2
EPSILON = 1e-05
MASKED = -1e30
F32 = jnp.float32
BF16 = jnp.bfloat16

AXES = ("lon", "lev", "lat")
LEV = 8
RING = 4
OFFSETS = (0, 1, -1, 2)
SHARES = 2 * RING
STEP = 2
BIAS_ROWS = 16
VMEM = 56 * 1024 * 1024


def decode(device):
    lat, lev, lon = device % 2, device // 2 % LEV, device // (2 * LEV)
    return (2 * lat + lon // 8, lon // 2 % 4, lon % 2, lev)


def encode(x, y, core, lev):
    x, y, lev = x % RING, y % RING, lev % LEV
    return (((x % 2) * 8 + y * 2 + core) * LEV + lev) * 2 + x // 2


def send(value, target):
    pairs = [(i, encode(*target(*decode(i)))) for i in range(2 * RING * RING * LEV)]
    return lax.ppermute(value, AXES, pairs)


def along(value, ring, step):
    def target(x, y, core, lev):
        if (core == 0) == (ring == 1):
            return (x + step, y, core, lev)
        return (x, y + step, core, lev)

    return send(value, target)


def along_levels(value, step):
    return send(value, lambda x, y, core, lev: (x, y, core, lev + step))


def swap_cores(value):
    return send(value, lambda x, y, core, lev: (x, y, 1 - core, lev))


def swap_levels(value):
    return send(value, lambda x, y, core, lev: (x, y, core, lev ^ 1))


def to_window(value, step):
    def target(x, y, core, lev):
        lon = (x % 2) * 8 + y * 2 + core
        index = (2 * lon + lev % 2 + step) % 32
        lon, side = index // 2, index % 2
        return (2 * (x // 2) + lon // 8, lon // 2 % 4, lon % 2, lev - lev % 2 + side)

    return send(value, target)


def from_next_lon(value):
    def target(x, y, core, lev):
        lon = ((x % 2) * 8 + y * 2 + core - 1) % 16
        return (2 * (x // 2) + lon // 8, lon // 2 % 4, lon % 2, lev)

    return send(value, target)


def after(values, *others):
    tied = lax.optimization_barrier((values, others))
    return tied[0]


def share_order():
    lon, lat = lax.axis_index("lon"), lax.axis_index("lat")
    x, y, core = 2 * lat + lon // 8, lon // 2 % 4, lon % 2
    which = (core + jnp.arange(2, dtype=jnp.int32)[:, None]) % 2
    place = jnp.where(which == 0, y, x) + jnp.array(OFFSETS, jnp.int32)[None]
    return (which * RING + place % RING).reshape(-1).astype(jnp.int32)


def own_rows(qkv_weight, out_weight, block, share):
    width, parts, local = qkv_weight.shape[1:]
    rows = width // SHARES
    start = share * rows
    zero = jnp.zeros_like(start)
    into = lax.dynamic_slice(
        qkv_weight, (zero + block, start, zero, zero), (1, rows, parts, local)
    )[0]
    outof = lax.dynamic_slice(out_weight, (zero + block, zero, start), (1, local, rows))[0].T
    return jnp.concatenate([into[:, part] for part in range(parts)] + [outof], axis=1)


def table_rows(bias_table, columns):
    high = lax.reduce_precision(bias_table, 8, 7)
    middle = lax.reduce_precision(bias_table - high, 8, 7)
    low = bias_table - high - middle
    flat = jnp.stack([high, middle, low]).reshape(-1)
    rows = -(-flat.shape[0] // columns // BIAS_ROWS) * BIAS_ROWS
    return jnp.pad(flat, (0, rows * columns - flat.shape[0])).reshape(rows, columns).astype(BF16)


def gather_levels(own):
    up, down = [own], [own]
    for _ in range(3):
        up.append(along_levels(up[-1], -1))
        down.append(along_levels(down[-1], 1))
    up.append(along_levels(up[-1], -1))
    return up + down[:0:-1]


def scatter_levels(messages):
    up, down = messages[LEV // 2], messages[LEV // 2 + 1]
    for step in range(LEV // 2 - 1, 0, -1):
        up = add_low(messages[step], along_levels(up, 1))
        if step > 1:
            down = add_low(messages[LEV + 1 - step], along_levels(down, -1))
    return add_low(messages[0], along_levels(up, 1), along_levels(down, -1))


def pack_kernel(*refs):
    parts, weights, rest = refs[:LEV], refs[LEV], refs[LEV + 1 :]
    rows = weights.shape[2]
    for index, part in enumerate(parts):
        for half in range(2):
            weights[half, index] = part[half * rows : (half + 1) * rows]
        for out in rest:
            out[index] = part[2 * rows :]


def pack_levels(parts, rows):
    height, columns = parts[0].shape
    out_shape = [jax.ShapeDtypeStruct((2, LEV, rows // 2, columns), BF16)]
    if height > rows:
        out_shape.append(jax.ShapeDtypeStruct((LEV, height - rows, columns), BF16))
    return pl.pallas_call(
        pack_kernel,
        out_shape=out_shape,
        compiler_params=pltpu.CompilerParams(vmem_limit_bytes=VMEM),
    )(*parts)


def second_ring(own):
    ahead = along(own, 2, -1)
    behind = along(own, 2, 1)
    return (own, ahead, behind, along(ahead[0], 2, -1), along(behind[1], 2, 1))


def add_low(*terms):
    return functools.reduce(jnp.add, [term.astype(F32) for term in terms]).astype(BF16)


def scatter_start(grads):
    return (
        along(grads[6], 2, 1),
        along(grads[7], 2, -1),
        along(grads[3], 2, 1),
        along(grads[4], 2, -1),
    )


def scatter_middle(grads, far_a, far_b):
    return (
        along(add_low(grads[2], far_a), 2, 1),
        along(add_low(grads[5], far_b), 2, -1),
    )


def levels_kernel(*refs):
    parts, bias, outs = refs[: 6 * BLOCKS], refs[6 * BLOCKS], refs[6 * BLOCKS + 1 :]
    rows = parts[0].shape[1]
    for level, out in enumerate(outs):
        for place in range(2 * BLOCKS):
            own, ahead, behind = parts[3 * place : 3 * place + 3]
            out[pl.ds(place * rows, rows), :] = own[level] + (ahead[level] + behind[level])
        out[pl.ds(2 * BLOCKS * rows, BIAS_ROWS), :] = bias[level]


def whole_of(*extent):
    return pl.BlockSpec(extent, lambda order: (0,) * len(extent))


def finish_sums(parts, bias_rows):
    rows, columns = parts[0].shape[1:]
    height = 2 * BLOCKS * rows + BIAS_ROWS
    messages = pl.pallas_call(
        levels_kernel,
        out_shape=[jax.ShapeDtypeStruct((height, columns), BF16)] * LEV,
        compiler_params=pltpu.CompilerParams(vmem_limit_bytes=VMEM),
    )(*parts, bias_rows)
    total = scatter_levels(messages)
    total = add_low(total, along(total, 1, 1), along(total, 1, -1), along(total, 1, 2))
    mine = [total, along(total, 2, -1), along(total, 2, 1), along(total, 2, -2)]
    return mine + [swap_cores(item) for item in mine]


def pick(first, own, other):
    return jnp.where(first, own, other)


def enter_windows(field, even):
    left, right = field[..., :WW, :], field[..., WW:, :]
    keep = pick(even, left, right)
    got = swap_levels(pick(even, right, left))
    window = jnp.stack([pick(even, keep, got), pick(even, got, keep)], axis=-4)
    window = jnp.moveaxis(window, -2, -4)
    flat = window.reshape(window.shape[:-4] + (SPAN, window.shape[-1]))
    return flat[..., : SPAN // 2, :], flat[..., SPAN // 2 :, :]


def leave_windows(halves, even):
    shape = (REACH, WL, WH, halves[0].shape[-1])
    window = jnp.concatenate([item.reshape(shape) for item in halves]).transpose(1, 2, 0, 3)
    own = pick(even, window[0], window[1])
    got = swap_levels(pick(even, window[1], window[0]))
    return jnp.concatenate([pick(even, own, got), pick(even, got, own)], axis=1)


def wrap_left(halves):
    return (halves[1], to_window(halves[0], -1))


def wrap_right(halves):
    return (to_window(halves[1], 1), halves[0])


def by_half(values):
    return jnp.broadcast_to(values.T[:, None], (WW, WL, WH)).reshape(1, SPAN)


ROW_GROUPS = WL * WH
LINES = (2 * WL - 1) * (2 * WH - 1)
STEPS = 2 * WW - 1


CORNERS = [p * WH * WW + q * WW + r for p in (0, WL - 1) for q in (0, WH - 1) for r in (0, WW - 1)]


LANES = 32
WIDE = 256
REVERSED = LINES * LANES


def offset_places():
    table = np.zeros((len(CORNERS) * SPAN, REVERSED), np.float32)
    for a in range(1 - WL, WL):
        for b in range(1 - WH, WH):
            for c in range(1 - WW, WW):
                p = [(size - 1) * (step > 0) for size, step in ((WL, a), (WH, b), (WW, c))]
                k = [at - step for at, step in zip(p, (a, b, c))]
                row = CORNERS.index((p[0] * WH + p[1]) * WW + p[2])
                offset = ((WL - 1 - a) * (2 * WH - 1) + WH - 1 - b) * LANES + c + WW - 1
                table[row * SPAN + (k[0] * WH + k[1]) * WW + k[2], offset] = 1
    return table


def line_lanes(line):
    level, row = line // WH, line % WH
    for other in range(WL):
        yield other, ((WL - 1 - level + other) * (2 * WH - 1) + WH - 1 - row) * LANES


def column_table():
    table = np.zeros((ROW_GROUPS, LANES, WW, WIDE), np.float32)
    for line in range(ROW_GROUPS):
        for p in range(WW):
            for k in range(WW):
                table[line, p - k + WW - 1, p, k * ROW_GROUPS + line] = 1
    return table.reshape(ROW_GROUPS * LANES, WW * WIDE).astype(BF16)


def slot_table(rel_index, slots):
    rows = jnp.concatenate([rel_index[at : at + 1] for at in CORNERS], axis=1)
    digits = jnp.concatenate([rows // 32, rows % 32]).astype(BF16)
    places = dot(digits, offset_places().astype(BF16))
    named = np.arange(REVERSED) % LANES < STEPS
    names = jnp.where(named, places[0] * 32 + places[1], -1).astype(jnp.int32)
    return (names[:, None] == jnp.arange(slots)[None, :]).astype(BF16)


TILE = 128


def bias_kernel(steps, columns, out, rows, spread):
    count = steps.shape[0] // 3
    side = WH * LANES

    @pl.when(pl.program_id(0) == 0)
    def _():
        for line in range(ROW_GROUPS):
            for other, lane in line_lanes(line):
                value = steps[:, lane : lane + side]
                for part in range(3):
                    start = (part * ROW_GROUPS + line) * count
                    rows[start : start + count, other * side : (other + 1) * side] = value[
                        part * count : (part + 1) * count
                    ]

    values = dot(rows[...], columns[...])
    size = ROW_GROUPS * count
    values = values[:size] + values[size : 2 * size] + values[2 * size :]
    for tile in range(WIDE // TILE):
        lanes = slice(tile * TILE, (tile + 1) * TILE)
        for line in range(ROW_GROUPS):
            spread[tile, pl.ds(line, count, ROW_GROUPS), :] = values[
                line * count : (line + 1) * count, lanes
            ]
        out[:, lanes] = spread[tile]


def expand_bias(tables, by_slot):
    count = tables.shape[1]
    steps = dot_nt(tables.reshape(3 * count, -1), by_slot).astype(BF16)
    return pl.pallas_call(
        bias_kernel,
        grid=(WW,),
        in_specs=[
            pl.BlockSpec(steps.shape, lambda c: (0, 0)),
            pl.BlockSpec((ROW_GROUPS * LANES, WIDE), lambda c: (0, c)),
        ],
        out_specs=pl.BlockSpec((count * ROW_GROUPS, WIDE), lambda c: (0, c)),
        out_shape=jax.ShapeDtypeStruct((count * ROW_GROUPS, WW * WIDE), F32),
        scratch_shapes=[
            pltpu.VMEM((3 * ROW_GROUPS * count, ROW_GROUPS * LANES), BF16),
            pltpu.VMEM((WIDE // TILE, ROW_GROUPS * count, TILE), F32),
        ],
        compiler_params=pltpu.CompilerParams(vmem_limit_bytes=VMEM),
    )(steps, column_table())


def slots_kernel(*refs):
    scores, columns, out, lines = refs[:BLOCKS], refs[BLOCKS], refs[BLOCKS + 1], refs[BLOCKS + 2]
    size = scores[0].shape[0]
    count = BLOCKS * size // ROW_GROUPS
    side = WH * LANES

    @pl.when(pl.program_id(0) == 0)
    def _():
        lines[...] = jnp.zeros_like(lines)

    for block in range(BLOCKS):
        part = dot_nt(scores[block][...].astype(BF16), columns[...])
        for tile in range(lines.shape[0]):
            lines[tile, pl.ds(block * size, size), :] += part[:, tile * TILE : (tile + 1) * TILE]

    @pl.when(pl.program_id(0) == WW - 1)
    def _():
        out[...] = jnp.zeros_like(out)
        for line in range(ROW_GROUPS):
            values = jnp.concatenate(
                [lines[tile, pl.ds(line, count, ROW_GROUPS), :] for tile in range(lines.shape[0])],
                axis=1,
            )
            for other, lane in line_lanes(line):
                out[:, lane : lane + side] += values[:, other * side : (other + 1) * side]


def slot_sums(scores, by_slot):
    size = scores[0].shape[0]
    count = BLOCKS * size // ROW_GROUPS
    wide = ROW_GROUPS * LANES
    steps = pl.pallas_call(
        slots_kernel,
        grid=(WW,),
        in_specs=[pl.BlockSpec((size, WIDE), lambda c: (0, c))] * BLOCKS
        + [pl.BlockSpec((wide, WIDE), lambda c: (0, c))],
        out_specs=pl.BlockSpec((count, REVERSED), lambda c: (0, 0)),
        out_shape=jax.ShapeDtypeStruct((count, REVERSED), F32),
        scratch_shapes=[pltpu.VMEM((wide // TILE, BLOCKS * size, TILE), F32)],
        compiler_params=pltpu.CompilerParams(vmem_limit_bytes=VMEM),
    )(*scores, column_table())
    return dot(steps.astype(BF16), by_slot)


def dot(a, b):
    return jnp.dot(a, b, preferred_element_type=F32)


def dot_nt(a, b):
    return lax.dot_general(a, b, (((1,), (1,)), ((), ())), preferred_element_type=F32)


def dot_tn(a, b):
    return lax.dot_general(a, b, (((0,), (0,)), ((), ())), preferred_element_type=F32)


def standardise(field):
    values = field.astype(F32)
    centre = jnp.mean(values, axis=-1, keepdims=True)
    spread = jnp.mean((values - centre) ** 2, axis=-1, keepdims=True)
    inv_spread = lax.rsqrt(spread + EPSILON)
    return (values - centre) * inv_spread, inv_spread


def norm_adjoint(cotan, field, gain):
    normed, inv_spread = standardise(field)
    scaled = cotan.astype(F32) * gain
    first = jnp.mean(scaled, axis=-1, keepdims=True)
    second = jnp.mean(scaled * normed, axis=-1, keepdims=True)
    return inv_spread * (scaled - first - normed * second)


def piece_slots():
    for index in range(PIECES):
        side, place = index // (RING * RING), index % (RING * RING)
        yield index, side, place


def collect_rows(order, pieces, weights, sub):
    rows = pieces[0].shape[2]
    for index in range(SHARES):
        side, place = index // RING, index % RING
        for half in range(2):
            if place < RING - 1:
                values = pieces[5 * side + place][half, sub]
            else:
                values = pieces[5 * side + RING - 1 + half][sub]
            start = pl.multiple_of((2 * order[index] + half) * rows, rows)
            weights[sub, pl.ds(start, rows), :] = values


def join(halves):
    return jnp.concatenate([item[...].astype(F32) for item in halves], axis=0)


def split(values, halves):
    halves[0][...] = values[: SPAN // 2].astype(BF16)
    halves[1][...] = values[SPAN // 2 :].astype(BF16)


def head_masks(width):
    lane = lax.broadcasted_iota(jnp.int32, (1, width), 1)
    return [(lane // (width // 2) == head).astype(F32).astype(BF16) for head in range(2)]


def forward_kernel(order, *refs):
    halves, (gain, marks, bias), pieces = refs[:2], refs[2:5], refs[5:15]
    after, (packed_out, mixed_out, probs_out) = refs[15:17], refs[17:20]
    weights, normed, total, allowed, added = refs[20:]
    group = pl.program_id(0)
    local = mixed_out.shape[-1]

    @pl.when(group == 0)
    def _():
        values, _ = standardise(join(halves))
        normed[...] = (values * gain[...]).astype(BF16)
        total[...] = jnp.zeros_like(total)
        here = lax.broadcasted_iota(jnp.int32, (SPAN, SPAN), 0)
        there = lax.broadcasted_iota(jnp.int32, (SPAN, SPAN), 1)
        labels = jnp.broadcast_to(marks[0:1].astype(F32), (SPAN, SPAN))
        living = jnp.broadcast_to(marks[1:2], (SPAN, SPAN))
        seen = (labels == labels.T) & ((living > 0) | (here == there))
        allowed[...] = jnp.where(seen, 1.0, 0.0)

    scale = (local // 2) ** (-0.5)
    for sub in range(STEP):
        collect_rows(order, pieces, weights, sub)
        for head in range(2):
            for column in range(WW):
                rows = pl.ds((2 * sub + head) * ROW_GROUPS, ROW_GROUPS)
                lanes = pl.ds(column * WIDE, SPAN)
                place = pl.ds(column * ROW_GROUPS, ROW_GROUPS)
                added[2 * sub + head, place, :] = bias[rows, lanes]
    masks = head_masks(local)
    heads = [(sub, head) for sub in range(STEP) for head in range(2)]
    queries, keys, values = [], [], []
    for sub in range(STEP):
        packed = dot(normed[...], weights[sub, :, : 3 * local]).astype(BF16)
        packed_out[sub] = packed
        queries.append(packed[:, :local])
        keys.append(packed[:, local : 2 * local])
        values.append(packed[:, 2 * local :])
    seen = allowed[...] > 0
    scores = [dot_nt(queries[sub], keys[sub] * masks[head]) for sub, head in heads]
    scores = [
        jnp.where(seen, item * scale + added[index], MASKED) for index, item in enumerate(scores)
    ]
    tops = [jnp.max(item, axis=-1, keepdims=True) for item in scores]
    grown = [jnp.exp(item - top) for item, top in zip(scores, tops)]
    sums = [jnp.sum(item, axis=-1, keepdims=True) for item in grown]
    probs = [item / total_weight for item, total_weight in zip(grown, sums)]
    for index, item in enumerate(probs):
        probs_out[index] = item
    parts = [
        dot(item.astype(BF16), values[sub] * masks[head])
        for item, (sub, head) in zip(probs, heads)
    ]
    mixed = [(parts[2 * sub] + parts[2 * sub + 1]).astype(BF16) for sub in range(STEP)]
    branch = total[...]
    for sub in range(STEP):
        mixed_out[sub] = mixed[sub]
        branch = branch + dot_nt(mixed[sub], weights[sub, :, 3 * local :]).astype(BF16).astype(F32)
    total[...] = branch

    @pl.when(group == LEV // STEP - 1)
    def _():
        split(join(halves) + total[...].astype(BF16).astype(F32), after)


def backward_kernel(last, order, *refs):
    refs = list(refs)

    def take(count):
        taken, refs[:] = refs[:count], refs[count:]
        return taken

    grad_out = take(2)
    later_grad, later_field = (take(2), take(2)) if last else (None, None)
    later_gain = take(1)[0] if last else None
    field, (gain, packed_in, mixed_in, probs_in), pieces = take(2), take(4), take(10)
    outs, (scores_out, operands) = take(2), take(2)
    weights, normed, up, total = take(4)
    carried = take(1)[0] if last else None
    step = pl.program_id(0)
    local = mixed_in.shape[-1]

    @pl.when(step == 0)
    def _():
        values, _ = standardise(join(field))
        normed[...] = (values * gain[...]).astype(BF16)
        upstream = join(grad_out)
        if last:
            upstream = upstream + norm_adjoint(join(later_grad), join(later_field), later_gain[...])
            carried[...] = upstream
        up[...] = upstream.astype(BF16)
        total[...] = jnp.zeros_like(total)

    scores_out[...] = jnp.zeros_like(scores_out)
    scale = (local // 2) ** (-0.5)
    for sub in range(STEP):
        collect_rows(order, pieces, weights, sub)
    masks = head_masks(local)
    heads = [(sub, head) for sub in range(STEP) for head in range(2)]
    packed = [packed_in[sub] for sub in range(STEP)]
    queries, keys, values = (
        [item[:, part * local : (part + 1) * local] for item in packed] for part in range(3)
    )
    cotans = [dot(up[...], weights[sub, :, 3 * local :]).astype(BF16) for sub in range(STEP)]
    grad_probs = [dot_nt(cotans[sub], values[sub] * masks[head]) for sub, head in heads]
    probs = [probs_in[index] for index in range(2 * STEP)]
    grad_value = [
        dot_tn(item.astype(BF16), cotans[sub] * masks[head])
        for item, (sub, head) in zip(probs, heads)
    ]
    inner = [
        jnp.sum(grad * item, axis=-1, keepdims=True) for grad, item in zip(grad_probs, probs)
    ]
    grad_scores = [
        item * (grad - dotted) for item, grad, dotted in zip(probs, grad_probs, inner)
    ]
    for index, item in enumerate(grad_scores):
        for column in range(WW):
            rows = pl.ds(index * ROW_GROUPS, ROW_GROUPS)
            lanes = pl.ds(column * WIDE, SPAN)
            scores_out[rows, lanes] = item[column * ROW_GROUPS : (column + 1) * ROW_GROUPS]
    low = [item.astype(BF16) for item in grad_scores]
    grad_query = [dot(item, keys[sub] * masks[head]) for item, (sub, head) in zip(low, heads)]
    grad_keys = [dot_tn(item, queries[sub] * masks[head]) for item, (sub, head) in zip(low, heads)]
    grad_normed = total[...]
    for sub in range(STEP):
        first, second = 2 * sub, 2 * sub + 1
        grad_packed = jnp.concatenate(
            [
                ((grad_query[first] + grad_query[second]) * scale).astype(BF16),
                ((grad_keys[first] + grad_keys[second]) * scale).astype(BF16),
                (grad_value[first] + grad_value[second]).astype(BF16),
            ],
            axis=1,
        )
        part = dot_nt(grad_packed, weights[sub, :, : 3 * local])
        grad_normed = grad_normed + part.astype(BF16).astype(F32)
        here = pl.ds(pl.multiple_of((STEP * step + sub) * local, local), local)
        operands[sub, :, : 3 * local] = grad_packed
        operands[sub, :, 3 * local : 4 * local] = mixed_in[sub]
        operands[sub, :, 4 * local : 5 * local] = normed[:, here]
        operands[sub, :, 5 * local :] = up[:, here]
    total[...] = grad_normed

    @pl.when(step == LEV // STEP - 1)
    def _():
        if last:
            grad_normed = total[...].astype(BF16)
            split(carried[...] + norm_adjoint(grad_normed, join(field), gain[...]), outs)
        else:
            split(total[...], outs)


def weights_kernel(order, mine, other, *refs):
    outs, (turned, normed, up) = refs[:8], refs[8:]
    step = pl.program_id(0)
    local = mine.shape[-1] // 6
    rows = normed.shape[0] // RING
    core = order[0] // RING

    @pl.when(step == 0)
    def _():
        for side, source in enumerate((mine, other)):
            for target, column in ((normed, 4 * local), (up, 5 * local)):
                for level in range(LEV // 2):
                    part = source[core * (LEV // 2) + level, :, column : column + local]
                    turned[level * local : (level + 1) * local] = part.T
                for place in range(RING):
                    start = pl.multiple_of((order[place] - core * RING) * rows, rows)
                    target[place * rows : (place + 1) * rows, side * SPAN : (side + 1) * SPAN] = (
                        turned[pl.ds(start, rows), :]
                    )

    packed = jnp.concatenate([item[step, :, : 3 * local] for item in (mine, other)])
    mixed = jnp.concatenate([item[step, :, 3 * local : 4 * local] for item in (mine, other)])
    into = dot(normed[...], packed).astype(BF16)
    outof = dot(up[...], mixed).astype(BF16)
    half = rows // 2
    for index, out in enumerate(outs):
        out[0, :, : 3 * local] = into[index * half : (index + 1) * half]
        out[0, :, 3 * local :] = outof[index * half : (index + 1) * half]


def finish_kernel(order, *refs):
    inputs, (into, outof, bias, turned) = refs[:SHARES], refs[SHARES:]
    rows = into.shape[2] // SHARES
    local = outof.shape[1]
    bias_total = jnp.zeros(bias.shape, F32)
    for source in inputs:
        bias_total += source[BLOCKS * rows :, :].astype(F32)
    bias[...] = bias_total
    for block in range(BLOCKS):
        for index, source in enumerate(inputs):
            start = pl.multiple_of(order[index] * rows, rows)
            values = source[block * rows : (block + 1) * rows, :].astype(F32)
            for part in range(3):
                into[block, part, pl.ds(start, rows), :] = values[:, part * local : (part + 1) * local]
            turned[pl.ds(start, rows), :] = values[:, 3 * local :]
        outof[block] = turned[...].T


def whole(*shape):
    return pl.BlockSpec(shape, lambda g, order: (0,) * len(shape))


def by_group(*shape):
    return pl.BlockSpec((STEP,) + shape, lambda g, order: (g,) + (0,) * len(shape))


def by_head():
    return pl.BlockSpec((2 * STEP, SPAN, SPAN), lambda g, order: (g, 0, 0))


def by_rows(base):
    start = base // STEP
    return pl.BlockSpec((2 * STEP * ROW_GROUPS, WW * WIDE), lambda g, order: (g + start, 0))


def piece_specs(rows, columns):
    pair = pl.BlockSpec((2, STEP, rows, columns), lambda g, order: (0, g, 0, 0))
    return ([pair] * (RING - 1) + [by_group(rows, columns)] * 2) * 2


def cost(flops, bytes_accessed):
    return pl.CostEstimate(flops=flops, bytes_accessed=bytes_accessed, transcendentals=0)


def run_forward(order, halves, gain, marks, bias, block, pieces):
    width = halves[0].shape[1]
    rows, columns = pieces[0].shape[2:]
    local = columns // 4
    shape = jax.ShapeDtypeStruct
    first, second, *saved = pl.pallas_call(
        forward_kernel,
        grid_spec=pltpu.PrefetchScalarGridSpec(
            num_scalar_prefetch=1,
            grid=(LEV // STEP,),
            in_specs=[
                whole(SPAN // 2, width),
                whole(SPAN // 2, width),
                whole(1, width),
                whole(2, SPAN),
                by_rows(block * LEV),
                *piece_specs(rows, columns),
            ],
            out_specs=[
                whole(SPAN // 2, width),
                whole(SPAN // 2, width),
                by_group(SPAN, 3 * local),
                by_group(SPAN, local),
                by_head(),
            ],
            scratch_shapes=[
                pltpu.VMEM((STEP, width, columns), BF16),
                pltpu.VMEM((SPAN, width), BF16),
                pltpu.VMEM((SPAN, width), F32),
                pltpu.VMEM((SPAN, SPAN), F32),
                pltpu.VMEM((2 * STEP, SPAN, SPAN), F32),
            ],
        ),
        out_shape=[
            shape((SPAN // 2, width), BF16),
            shape((SPAN // 2, width), BF16),
            shape((LEV, SPAN, 3 * local), BF16),
            shape((LEV, SPAN, local), BF16),
            shape((2 * LEV, SPAN, SPAN), F32),
        ],
        compiler_params=pltpu.CompilerParams(vmem_limit_bytes=VMEM),
        cost_estimate=cost(14 * 10**9, 2 * 10**7),
    )(order, *halves, gain, marks, bias, *pieces)
    return (first, second), saved


def run_backward(order, last, upstream, halves, gain, saved, pieces):
    width = halves[0].shape[1]
    rows, columns = pieces[0].shape[2:]
    local = columns // 4
    shape = jax.ShapeDtypeStruct
    half = whole(SPAN // 2, width)
    above = [half] * 2
    scratch = [
        pltpu.VMEM((STEP, width, columns), BF16),
        pltpu.VMEM((SPAN, width), BF16),
        pltpu.VMEM((SPAN, width), BF16),
        pltpu.VMEM((SPAN, width), F32),
    ]
    if last:
        above += [half] * 4 + [whole(1, width)]
        scratch.append(pltpu.VMEM((SPAN, width), F32))
    first, second, scores, operands = pl.pallas_call(
        functools.partial(backward_kernel, last),
        grid_spec=pltpu.PrefetchScalarGridSpec(
            num_scalar_prefetch=1,
            grid=(LEV // STEP,),
            in_specs=[
                *above,
                half,
                half,
                whole(1, width),
                by_group(SPAN, 3 * local),
                by_group(SPAN, local),
                by_head(),
                *piece_specs(rows, columns),
            ],
            out_specs=[half, half, by_rows(0), by_group(SPAN, 6 * local)],
            scratch_shapes=scratch,
        ),
        out_shape=[
            shape((SPAN // 2, width), BF16),
            shape((SPAN // 2, width), BF16),
            shape((2 * LEV * ROW_GROUPS, WW * WIDE), F32),
            shape((LEV, SPAN, 6 * local), BF16),
        ],
        compiler_params=pltpu.CompilerParams(vmem_limit_bytes=VMEM),
        cost_estimate=cost(14 * 10**9, 2 * 10**7),
    )(order, *upstream, *halves, gain, *saved, *pieces)
    return (first, second), scores, operands


def run_weights(order, mine, other, rows):
    local = mine.shape[-1] // 6
    width, columns = LEV * local, 4 * local
    return pl.pallas_call(
        weights_kernel,
        grid_spec=pltpu.PrefetchScalarGridSpec(
            num_scalar_prefetch=1,
            grid=(LEV,),
            in_specs=[whole(*mine.shape), whole(*other.shape)],
            out_specs=[pl.BlockSpec((1, rows, columns), lambda g, order: (g, 0, 0))] * 8,
            scratch_shapes=[
                pltpu.VMEM((width // 2, SPAN), BF16),
                pltpu.VMEM((width // 2, 2 * SPAN), BF16),
                pltpu.VMEM((width // 2, 2 * SPAN), BF16),
            ],
        ),
        out_shape=[jax.ShapeDtypeStruct((LEV, rows, columns), BF16)] * 8,
        compiler_params=pltpu.CompilerParams(vmem_limit_bytes=VMEM),
        cost_estimate=cost(5 * 10**9, 10**7),
    )(order, mine, other)


def run_finish(order, parts, width, local):
    shape = jax.ShapeDtypeStruct

    shapes = [
        (BLOCKS, 3, width, local),
        (BLOCKS, local, width),
        (BIAS_ROWS, 4 * local),
    ]
    return pl.pallas_call(
        finish_kernel,
        grid_spec=pltpu.PrefetchScalarGridSpec(
            num_scalar_prefetch=1,
            grid=(),
            in_specs=[whole_of(*item.shape) for item in parts],
            out_specs=[whole_of(*extent) for extent in shapes],
            scratch_shapes=[pltpu.VMEM((width, local), F32)],
        ),
        out_shape=[shape(extent, F32) for extent in shapes],
        compiler_params=pltpu.CompilerParams(vmem_limit_bytes=VMEM),
    )(order, *parts)


def bias_message(scores, by_slot, columns):
    sums = slot_sums(scores, by_slot)
    slots = sums.shape[-1]
    flat = sums.reshape(BLOCKS, LEV, 2 * slots).transpose(1, 0, 2).reshape(LEV, -1)
    flat = jnp.pad(flat, ((0, 0), (0, BIAS_ROWS * columns - flat.shape[1])))
    return flat.reshape(LEV, BIAS_ROWS, columns).astype(BF16)


def on_device(
    tokens,
    norm_gain,
    qkv_weight,
    out_weight,
    bias_table,
    rel_index,
    region_ids,
    row_valid,
    grad_out,
):
    width = tokens.shape[-1]
    local = qkv_weight.shape[-1]
    slots = bias_table.shape[-1]
    columns = 4 * local
    rows = width // SHARES
    even = lax.axis_index("lev") % 2 == 0
    order = share_order()
    gains = [norm_gain[block : block + 1] for block in range(BLOCKS)]

    own = [own_rows(qkv_weight, out_weight, b, order[0]) for b in range(BLOCKS)]
    own[0] = jnp.concatenate([own[0], table_rows(bias_table, columns)])
    part, tables = pack_levels(gather_levels(own[0]), rows)
    pieces_0 = second_ring(part)
    own[1], tokens, grad_out = after((own[1], tokens, grad_out), part)
    (part,) = pack_levels(gather_levels(own[1]), rows)
    pieces_1 = second_ring(after(part, *pieces_0[3:]))
    pieces_0 = pieces_0 + tuple(swap_cores(item) for item in pieces_0)

    both = enter_windows(jnp.concatenate([tokens, grad_out]), even)
    start = tuple(item[0] for item in both)
    grad_start = tuple(item[1] for item in both)
    grad_shifted = wrap_left(grad_start)

    following = from_next_lon(region_ids[:, :REACH])
    shifted = jnp.concatenate([region_ids[:, REACH:], following], axis=1)
    living = by_half(jnp.broadcast_to(row_valid[:, None], (WH, WW)))
    marks = [
        jnp.concatenate([by_half(pick(even, item[:, :WW], item[:, WW:])), living])
        for item in (region_ids, shifted)
    ]

    by_slot = slot_table(rel_index, slots)
    parts = tables.reshape(LEV, -1)[:, : 3 * bias_table.size]
    parts = parts.reshape(LEV, 3, BLOCKS, 2, slots).transpose(1, 2, 0, 3, 4)
    bias = expand_bias(parts.reshape(3, BLOCKS * 2 * LEV, slots), by_slot)

    middle, saved_0 = run_forward(order, start, gains[0], marks[0], bias, 0, pieces_0)
    second = wrap_left(middle)
    pieces_1 = pieces_1[:1] + tuple(after(pieces_1[1:], middle[0]))
    pieces_1 = pieces_1 + tuple(swap_cores(item) for item in pieces_1)
    ended, saved_1 = run_forward(order, second, gains[1], marks[1], bias, 1, pieces_1)

    grad_normed, scores_1, operands = run_backward(
        order, False, grad_shifted, second, gains[1], saved_1, pieces_1
    )
    later_grad = wrap_right(grad_normed)
    grads_1 = run_weights(order, operands, swap_cores(operands), rows // 2)
    far_a, far_b, ahead_b, behind_a = scatter_start(grads_1)

    upstream = after([*grad_start, *later_grad, *middle, gains[1]], *grads_1)
    grad_first, scores_0, operands = run_backward(
        order, True, upstream, start, gains[0], saved_0, pieces_0
    )
    operands, far_a, far_b, ahead_b, behind_a = after(
        (operands, far_a, far_b, ahead_b, behind_a)
    )
    ahead_a, behind_b = scatter_middle(grads_1, far_a, far_b)
    grads_0 = run_weights(order, operands, swap_cores(operands), rows // 2)
    parts_1 = (grads_1[0], ahead_a, behind_a, grads_1[1], ahead_b, behind_b)
    far_a, far_b, ahead_b, behind_a = scatter_start(grads_0)
    ahead_a, behind_b = scatter_middle(grads_0, far_a, far_b)
    parts_0 = (grads_0[0], ahead_a, behind_a, grads_0[1], ahead_b, behind_b)

    message = bias_message((scores_0, scores_1), by_slot, columns)
    finished = finish_sums(parts_0 + parts_1, message)
    grad_tokens = leave_windows(grad_first, even)
    ended = after(ended, grad_first)
    output = leave_windows(wrap_right(ended), even)

    grad_qkv, grad_out_weight, bias_rows = run_finish(order, finished, width, local)
    grad_qkv = grad_qkv.transpose(0, 2, 1, 3)
    grad_bias = bias_rows.reshape(-1)[: BLOCKS * 2 * slots].reshape(BLOCKS, 2, slots)
    return (output[None], grad_tokens[None], grad_qkv, grad_out_weight, grad_bias)


def solution(mesh):
    placed = (
        P("lev", "lat", "lon", None),
        P(),
        P(None, None, None, "lev"),
        P(None, "lev", None),
        P(None, "lev", None),
        P(),
        P("lat", "lon"),
        P("lat"),
        P("lev", "lat", "lon", None),
    )
    return jax.shard_map(
        on_device,
        mesh=mesh,
        in_specs=placed,
        out_specs=(
            P("lev", "lat", "lon", None),
            P("lev", "lat", "lon", None),
            P(None, None, None, "lev"),
            P(None, "lev", None),
            P(None, "lev", None),
        ),
        check_vma=False,
    )
```

```python
import functools

import jax
import jax.numpy as jnp
import numpy as np
from jax import lax
from jax.experimental import pallas as pl
from jax.experimental.pallas import tpu as pltpu
from jax.sharding import PartitionSpec as P

WL = 2
WH = 6
WW = 12
SPAN = WL * WH * WW
REACH = WW // 2
BLOCKS = 2
EPSILON = 1e-05
MASKED = -1e30
F32 = jnp.float32
BF16 = jnp.bfloat16

AXES = ("lon", "lev", "lat")
LEV = 8
RING = 4
OFFSETS = (0, 1, -1, 2)
SHARES = 2 * RING
STEP = 2
BIAS_ROWS = 16
VMEM = 56 * 1024 * 1024


def decode(device):
    lat, lev, lon = device % 2, device // 2 % LEV, device // (2 * LEV)
    return (2 * lat + lon // 8, lon // 2 % 4, lon % 2, lev)


def encode(x, y, core, lev):
    x, y, lev = x % RING, y % RING, lev % LEV
    return (((x % 2) * 8 + y * 2 + core) * LEV + lev) * 2 + x // 2


def send(value, target):
    pairs = [(i, encode(*target(*decode(i)))) for i in range(2 * RING * RING * LEV)]
    return lax.ppermute(value, AXES, pairs)


def along(value, ring, step):
    def target(x, y, core, lev):
        if (core == 0) == (ring == 1):
            return (x + step, y, core, lev)
        return (x, y + step, core, lev)

    return send(value, target)


def along_levels(value, step):
    return send(value, lambda x, y, core, lev: (x, y, core, lev + step))


def swap_cores(value):
    return send(value, lambda x, y, core, lev: (x, y, 1 - core, lev))


def swap_levels(value):
    return send(value, lambda x, y, core, lev: (x, y, core, lev ^ 1))


def to_window(value, step):
    def target(x, y, core, lev):
        lon = (x % 2) * 8 + y * 2 + core
        index = (2 * lon + lev % 2 + step) % 32
        lon, side = index // 2, index % 2
        return (2 * (x // 2) + lon // 8, lon // 2 % 4, lon % 2, lev - lev % 2 + side)

    return send(value, target)


def from_next_lon(value):
    def target(x, y, core, lev):
        lon = ((x % 2) * 8 + y * 2 + core - 1) % 16
        return (2 * (x // 2) + lon // 8, lon // 2 % 4, lon % 2, lev)

    return send(value, target)


def after(values, *others):
    tied = lax.optimization_barrier((values, others))
    return tied[0]


def share_order():
    lon, lat = lax.axis_index("lon"), lax.axis_index("lat")
    x, y, core = 2 * lat + lon // 8, lon // 2 % 4, lon % 2
    which = (core + jnp.arange(2, dtype=jnp.int32)[:, None]) % 2
    place = jnp.where(which == 0, y, x) + jnp.array(OFFSETS, jnp.int32)[None]
    return (which * RING + place % RING).reshape(-1).astype(jnp.int32)


def own_rows(qkv_weight, out_weight, block, share):
    width, parts, local = qkv_weight.shape[1:]
    rows = width // SHARES
    start = share * rows
    zero = jnp.zeros_like(start)
    into = lax.dynamic_slice(
        qkv_weight, (zero + block, start, zero, zero), (1, rows, parts, local)
    )[0]
    outof = lax.dynamic_slice(out_weight, (zero + block, zero, start), (1, local, rows))[0].T
    return jnp.concatenate([into[:, part] for part in range(parts)] + [outof], axis=1)


def table_rows(bias_table, columns):
    high = lax.reduce_precision(bias_table, 8, 7)
    middle = lax.reduce_precision(bias_table - high, 8, 7)
    low = bias_table - high - middle
    flat = jnp.stack([high, middle, low]).reshape(-1)
    rows = -(-flat.shape[0] // columns // BIAS_ROWS) * BIAS_ROWS
    return jnp.pad(flat, (0, rows * columns - flat.shape[0])).reshape(rows, columns).astype(BF16)


def gather_levels(own):
    up, down = [own], [own]
    for _ in range(3):
        up.append(along_levels(up[-1], -1))
        down.append(along_levels(down[-1], 1))
    up.append(along_levels(up[-1], -1))
    return up + down[:0:-1]


def scatter_levels(messages):
    up, down = messages[LEV // 2], messages[LEV // 2 + 1]
    for step in range(LEV // 2 - 1, 0, -1):
        up = add_low(messages[step], along_levels(up, 1))
        if step > 1:
            down = add_low(messages[LEV + 1 - step], along_levels(down, -1))
    return add_low(messages[0], along_levels(up, 1), along_levels(down, -1))


def pack_kernel(*refs):
    parts, weights, rest = refs[:LEV], refs[LEV], refs[LEV + 1 :]
    rows = weights.shape[2]
    for index, part in enumerate(parts):
        for half in range(2):
            weights[half, index] = part[half * rows : (half + 1) * rows]
        for out in rest:
            out[index] = part[2 * rows :]


def pack_levels(parts, rows):
    height, columns = parts[0].shape
    out_shape = [jax.ShapeDtypeStruct((2, LEV, rows // 2, columns), BF16)]
    if height > rows:
        out_shape.append(jax.ShapeDtypeStruct((LEV, height - rows, columns), BF16))
    return pl.pallas_call(
        pack_kernel,
        out_shape=out_shape,
        compiler_params=pltpu.CompilerParams(vmem_limit_bytes=VMEM),
    )(*parts)


def second_ring(own):
    ahead = along(own, 2, -1)
    behind = along(own, 2, 1)
    return (own, ahead, behind, along(ahead[0], 2, -1), along(behind[1], 2, 1))


def add_low(*terms):
    return functools.reduce(jnp.add, [term.astype(F32) for term in terms]).astype(BF16)


def scatter_start(grads):
    return (
        along(grads[6], 2, 1),
        along(grads[7], 2, -1),
        along(grads[3], 2, 1),
        along(grads[4], 2, -1),
    )


def scatter_middle(grads, far_a, far_b):
    return (
        along(add_low(grads[2], far_a), 2, 1),
        along(add_low(grads[5], far_b), 2, -1),
    )


def levels_kernel(*refs):
    parts, bias, outs = refs[: 6 * BLOCKS], refs[6 * BLOCKS], refs[6 * BLOCKS + 1 :]
    rows = parts[0].shape[1]
    for level, out in enumerate(outs):
        for place in range(2 * BLOCKS):
            own, ahead, behind = parts[3 * place : 3 * place + 3]
            out[pl.ds(place * rows, rows), :] = own[level] + (ahead[level] + behind[level])
        out[pl.ds(2 * BLOCKS * rows, BIAS_ROWS), :] = bias[level]


def whole_of(*extent):
    return pl.BlockSpec(extent, lambda order: (0,) * len(extent))


def finish_sums(parts, bias_rows):
    rows, columns = parts[0].shape[1:]
    height = 2 * BLOCKS * rows + BIAS_ROWS
    messages = pl.pallas_call(
        levels_kernel,
        out_shape=[jax.ShapeDtypeStruct((height, columns), BF16)] * LEV,
        compiler_params=pltpu.CompilerParams(vmem_limit_bytes=VMEM),
    )(*parts, bias_rows)
    total = scatter_levels(messages)
    total = add_low(total, along(total, 1, 1), along(total, 1, -1), along(total, 1, 2))
    mine = [total, along(total, 2, -1), along(total, 2, 1), along(total, 2, -2)]
    return mine + [swap_cores(item) for item in mine]


def pick(first, own, other):
    return jnp.where(first, own, other)


def enter_windows(field, even):
    left, right = field[..., :WW, :], field[..., WW:, :]
    keep = pick(even, left, right)
    got = swap_levels(pick(even, right, left))
    window = jnp.stack([pick(even, keep, got), pick(even, got, keep)], axis=-4)
    window = jnp.moveaxis(window, -2, -4)
    flat = window.reshape(window.shape[:-4] + (SPAN, window.shape[-1]))
    return flat[..., : SPAN // 2, :], flat[..., SPAN // 2 :, :]


def leave_windows(halves, even):
    shape = (REACH, WL, WH, halves[0].shape[-1])
    window = jnp.concatenate([item.reshape(shape) for item in halves]).transpose(1, 2, 0, 3)
    own = pick(even, window[0], window[1])
    got = swap_levels(pick(even, window[1], window[0]))
    return jnp.concatenate([pick(even, own, got), pick(even, got, own)], axis=1)


def wrap_left(halves):
    return (halves[1], to_window(halves[0], -1))


def wrap_right(halves):
    return (to_window(halves[1], 1), halves[0])


def by_half(values):
    return jnp.broadcast_to(values.T[:, None], (WW, WL, WH)).reshape(1, SPAN)


ROW_GROUPS = WL * WH
LINES = (2 * WL - 1) * (2 * WH - 1)
STEPS = 2 * WW - 1


CORNERS = [p * WH * WW + q * WW + r for p in (0, WL - 1) for q in (0, WH - 1) for r in (0, WW - 1)]


LANES = 32
WIDE = 256
REVERSED = LINES * LANES


def offset_places():
    table = np.zeros((len(CORNERS) * SPAN, REVERSED), np.float32)
    for a in range(1 - WL, WL):
        for b in range(1 - WH, WH):
            for c in range(1 - WW, WW):
                p = [(size - 1) * (step > 0) for size, step in ((WL, a), (WH, b), (WW, c))]
                k = [at - step for at, step in zip(p, (a, b, c))]
                row = CORNERS.index((p[0] * WH + p[1]) * WW + p[2])
                offset = ((WL - 1 - a) * (2 * WH - 1) + WH - 1 - b) * LANES + c + WW - 1
                table[row * SPAN + (k[0] * WH + k[1]) * WW + k[2], offset] = 1
    return table


def line_lanes(line):
    level, row = line // WH, line % WH
    for other in range(WL):
        yield other, ((WL - 1 - level + other) * (2 * WH - 1) + WH - 1 - row) * LANES


def column_table():
    table = np.zeros((ROW_GROUPS, LANES, WW, WIDE), np.float32)
    for line in range(ROW_GROUPS):
        for p in range(WW):
            for k in range(WW):
                table[line, p - k + WW - 1, p, k * ROW_GROUPS + line] = 1
    return table.reshape(ROW_GROUPS * LANES, WW * WIDE).astype(BF16)


def slot_table(rel_index, slots):
    rows = jnp.concatenate([rel_index[at : at + 1] for at in CORNERS], axis=1)
    digits = jnp.concatenate([rows // 32, rows % 32]).astype(BF16)
    places = dot(digits, offset_places().astype(BF16))
    named = np.arange(REVERSED) % LANES < STEPS
    names = jnp.where(named, places[0] * 32 + places[1], -1).astype(jnp.int32)
    return (names[:, None] == jnp.arange(slots)[None, :]).astype(BF16)


TILE = 128
BIAS_LANES = 2 * WIDE
SLOT_LANES = 4 * WIDE


def bias_kernel(steps, columns, out, rows, spread):
    count = steps.shape[0] // 3
    side = WH * LANES

    @pl.when(pl.program_id(0) == 0)
    def _():
        for line in range(ROW_GROUPS):
            for other, lane in line_lanes(line):
                value = steps[:, lane : lane + side]
                for part in range(3):
                    start = (part * ROW_GROUPS + line) * count
                    rows[start : start + count, other * side : (other + 1) * side] = value[
                        part * count : (part + 1) * count
                    ]

    values = dot(rows[...], columns[...])
    size = ROW_GROUPS * count
    values = values[:size] + values[size : 2 * size] + values[2 * size :]
    for tile in range(BIAS_LANES // TILE):
        lanes = slice(tile * TILE, (tile + 1) * TILE)
        for line in range(ROW_GROUPS):
            spread[tile, pl.ds(line, count, ROW_GROUPS), :] = values[
                line * count : (line + 1) * count, lanes
            ]
        out[:, lanes] = spread[tile]


def expand_bias(tables, by_slot):
    count = tables.shape[1]
    steps = dot_nt(tables.reshape(3 * count, -1), by_slot).astype(BF16)
    return pl.pallas_call(
        bias_kernel,
        grid=(WW * WIDE // BIAS_LANES,),
        in_specs=[
            pl.BlockSpec(steps.shape, lambda c: (0, 0)),
            pl.BlockSpec((ROW_GROUPS * LANES, BIAS_LANES), lambda c: (0, c)),
        ],
        out_specs=pl.BlockSpec((count * ROW_GROUPS, BIAS_LANES), lambda c: (0, c)),
        out_shape=jax.ShapeDtypeStruct((count * ROW_GROUPS, WW * WIDE), F32),
        scratch_shapes=[
            pltpu.VMEM((3 * ROW_GROUPS * count, ROW_GROUPS * LANES), BF16),
            pltpu.VMEM((BIAS_LANES // TILE, ROW_GROUPS * count, TILE), F32),
        ],
        compiler_params=pltpu.CompilerParams(vmem_limit_bytes=VMEM),
    )(steps, column_table())


def slots_kernel(*refs):
    scores, columns, out, lines = refs[:BLOCKS], refs[BLOCKS], refs[BLOCKS + 1], refs[BLOCKS + 2]
    size = scores[0].shape[0]
    count = BLOCKS * size // ROW_GROUPS
    side = WH * LANES

    @pl.when(pl.program_id(0) == 0)
    def _():
        lines[...] = jnp.zeros_like(lines)

    for block in range(BLOCKS):
        part = dot_nt(scores[block][...].astype(BF16), columns[...])
        for tile in range(lines.shape[0]):
            lines[tile, pl.ds(block * size, size), :] += part[:, tile * TILE : (tile + 1) * TILE]

    @pl.when(pl.program_id(0) == WW * WIDE // SLOT_LANES - 1)
    def _():
        out[...] = jnp.zeros_like(out)
        for line in range(ROW_GROUPS):
            values = jnp.concatenate(
                [lines[tile, pl.ds(line, count, ROW_GROUPS), :] for tile in range(lines.shape[0])],
                axis=1,
            )
            for other, lane in line_lanes(line):
                out[:, lane : lane + side] += values[:, other * side : (other + 1) * side]


def slot_sums(scores, by_slot):
    size = scores[0].shape[0]
    count = BLOCKS * size // ROW_GROUPS
    wide = ROW_GROUPS * LANES
    steps = pl.pallas_call(
        slots_kernel,
        grid=(WW * WIDE // SLOT_LANES,),
        in_specs=[pl.BlockSpec((size, SLOT_LANES), lambda c: (0, c))] * BLOCKS
        + [pl.BlockSpec((wide, SLOT_LANES), lambda c: (0, c))],
        out_specs=pl.BlockSpec((count, REVERSED), lambda c: (0, 0)),
        out_shape=jax.ShapeDtypeStruct((count, REVERSED), F32),
        scratch_shapes=[pltpu.VMEM((wide // TILE, BLOCKS * size, TILE), F32)],
        compiler_params=pltpu.CompilerParams(vmem_limit_bytes=VMEM),
    )(*scores, column_table())
    return dot(steps.astype(BF16), by_slot)


def dot(a, b):
    return jnp.dot(a, b, preferred_element_type=F32)


def dot_nt(a, b):
    return lax.dot_general(a, b, (((1,), (1,)), ((), ())), preferred_element_type=F32)


def dot_tn(a, b):
    return lax.dot_general(a, b, (((0,), (0,)), ((), ())), preferred_element_type=F32)


def standardise(field):
    values = field.astype(F32)
    centre = jnp.mean(values, axis=-1, keepdims=True)
    spread = jnp.mean((values - centre) ** 2, axis=-1, keepdims=True)
    inv_spread = lax.rsqrt(spread + EPSILON)
    return (values - centre) * inv_spread, inv_spread


def norm_adjoint(cotan, field, gain):
    normed, inv_spread = standardise(field)
    scaled = cotan.astype(F32) * gain
    first = jnp.mean(scaled, axis=-1, keepdims=True)
    second = jnp.mean(scaled * normed, axis=-1, keepdims=True)
    return inv_spread * (scaled - first - normed * second)


def piece_slots():
    for index in range(PIECES):
        side, place = index // (RING * RING), index % (RING * RING)
        yield index, side, place


def collect_rows(order, pieces, weights, sub):
    rows, local = pieces[0].shape[2], pieces[0].shape[3] // 4
    into, last = 3 * local, STEP * 3 * local
    for index in range(SHARES):
        side, place = index // RING, index % RING
        for half in range(2):
            if place < RING - 1:
                values = pieces[5 * side + place][half, sub]
            else:
                values = pieces[5 * side + RING - 1 + half][sub]
            start = pl.multiple_of((2 * order[index] + half) * rows, rows)
            weights[pl.ds(start, rows), sub * into : (sub + 1) * into] = values[:, :into]
            weights[pl.ds(start, rows), last + sub * local : last + (sub + 1) * local] = values[
                :, into:
            ]


def join(halves):
    return jnp.concatenate([item[...].astype(F32) for item in halves], axis=0)


def split(values, halves):
    halves[0][...] = values[: SPAN // 2].astype(BF16)
    halves[1][...] = values[SPAN // 2 :].astype(BF16)


def head_masks(width):
    lane = lax.broadcasted_iota(jnp.int32, (1, width), 1)
    return [(lane // (width // 2) == head).astype(F32).astype(BF16) for head in range(2)]


def forward_kernel(order, *refs):
    halves, (gain, marks, bias), pieces = refs[:2], refs[2:5], refs[5:15]
    after, (packed_out, mixed_out, probs_out) = refs[15:17], refs[17:20]
    weights, normed, total, allowed, added = refs[20:]
    group = pl.program_id(0)
    local = mixed_out.shape[-1]

    @pl.when(group == 0)
    def _():
        values, _ = standardise(join(halves))
        normed[...] = (values * gain[...]).astype(BF16)
        total[...] = jnp.zeros_like(total)
        here = lax.broadcasted_iota(jnp.int32, (SPAN, SPAN), 0)
        there = lax.broadcasted_iota(jnp.int32, (SPAN, SPAN), 1)
        labels = jnp.broadcast_to(marks[0:1].astype(F32), (SPAN, SPAN))
        living = jnp.broadcast_to(marks[1:2], (SPAN, SPAN))
        seen = (labels == labels.T) & ((living > 0) | (here == there))
        allowed[...] = jnp.where(seen, 1.0, 0.0)

    scale = (local // 2) ** (-0.5)
    for sub in range(STEP):
        collect_rows(order, pieces, weights, sub)
        for head in range(2):
            for column in range(WW):
                rows = pl.ds((2 * sub + head) * ROW_GROUPS, ROW_GROUPS)
                lanes = pl.ds(column * WIDE, SPAN)
                place = pl.ds(column * ROW_GROUPS, ROW_GROUPS)
                added[2 * sub + head, place, :] = bias[rows, lanes]
    masks = head_masks(local)
    heads = [(sub, head) for sub in range(STEP) for head in range(2)]
    queries, keys, values = [], [], []
    last = STEP * 3 * local
    side_by_side = dot(normed[...], weights[:, :last]).astype(BF16)
    for sub in range(STEP):
        packed = side_by_side[:, sub * 3 * local : (sub + 1) * 3 * local]
        packed_out[sub] = packed
        queries.append(packed[:, :local])
        keys.append(packed[:, local : 2 * local])
        values.append(packed[:, 2 * local :])
    seen = allowed[...] > 0
    scores = [dot_nt(queries[sub], keys[sub] * masks[head]) for sub, head in heads]
    scores = [
        jnp.where(seen, item * scale + added[index], MASKED) for index, item in enumerate(scores)
    ]
    tops = [jnp.max(item, axis=-1, keepdims=True) for item in scores]
    grown = [jnp.exp(item - top) for item, top in zip(scores, tops)]
    sums = [jnp.sum(item, axis=-1, keepdims=True) for item in grown]
    probs = [item / total_weight for item, total_weight in zip(grown, sums)]
    for index, item in enumerate(probs):
        probs_out[index] = item
    parts = [
        dot(item.astype(BF16), values[sub] * masks[head])
        for item, (sub, head) in zip(probs, heads)
    ]
    mixed = [(parts[2 * sub] + parts[2 * sub + 1]).astype(BF16) for sub in range(STEP)]
    for sub in range(STEP):
        mixed_out[sub] = mixed[sub]
    branch = dot_nt(jnp.concatenate(mixed, axis=1), weights[:, last:])
    total[...] += branch.astype(BF16).astype(F32)

    @pl.when(group == LEV // STEP - 1)
    def _():
        split(join(halves) + total[...].astype(BF16).astype(F32), after)


def backward_kernel(last, order, *refs):
    refs = list(refs)

    def take(count):
        taken, refs[:] = refs[:count], refs[count:]
        return taken

    grad_out = take(2)
    later_grad, later_field = (take(2), take(2)) if last else (None, None)
    later_gain = take(1)[0] if last else None
    field, (gain, packed_in, mixed_in, probs_in), pieces = take(2), take(4), take(10)
    outs, (scores_out, operands) = take(2), take(2)
    weights, normed, up, total = take(4)
    carried = take(1)[0] if last else None
    step = pl.program_id(0)
    local = mixed_in.shape[-1]

    @pl.when(step == 0)
    def _():
        values, _ = standardise(join(field))
        normed[...] = (values * gain[...]).astype(BF16)
        upstream = join(grad_out)
        if last:
            upstream = upstream + norm_adjoint(join(later_grad), join(later_field), later_gain[...])
            carried[...] = upstream
        up[...] = upstream.astype(BF16)
        total[...] = jnp.zeros_like(total)

    scores_out[...] = jnp.zeros_like(scores_out)
    scale = (local // 2) ** (-0.5)
    for sub in range(STEP):
        collect_rows(order, pieces, weights, sub)
    masks = head_masks(local)
    heads = [(sub, head) for sub in range(STEP) for head in range(2)]
    packed = [packed_in[sub] for sub in range(STEP)]
    queries, keys, values = (
        [item[:, part * local : (part + 1) * local] for item in packed] for part in range(3)
    )
    last_column = STEP * 3 * local
    cotan = dot(up[...], weights[:, last_column:]).astype(BF16)
    cotans = [cotan[:, sub * local : (sub + 1) * local] for sub in range(STEP)]
    grad_probs = [dot_nt(cotans[sub], values[sub] * masks[head]) for sub, head in heads]
    probs = [probs_in[index] for index in range(2 * STEP)]
    grad_value = [
        dot_tn(item.astype(BF16), cotans[sub] * masks[head])
        for item, (sub, head) in zip(probs, heads)
    ]
    inner = [
        jnp.sum(grad * item, axis=-1, keepdims=True) for grad, item in zip(grad_probs, probs)
    ]
    grad_scores = [
        item * (grad - dotted) for item, grad, dotted in zip(probs, grad_probs, inner)
    ]
    for index, item in enumerate(grad_scores):
        for column in range(WW):
            rows = pl.ds(index * ROW_GROUPS, ROW_GROUPS)
            lanes = pl.ds(column * WIDE, SPAN)
            scores_out[rows, lanes] = item[column * ROW_GROUPS : (column + 1) * ROW_GROUPS]
    low = [item.astype(BF16) for item in grad_scores]
    grad_query = [dot(item, keys[sub] * masks[head]) for item, (sub, head) in zip(low, heads)]
    grad_keys = [dot_tn(item, queries[sub] * masks[head]) for item, (sub, head) in zip(low, heads)]
    packed_parts = []
    for sub in range(STEP):
        first, second = 2 * sub, 2 * sub + 1
        grad_packed = jnp.concatenate(
            [
                ((grad_query[first] + grad_query[second]) * scale).astype(BF16),
                ((grad_keys[first] + grad_keys[second]) * scale).astype(BF16),
                (grad_value[first] + grad_value[second]).astype(BF16),
            ],
            axis=1,
        )
        packed_parts.append(grad_packed)
        here = pl.ds(pl.multiple_of((STEP * step + sub) * local, local), local)
        operands[sub, :, : 3 * local] = grad_packed
        operands[sub, :, 3 * local : 4 * local] = mixed_in[sub]
        operands[sub, :, 4 * local : 5 * local] = normed[:, here]
        operands[sub, :, 5 * local :] = up[:, here]
    part = dot_nt(jnp.concatenate(packed_parts, axis=1), weights[:, :last_column])
    total[...] += part.astype(BF16).astype(F32)

    @pl.when(step == LEV // STEP - 1)
    def _():
        if last:
            grad_normed = total[...].astype(BF16)
            split(carried[...] + norm_adjoint(grad_normed, join(field), gain[...]), outs)
        else:
            split(total[...], outs)


def weights_kernel(order, mine, other, *refs):
    outs, (turned, normed, up) = refs[:8], refs[8:]
    step = pl.program_id(0)
    local = mine.shape[-1] // 6
    rows = normed.shape[0] // RING
    core = order[0] // RING

    @pl.when(step == 0)
    def _():
        for side, source in enumerate((mine, other)):
            for target, column in ((normed, 4 * local), (up, 5 * local)):
                for level in range(LEV // 2):
                    part = source[core * (LEV // 2) + level, :, column : column + local]
                    turned[level * local : (level + 1) * local] = part.T
                for place in range(RING):
                    start = pl.multiple_of((order[place] - core * RING) * rows, rows)
                    target[place * rows : (place + 1) * rows, side * SPAN : (side + 1) * SPAN] = (
                        turned[pl.ds(start, rows), :]
                    )

    def side_by_side(first, last):
        return jnp.concatenate(
            [
                jnp.concatenate([item[STEP * step + sub, :, first:last] for sub in range(STEP)], axis=1)
                for item in (mine, other)
            ]
        )

    into = dot(normed[...], side_by_side(0, 3 * local)).astype(BF16)
    outof = dot(up[...], side_by_side(3 * local, 4 * local)).astype(BF16)
    half = rows // 2
    for index, out in enumerate(outs):
        place = slice(index * half, (index + 1) * half)
        for sub in range(STEP):
            out[sub, :, : 3 * local] = into[place, sub * 3 * local : (sub + 1) * 3 * local]
            out[sub, :, 3 * local :] = outof[place, sub * local : (sub + 1) * local]


def finish_kernel(order, *refs):
    inputs, (into, outof, bias, turned) = refs[:SHARES], refs[SHARES:]
    rows = into.shape[2] // SHARES
    local = outof.shape[1]
    bias_total = jnp.zeros(bias.shape, F32)
    for source in inputs:
        bias_total += source[BLOCKS * rows :, :].astype(F32)
    bias[...] = bias_total
    for block in range(BLOCKS):
        for index, source in enumerate(inputs):
            start = pl.multiple_of(order[index] * rows, rows)
            values = source[block * rows : (block + 1) * rows, :].astype(F32)
            for part in range(3):
                into[block, part, pl.ds(start, rows), :] = values[:, part * local : (part + 1) * local]
            turned[pl.ds(start, rows), :] = values[:, 3 * local :]
        outof[block] = turned[...].T


def whole(*shape):
    return pl.BlockSpec(shape, lambda g, order: (0,) * len(shape))


def by_group(*shape):
    return pl.BlockSpec((STEP,) + shape, lambda g, order: (g,) + (0,) * len(shape))


def by_head():
    return pl.BlockSpec((2 * STEP, SPAN, SPAN), lambda g, order: (g, 0, 0))


def by_rows(base):
    start = base // STEP
    return pl.BlockSpec((2 * STEP * ROW_GROUPS, WW * WIDE), lambda g, order: (g + start, 0))


def piece_specs(rows, columns):
    pair = pl.BlockSpec((2, STEP, rows, columns), lambda g, order: (0, g, 0, 0))
    return ([pair] * (RING - 1) + [by_group(rows, columns)] * 2) * 2


def cost(flops, bytes_accessed):
    return pl.CostEstimate(flops=flops, bytes_accessed=bytes_accessed, transcendentals=0)


def run_forward(order, halves, gain, marks, bias, block, pieces):
    width = halves[0].shape[1]
    rows, columns = pieces[0].shape[2:]
    local = columns // 4
    shape = jax.ShapeDtypeStruct
    first, second, *saved = pl.pallas_call(
        forward_kernel,
        grid_spec=pltpu.PrefetchScalarGridSpec(
            num_scalar_prefetch=1,
            grid=(LEV // STEP,),
            in_specs=[
                whole(SPAN // 2, width),
                whole(SPAN // 2, width),
                whole(1, width),
                whole(2, SPAN),
                by_rows(block * LEV),
                *piece_specs(rows, columns),
            ],
            out_specs=[
                whole(SPAN // 2, width),
                whole(SPAN // 2, width),
                by_group(SPAN, 3 * local),
                by_group(SPAN, local),
                by_head(),
            ],
            scratch_shapes=[
                pltpu.VMEM((width, STEP * columns), BF16),
                pltpu.VMEM((SPAN, width), BF16),
                pltpu.VMEM((SPAN, width), F32),
                pltpu.VMEM((SPAN, SPAN), F32),
                pltpu.VMEM((2 * STEP, SPAN, SPAN), F32),
            ],
        ),
        out_shape=[
            shape((SPAN // 2, width), BF16),
            shape((SPAN // 2, width), BF16),
            shape((LEV, SPAN, 3 * local), BF16),
            shape((LEV, SPAN, local), BF16),
            shape((2 * LEV, SPAN, SPAN), F32),
        ],
        compiler_params=pltpu.CompilerParams(vmem_limit_bytes=VMEM),
        cost_estimate=cost(14 * 10**9, 2 * 10**7),
    )(order, *halves, gain, marks, bias, *pieces)
    return (first, second), saved


def run_backward(order, last, upstream, halves, gain, saved, pieces):
    width = halves[0].shape[1]
    rows, columns = pieces[0].shape[2:]
    local = columns // 4
    shape = jax.ShapeDtypeStruct
    half = whole(SPAN // 2, width)
    above = [half] * 2
    scratch = [
        pltpu.VMEM((width, STEP * columns), BF16),
        pltpu.VMEM((SPAN, width), BF16),
        pltpu.VMEM((SPAN, width), BF16),
        pltpu.VMEM((SPAN, width), F32),
    ]
    if last:
        above += [half] * 4 + [whole(1, width)]
        scratch.append(pltpu.VMEM((SPAN, width), F32))
    first, second, scores, operands = pl.pallas_call(
        functools.partial(backward_kernel, last),
        grid_spec=pltpu.PrefetchScalarGridSpec(
            num_scalar_prefetch=1,
            grid=(LEV // STEP,),
            in_specs=[
                *above,
                half,
                half,
                whole(1, width),
                by_group(SPAN, 3 * local),
                by_group(SPAN, local),
                by_head(),
                *piece_specs(rows, columns),
            ],
            out_specs=[half, half, by_rows(0), by_group(SPAN, 6 * local)],
            scratch_shapes=scratch,
        ),
        out_shape=[
            shape((SPAN // 2, width), BF16),
            shape((SPAN // 2, width), BF16),
            shape((2 * LEV * ROW_GROUPS, WW * WIDE), F32),
            shape((LEV, SPAN, 6 * local), BF16),
        ],
        compiler_params=pltpu.CompilerParams(vmem_limit_bytes=VMEM),
        cost_estimate=cost(14 * 10**9, 2 * 10**7),
    )(order, *upstream, *halves, gain, *saved, *pieces)
    return (first, second), scores, operands


def run_weights(order, mine, other, rows):
    local = mine.shape[-1] // 6
    width, columns = LEV * local, 4 * local
    return pl.pallas_call(
        weights_kernel,
        grid_spec=pltpu.PrefetchScalarGridSpec(
            num_scalar_prefetch=1,
            grid=(LEV // STEP,),
            in_specs=[whole(*mine.shape), whole(*other.shape)],
            out_specs=[by_group(rows, columns)] * 8,
            scratch_shapes=[
                pltpu.VMEM((width // 2, SPAN), BF16),
                pltpu.VMEM((width // 2, 2 * SPAN), BF16),
                pltpu.VMEM((width // 2, 2 * SPAN), BF16),
            ],
        ),
        out_shape=[jax.ShapeDtypeStruct((LEV, rows, columns), BF16)] * 8,
        compiler_params=pltpu.CompilerParams(vmem_limit_bytes=VMEM),
        cost_estimate=cost(5 * 10**9, 10**7),
    )(order, mine, other)


def run_finish(order, parts, width, local):
    shape = jax.ShapeDtypeStruct

    shapes = [
        (BLOCKS, 3, width, local),
        (BLOCKS, local, width),
        (BIAS_ROWS, 4 * local),
    ]
    return pl.pallas_call(
        finish_kernel,
        grid_spec=pltpu.PrefetchScalarGridSpec(
            num_scalar_prefetch=1,
            grid=(),
            in_specs=[whole_of(*item.shape) for item in parts],
            out_specs=[whole_of(*extent) for extent in shapes],
            scratch_shapes=[pltpu.VMEM((width, local), F32)],
        ),
        out_shape=[shape(extent, F32) for extent in shapes],
        compiler_params=pltpu.CompilerParams(vmem_limit_bytes=VMEM),
    )(order, *parts)


def bias_message(scores, by_slot, columns):
    sums = slot_sums(scores, by_slot)
    slots = sums.shape[-1]
    flat = sums.reshape(BLOCKS, LEV, 2 * slots).transpose(1, 0, 2).reshape(LEV, -1)
    flat = jnp.pad(flat, ((0, 0), (0, BIAS_ROWS * columns - flat.shape[1])))
    return flat.reshape(LEV, BIAS_ROWS, columns).astype(BF16)


def on_device(
    tokens,
    norm_gain,
    qkv_weight,
    out_weight,
    bias_table,
    rel_index,
    region_ids,
    row_valid,
    grad_out,
):
    width = tokens.shape[-1]
    local = qkv_weight.shape[-1]
    slots = bias_table.shape[-1]
    columns = 4 * local
    rows = width // SHARES
    even = lax.axis_index("lev") % 2 == 0
    order = share_order()
    gains = [norm_gain[block : block + 1] for block in range(BLOCKS)]

    own = [own_rows(qkv_weight, out_weight, b, order[0]) for b in range(BLOCKS)]
    own[0] = jnp.concatenate([own[0], table_rows(bias_table, columns)])
    part, tables = pack_levels(gather_levels(own[0]), rows)
    pieces_0 = second_ring(part)
    own[1], tokens, grad_out = after((own[1], tokens, grad_out), part)
    (part,) = pack_levels(gather_levels(own[1]), rows)
    pieces_1 = second_ring(after(part, *pieces_0[3:]))

    both = enter_windows(jnp.concatenate([tokens, grad_out]), even)
    start = tuple(item[0] for item in both)
    grad_start = tuple(item[1] for item in both)
    grad_shifted = wrap_left(grad_start)

    following = from_next_lon(region_ids[:, :REACH])
    shifted = jnp.concatenate([region_ids[:, REACH:], following], axis=1)
    living = by_half(jnp.broadcast_to(row_valid[:, None], (WH, WW)))
    marks = [
        jnp.concatenate([by_half(pick(even, item[:, :WW], item[:, WW:])), living])
        for item in (region_ids, shifted)
    ]

    by_slot = slot_table(rel_index, slots)
    parts = tables.reshape(LEV, -1)[:, : 3 * bias_table.size]
    parts = parts.reshape(LEV, 3, BLOCKS, 2, slots).transpose(1, 2, 0, 3, 4)
    bias = expand_bias(parts.reshape(3, BLOCKS * 2 * LEV, slots), by_slot)
    pieces_0 = pieces_0[:1] + tuple(after(pieces_0[1:], bias))
    pieces_0 = pieces_0 + tuple(swap_cores(item) for item in pieces_0)

    middle, saved_0 = run_forward(order, start, gains[0], marks[0], bias, 0, pieces_0)
    second = wrap_left(middle)
    pieces_1 = pieces_1[:1] + tuple(after(pieces_1[1:], middle[0]))
    pieces_1 = pieces_1 + tuple(swap_cores(item) for item in pieces_1)
    ended, saved_1 = run_forward(order, second, gains[1], marks[1], bias, 1, pieces_1)

    grad_normed, scores_1, operands_1 = run_backward(
        order, False, grad_shifted, second, gains[1], saved_1, pieces_1
    )
    later_grad = wrap_right(grad_normed)
    swapped_1 = swap_cores(operands_1)
    upstream = [*grad_start, *later_grad, *middle, gains[1]]
    grad_first, scores_0, operands_0 = run_backward(
        order, True, upstream, start, gains[0], saved_0, pieces_0
    )
    swapped_0 = swap_cores(operands_0)
    operands_1, swapped_1 = after((operands_1, swapped_1), operands_0)
    grads_1 = run_weights(order, operands_1, swapped_1, rows // 2)
    begun = scatter_start(grads_1)
    operands_0, swapped_0 = after((operands_0, swapped_0), *grads_1)
    grads_0 = run_weights(order, operands_0, swapped_0, rows // 2)
    far_a, far_b, ahead_b, behind_a = after(begun, *grads_0)
    ahead_a, behind_b = scatter_middle(grads_1, far_a, far_b)
    parts_1 = (grads_1[0], ahead_a, behind_a, grads_1[1], ahead_b, behind_b)
    far_a, far_b, ahead_b, behind_a = scatter_start(grads_0)
    ahead_a, behind_b = scatter_middle(grads_0, far_a, far_b)
    parts_0 = (grads_0[0], ahead_a, behind_a, grads_0[1], ahead_b, behind_b)

    scores = after((scores_0, scores_1), *grads_0)
    message = bias_message(scores, by_slot, columns)
    finished = finish_sums(parts_0 + parts_1, message)
    grad_tokens = leave_windows(grad_first, even)
    ended = after(ended, grad_first)
    output = leave_windows(wrap_right(ended), even)

    grad_qkv, grad_out_weight, bias_rows = run_finish(order, finished, width, local)
    grad_qkv = grad_qkv.transpose(0, 2, 1, 3)
    grad_bias = bias_rows.reshape(-1)[: BLOCKS * 2 * slots].reshape(BLOCKS, 2, slots)
    return (output[None], grad_tokens[None], grad_qkv, grad_out_weight, grad_bias)


def solution(mesh):
    placed = (
        P("lev", "lat", "lon", None),
        P(),
        P(None, None, None, "lev"),
        P(None, "lev", None),
        P(None, "lev", None),
        P(),
        P("lat", "lon"),
        P("lat"),
        P("lev", "lat", "lon", None),
    )
    return jax.shard_map(
        on_device,
        mesh=mesh,
        in_specs=placed,
        out_specs=(
            P("lev", "lat", "lon", None),
            P("lev", "lat", "lon", None),
            P(None, None, None, "lev"),
            P(None, "lev", None),
            P(None, "lev", None),
        ),
        check_vma=False,
    )
```

```python
import functools

import jax
import jax.numpy as jnp
import numpy as np
from jax import lax
from jax.experimental import pallas as pl
from jax.experimental.pallas import tpu as pltpu
from jax.sharding import PartitionSpec as P

WL = 2
WH = 6
WW = 12
SPAN = WL * WH * WW
REACH = WW // 2
BLOCKS = 2
EPSILON = 1e-05
MASKED = -1e30
F32 = jnp.float32
BF16 = jnp.bfloat16

AXES = ("lon", "lev", "lat")
LEV = 8
RING = 4
OFFSETS = (0, 1, -1, 2)
SHARES = 2 * RING
STEP = 2
BIAS_ROWS = 16
VMEM = 56 * 1024 * 1024


def decode(device):
    lat, lev, lon = device % 2, device // 2 % LEV, device // (2 * LEV)
    return (2 * lat + lon // 8, lon // 2 % 4, lon % 2, lev)


def encode(x, y, core, lev):
    x, y, lev = x % RING, y % RING, lev % LEV
    return (((x % 2) * 8 + y * 2 + core) * LEV + lev) * 2 + x // 2


def send(value, target):
    pairs = [(i, encode(*target(*decode(i)))) for i in range(2 * RING * RING * LEV)]
    return lax.ppermute(value, AXES, pairs)


def along(value, ring, step):
    def target(x, y, core, lev):
        if (core == 0) == (ring == 1):
            return (x + step, y, core, lev)
        return (x, y + step, core, lev)

    return send(value, target)


def along_levels(value, step):
    return send(value, lambda x, y, core, lev: (x, y, core, lev + step))


def swap_cores(value):
    return send(value, lambda x, y, core, lev: (x, y, 1 - core, lev))


def swap_levels(value):
    return send(value, lambda x, y, core, lev: (x, y, core, lev ^ 1))


def to_window(value, step):
    def target(x, y, core, lev):
        lon = (x % 2) * 8 + y * 2 + core
        index = (2 * lon + lev % 2 + step) % 32
        lon, side = index // 2, index % 2
        return (2 * (x // 2) + lon // 8, lon // 2 % 4, lon % 2, lev - lev % 2 + side)

    return send(value, target)


def from_next_lon(value):
    def target(x, y, core, lev):
        lon = ((x % 2) * 8 + y * 2 + core - 1) % 16
        return (2 * (x // 2) + lon // 8, lon // 2 % 4, lon % 2, lev)

    return send(value, target)


def after(values, *others):
    tied = lax.optimization_barrier((values, others))
    return tied[0]


def share_order():
    lon, lat = lax.axis_index("lon"), lax.axis_index("lat")
    x, y, core = 2 * lat + lon // 8, lon // 2 % 4, lon % 2
    which = (core + jnp.arange(2, dtype=jnp.int32)[:, None]) % 2
    place = jnp.where(which == 0, y, x) + jnp.array(OFFSETS, jnp.int32)[None]
    return (which * RING + place % RING).reshape(-1).astype(jnp.int32)


def own_rows(qkv_weight, out_weight, block, share):
    width, parts, local = qkv_weight.shape[1:]
    rows = width // SHARES
    start = share * rows
    zero = jnp.zeros_like(start)
    into = lax.dynamic_slice(
        qkv_weight, (zero + block, start, zero, zero), (1, rows, parts, local)
    )[0]
    outof = lax.dynamic_slice(out_weight, (zero + block, zero, start), (1, local, rows))[0].T
    return jnp.concatenate([into[:, part] for part in range(parts)] + [outof], axis=1)


def table_rows(bias_table, columns):
    high = lax.reduce_precision(bias_table, 8, 7)
    middle = lax.reduce_precision(bias_table - high, 8, 7)
    low = bias_table - high - middle
    flat = jnp.stack([high, middle, low]).reshape(-1)
    rows = -(-flat.shape[0] // columns // BIAS_ROWS) * BIAS_ROWS
    return jnp.pad(flat, (0, rows * columns - flat.shape[0])).reshape(rows, columns).astype(BF16)


def gather_levels(own):
    up, down = [own], [own]
    for _ in range(3):
        up.append(along_levels(up[-1], -1))
        down.append(along_levels(down[-1], 1))
    up.append(along_levels(up[-1], -1))
    return up + down[:0:-1]


def scatter_levels(messages):
    up, down = messages[LEV // 2], messages[LEV // 2 + 1]
    for step in range(LEV // 2 - 1, 0, -1):
        up = add_low(messages[step], along_levels(up, 1))
        if step > 1:
            down = add_low(messages[LEV + 1 - step], along_levels(down, -1))
    return add_low(messages[0], along_levels(up, 1), along_levels(down, -1))


def pack_kernel(*refs):
    parts, weights, tables = refs[:LEV], refs[LEV : LEV + BLOCKS], refs[LEV + BLOCKS]
    rows = weights[0].shape[2]
    for index, part in enumerate(parts):
        for block in range(BLOCKS):
            for half in range(2):
                start = (2 * block + half) * rows
                weights[block][half, index] = part[start : start + rows]
        tables[index] = part[2 * BLOCKS * rows :]


def pack_levels(parts, rows):
    height, columns = parts[0].shape
    out_shape = [jax.ShapeDtypeStruct((2, LEV, rows // 2, columns), BF16)] * BLOCKS
    out_shape.append(jax.ShapeDtypeStruct((LEV, height - BLOCKS * rows, columns), BF16))
    return pl.pallas_call(
        pack_kernel,
        out_shape=out_shape,
        compiler_params=pltpu.CompilerParams(vmem_limit_bytes=VMEM),
    )(*parts)


def second_ring(own, *others):
    ahead, behind, swapped = along(own, 2, -1), along(own, 2, 1), swap_cores(own)
    ahead, behind = after((ahead, behind), swapped, *others)
    far_a, far_b = along(ahead[0], 2, -1), along(behind[1], 2, 1)
    rest = (ahead, behind, far_a, far_b)
    return (own, *rest, swapped, *[swap_cores(item) for item in rest])


def add_low(*terms):
    return functools.reduce(jnp.add, [term.astype(F32) for term in terms]).astype(BF16)


def scatter_start(grads):
    return (
        along(grads[6], 2, 1),
        along(grads[7], 2, -1),
        along(grads[3], 2, 1),
        along(grads[4], 2, -1),
    )


def scatter_middle(grads, far_a, far_b):
    return (
        along(add_low(grads[2], far_a), 2, 1),
        along(add_low(grads[5], far_b), 2, -1),
    )


def levels_kernel(*refs):
    parts, bias, outs = refs[: 6 * BLOCKS], refs[6 * BLOCKS], refs[6 * BLOCKS + 1 :]
    rows = parts[0].shape[1]
    for level, out in enumerate(outs):
        for place in range(2 * BLOCKS):
            own, ahead, behind = parts[3 * place : 3 * place + 3]
            out[pl.ds(place * rows, rows), :] = own[level] + (ahead[level] + behind[level])
        out[pl.ds(2 * BLOCKS * rows, BIAS_ROWS), :] = bias[level]


def whole_of(*extent):
    return pl.BlockSpec(extent, lambda order: (0,) * len(extent))


def sum_levels(parts, bias_rows):
    rows, columns = parts[0].shape[1:]
    height = 2 * BLOCKS * rows + BIAS_ROWS
    messages = pl.pallas_call(
        levels_kernel,
        out_shape=[jax.ShapeDtypeStruct((height, columns), BF16)] * LEV,
        compiler_params=pltpu.CompilerParams(vmem_limit_bytes=VMEM),
    )(*parts, bias_rows)
    return scatter_levels(messages)


def spread_sums(total):
    total = add_low(total, along(total, 1, 1), along(total, 1, -1), along(total, 1, 2))
    mine = [total, along(total, 2, -1), along(total, 2, 1), along(total, 2, -2)]
    return mine + [swap_cores(item) for item in mine]


def pick(first, own, other):
    return jnp.where(first, own, other)


def enter_windows(field, even):
    left, right = field[..., :WW, :], field[..., WW:, :]
    keep = pick(even, left, right)
    got = swap_levels(pick(even, right, left))
    window = jnp.stack([pick(even, keep, got), pick(even, got, keep)], axis=-4)
    window = jnp.moveaxis(window, -2, -4)
    flat = window.reshape(window.shape[:-4] + (SPAN, window.shape[-1]))
    return flat[..., : SPAN // 2, :], flat[..., SPAN // 2 :, :]


def leave_windows(halves, even):
    shape = (REACH, WL, WH, halves[0].shape[-1])
    window = jnp.concatenate([item.reshape(shape) for item in halves]).transpose(1, 2, 0, 3)
    own = pick(even, window[0], window[1])
    got = swap_levels(pick(even, window[1], window[0]))
    return jnp.concatenate([pick(even, own, got), pick(even, got, own)], axis=1)


def wrap_left(halves):
    return (halves[1], to_window(halves[0], -1))


def wrap_right(halves):
    return (to_window(halves[1], 1), halves[0])


def by_half(values):
    return jnp.broadcast_to(values.T[:, None], (WW, WL, WH)).reshape(1, SPAN)


ROW_GROUPS = WL * WH
LINES = (2 * WL - 1) * (2 * WH - 1)
STEPS = 2 * WW - 1


CORNERS = [p * WH * WW + q * WW + r for p in (0, WL - 1) for q in (0, WH - 1) for r in (0, WW - 1)]


LANES = 32
WIDE = 256
REVERSED = LINES * LANES


def offset_places():
    table = np.zeros((len(CORNERS) * SPAN, REVERSED), np.float32)
    for a in range(1 - WL, WL):
        for b in range(1 - WH, WH):
            for c in range(1 - WW, WW):
                p = [(size - 1) * (step > 0) for size, step in ((WL, a), (WH, b), (WW, c))]
                k = [at - step for at, step in zip(p, (a, b, c))]
                row = CORNERS.index((p[0] * WH + p[1]) * WW + p[2])
                offset = ((WL - 1 - a) * (2 * WH - 1) + WH - 1 - b) * LANES + c + WW - 1
                table[row * SPAN + (k[0] * WH + k[1]) * WW + k[2], offset] = 1
    return table


def line_lanes(line):
    level, row = line // WH, line % WH
    for other in range(WL):
        yield other, ((WL - 1 - level + other) * (2 * WH - 1) + WH - 1 - row) * LANES


def column_table():
    table = np.zeros((ROW_GROUPS, LANES, WW, WIDE), np.float32)
    for line in range(ROW_GROUPS):
        for p in range(WW):
            for k in range(WW):
                table[line, p - k + WW - 1, p, k * ROW_GROUPS + line] = 1
    return table.reshape(ROW_GROUPS * LANES, WW * WIDE).astype(BF16)


def slot_table(rel_index, slots):
    rows = jnp.concatenate([rel_index[at : at + 1] for at in CORNERS], axis=1)
    digits = jnp.concatenate([rows // 32, rows % 32]).astype(BF16)
    places = dot(digits, offset_places().astype(BF16))
    named = np.arange(REVERSED) % LANES < STEPS
    names = jnp.where(named, places[0] * 32 + places[1], -1).astype(jnp.int32)
    return (names[:, None] == jnp.arange(slots)[None, :]).astype(BF16)


TILE = 128
BIAS_LANES = 2 * WIDE
SLOT_LANES = 4 * WIDE


def bias_kernel(steps, columns, out, rows, spread):
    count = steps.shape[0] // 3
    side = WH * LANES

    @pl.when(pl.program_id(0) == 0)
    def _():
        for line in range(ROW_GROUPS):
            for other, lane in line_lanes(line):
                value = steps[:, lane : lane + side]
                for part in range(3):
                    start = (part * ROW_GROUPS + line) * count
                    rows[start : start + count, other * side : (other + 1) * side] = value[
                        part * count : (part + 1) * count
                    ]

    values = dot(rows[...], columns[...])
    size = ROW_GROUPS * count
    values = values[:size] + values[size : 2 * size] + values[2 * size :]
    for tile in range(BIAS_LANES // TILE):
        lanes = slice(tile * TILE, (tile + 1) * TILE)
        for line in range(ROW_GROUPS):
            spread[tile, pl.ds(line, count, ROW_GROUPS), :] = values[
                line * count : (line + 1) * count, lanes
            ]
        out[:, lanes] = spread[tile]


def expand_bias(tables, by_slot):
    count = tables.shape[1]
    steps = dot_nt(tables.reshape(3 * count, -1), by_slot).astype(BF16)
    return pl.pallas_call(
        bias_kernel,
        grid=(WW * WIDE // BIAS_LANES,),
        in_specs=[
            pl.BlockSpec(steps.shape, lambda c: (0, 0)),
            pl.BlockSpec((ROW_GROUPS * LANES, BIAS_LANES), lambda c: (0, c)),
        ],
        out_specs=pl.BlockSpec((count * ROW_GROUPS, BIAS_LANES), lambda c: (0, c)),
        out_shape=jax.ShapeDtypeStruct((count * ROW_GROUPS, WW * WIDE), F32),
        scratch_shapes=[
            pltpu.VMEM((3 * ROW_GROUPS * count, ROW_GROUPS * LANES), BF16),
            pltpu.VMEM((BIAS_LANES // TILE, ROW_GROUPS * count, TILE), F32),
        ],
        compiler_params=pltpu.CompilerParams(vmem_limit_bytes=VMEM),
        cost_estimate=cost(9 * 10**9, 10**7),
    )(steps, column_table())


def slots_kernel(*refs):
    scores, columns, out, lines = refs[:BLOCKS], refs[BLOCKS], refs[BLOCKS + 1], refs[BLOCKS + 2]
    size = scores[0].shape[0]
    count = BLOCKS * size // ROW_GROUPS
    side = WH * LANES

    @pl.when(pl.program_id(0) == 0)
    def _():
        lines[...] = jnp.zeros_like(lines)

    for block in range(BLOCKS):
        part = dot_nt(scores[block][...].astype(BF16), columns[...])
        for tile in range(lines.shape[0]):
            lines[tile, pl.ds(block * size, size), :] += part[:, tile * TILE : (tile + 1) * TILE]

    @pl.when(pl.program_id(0) == WW * WIDE // SLOT_LANES - 1)
    def _():
        out[...] = jnp.zeros_like(out)
        for line in range(ROW_GROUPS):
            values = jnp.concatenate(
                [lines[tile, pl.ds(line, count, ROW_GROUPS), :] for tile in range(lines.shape[0])],
                axis=1,
            )
            for other, lane in line_lanes(line):
                out[:, lane : lane + side] += values[:, other * side : (other + 1) * side]


def slot_sums(scores, by_slot):
    size = scores[0].shape[0]
    count = BLOCKS * size // ROW_GROUPS
    wide = ROW_GROUPS * LANES
    steps = pl.pallas_call(
        slots_kernel,
        grid=(WW * WIDE // SLOT_LANES,),
        in_specs=[pl.BlockSpec((size, SLOT_LANES), lambda c: (0, c))] * BLOCKS
        + [pl.BlockSpec((wide, SLOT_LANES), lambda c: (0, c))],
        out_specs=pl.BlockSpec((count, REVERSED), lambda c: (0, 0)),
        out_shape=jax.ShapeDtypeStruct((count, REVERSED), F32),
        scratch_shapes=[pltpu.VMEM((wide // TILE, BLOCKS * size, TILE), F32)],
        compiler_params=pltpu.CompilerParams(vmem_limit_bytes=VMEM),
        cost_estimate=cost(6 * 10**9, 10**7),
    )(*scores, column_table())
    return dot(steps.astype(BF16), by_slot)


def dot(a, b):
    return jnp.dot(a, b, preferred_element_type=F32)


def dot_nt(a, b):
    return lax.dot_general(a, b, (((1,), (1,)), ((), ())), preferred_element_type=F32)


def dot_tn(a, b):
    return lax.dot_general(a, b, (((0,), (0,)), ((), ())), preferred_element_type=F32)


def standardise(field):
    values = field.astype(F32)
    centre = jnp.mean(values, axis=-1, keepdims=True)
    spread = jnp.mean((values - centre) ** 2, axis=-1, keepdims=True)
    inv_spread = lax.rsqrt(spread + EPSILON)
    return (values - centre) * inv_spread, inv_spread


def norm_adjoint(cotan, field, gain):
    normed, inv_spread = standardise(field)
    scaled = cotan.astype(F32) * gain
    first = jnp.mean(scaled, axis=-1, keepdims=True)
    second = jnp.mean(scaled * normed, axis=-1, keepdims=True)
    return inv_spread * (scaled - first - normed * second)


def piece_slots():
    for index in range(PIECES):
        side, place = index // (RING * RING), index % (RING * RING)
        yield index, side, place


def collect_rows(order, pieces, weights, sub):
    rows, local = pieces[0].shape[2], pieces[0].shape[3] // 4
    into, last = 3 * local, STEP * 3 * local
    for index in range(SHARES):
        side, place = index // RING, index % RING
        for half in range(2):
            if place < RING - 1:
                values = pieces[5 * side + place][half, sub]
            else:
                values = pieces[5 * side + RING - 1 + half][sub]
            start = pl.multiple_of((2 * order[index] + half) * rows, rows)
            weights[pl.ds(start, rows), sub * into : (sub + 1) * into] = values[:, :into]
            weights[pl.ds(start, rows), last + sub * local : last + (sub + 1) * local] = values[
                :, into:
            ]


def join(halves):
    return jnp.concatenate([item[...].astype(F32) for item in halves], axis=0)


def split(values, halves):
    halves[0][...] = values[: SPAN // 2].astype(BF16)
    halves[1][...] = values[SPAN // 2 :].astype(BF16)


def head_masks(width):
    lane = lax.broadcasted_iota(jnp.int32, (1, width), 1)
    return [(lane // (width // 2) == head).astype(F32).astype(BF16) for head in range(2)]


def forward_kernel(order, *refs):
    halves, (gain, marks, bias), pieces = refs[:2], refs[2:5], refs[5:15]
    after, (packed_out, mixed_out, probs_out) = refs[15:17], refs[17:20]
    weights, normed, total, allowed, added = refs[20:]
    group = pl.program_id(0)
    local = mixed_out.shape[-1]

    @pl.when(group == 0)
    def _():
        values, _ = standardise(join(halves))
        normed[...] = (values * gain[...]).astype(BF16)
        total[...] = jnp.zeros_like(total)
        here = lax.broadcasted_iota(jnp.int32, (SPAN, SPAN), 0)
        there = lax.broadcasted_iota(jnp.int32, (SPAN, SPAN), 1)
        labels = jnp.broadcast_to(marks[0:1].astype(F32), (SPAN, SPAN))
        living = jnp.broadcast_to(marks[1:2], (SPAN, SPAN))
        seen = (labels == labels.T) & ((living > 0) | (here == there))
        allowed[...] = jnp.where(seen, 1.0, 0.0)

    scale = (local // 2) ** (-0.5)
    for sub in range(STEP):
        collect_rows(order, pieces, weights, sub)
        for head in range(2):
            for column in range(WW):
                rows = pl.ds((2 * sub + head) * ROW_GROUPS, ROW_GROUPS)
                lanes = pl.ds(column * WIDE, SPAN)
                place = pl.ds(column * ROW_GROUPS, ROW_GROUPS)
                added[2 * sub + head, place, :] = bias[rows, lanes]
    masks = head_masks(local)
    heads = [(sub, head) for sub in range(STEP) for head in range(2)]
    queries, keys, values = [], [], []
    last = STEP * 3 * local
    side_by_side = dot(normed[...], weights[:, :last]).astype(BF16)
    for sub in range(STEP):
        packed = side_by_side[:, sub * 3 * local : (sub + 1) * 3 * local]
        packed_out[sub] = packed
        queries.append(packed[:, :local])
        keys.append(packed[:, local : 2 * local])
        values.append(packed[:, 2 * local :])
    seen = allowed[...] > 0
    scores = [dot_nt(queries[sub], keys[sub] * masks[head]) for sub, head in heads]
    scores = [
        jnp.where(seen, item * scale + added[index], MASKED) for index, item in enumerate(scores)
    ]
    tops = [jnp.max(item, axis=-1, keepdims=True) for item in scores]
    grown = [jnp.exp(item - top) for item, top in zip(scores, tops)]
    sums = [jnp.sum(item, axis=-1, keepdims=True) for item in grown]
    probs = [item / total_weight for item, total_weight in zip(grown, sums)]
    for index, item in enumerate(probs):
        probs_out[index] = item
    parts = [
        dot(item.astype(BF16), values[sub] * masks[head])
        for item, (sub, head) in zip(probs, heads)
    ]
    mixed = [(parts[2 * sub] + parts[2 * sub + 1]).astype(BF16) for sub in range(STEP)]
    for sub in range(STEP):
        mixed_out[sub] = mixed[sub]
    branch = dot_nt(jnp.concatenate(mixed, axis=1), weights[:, last:])
    total[...] += branch.astype(BF16).astype(F32)

    @pl.when(group == LEV // STEP - 1)
    def _():
        split(join(halves) + total[...].astype(BF16).astype(F32), after)


def backward_kernel(last, order, *refs):
    refs = list(refs)

    def take(count):
        taken, refs[:] = refs[:count], refs[count:]
        return taken

    grad_out = take(2)
    later_grad, later_field = (take(2), take(2)) if last else (None, None)
    later_gain = take(1)[0] if last else None
    field, (gain, packed_in, mixed_in, probs_in), pieces = take(2), take(4), take(10)
    outs, (scores_out, operands) = take(2), take(2)
    weights, normed, up, total = take(4)
    carried = take(1)[0] if last else None
    step = pl.program_id(0)
    local = mixed_in.shape[-1]

    @pl.when(step == 0)
    def _():
        values, _ = standardise(join(field))
        normed[...] = (values * gain[...]).astype(BF16)
        upstream = join(grad_out)
        if last:
            upstream = upstream + norm_adjoint(join(later_grad), join(later_field), later_gain[...])
            carried[...] = upstream
        up[...] = upstream.astype(BF16)
        total[...] = jnp.zeros_like(total)

    scores_out[...] = jnp.zeros_like(scores_out)
    scale = (local // 2) ** (-0.5)
    for sub in range(STEP):
        collect_rows(order, pieces, weights, sub)
    masks = head_masks(local)
    heads = [(sub, head) for sub in range(STEP) for head in range(2)]
    packed = [packed_in[sub] for sub in range(STEP)]
    queries, keys, values = (
        [item[:, part * local : (part + 1) * local] for item in packed] for part in range(3)
    )
    last_column = STEP * 3 * local
    cotan = dot(up[...], weights[:, last_column:]).astype(BF16)
    cotans = [cotan[:, sub * local : (sub + 1) * local] for sub in range(STEP)]
    grad_probs = [dot_nt(cotans[sub], values[sub] * masks[head]) for sub, head in heads]
    probs = [probs_in[index] for index in range(2 * STEP)]
    grad_value = [
        dot_tn(item.astype(BF16), cotans[sub] * masks[head])
        for item, (sub, head) in zip(probs, heads)
    ]
    inner = [
        jnp.sum(grad * item, axis=-1, keepdims=True) for grad, item in zip(grad_probs, probs)
    ]
    grad_scores = [
        item * (grad - dotted) for item, grad, dotted in zip(probs, grad_probs, inner)
    ]
    for index, item in enumerate(grad_scores):
        for column in range(WW):
            rows = pl.ds(index * ROW_GROUPS, ROW_GROUPS)
            lanes = pl.ds(column * WIDE, SPAN)
            scores_out[rows, lanes] = item[column * ROW_GROUPS : (column + 1) * ROW_GROUPS]
    low = [item.astype(BF16) for item in grad_scores]
    grad_query = [dot(item, keys[sub] * masks[head]) for item, (sub, head) in zip(low, heads)]
    grad_keys = [dot_tn(item, queries[sub] * masks[head]) for item, (sub, head) in zip(low, heads)]
    packed_parts = []
    for sub in range(STEP):
        first, second = 2 * sub, 2 * sub + 1
        grad_packed = jnp.concatenate(
            [
                ((grad_query[first] + grad_query[second]) * scale).astype(BF16),
                ((grad_keys[first] + grad_keys[second]) * scale).astype(BF16),
                (grad_value[first] + grad_value[second]).astype(BF16),
            ],
            axis=1,
        )
        packed_parts.append(grad_packed)
        here = pl.ds(pl.multiple_of((STEP * step + sub) * local, local), local)
        operands[sub, :, : 3 * local] = grad_packed
        operands[sub, :, 3 * local : 4 * local] = mixed_in[sub]
        operands[sub, :, 4 * local : 5 * local] = normed[:, here]
        operands[sub, :, 5 * local :] = up[:, here]
    part = dot_nt(jnp.concatenate(packed_parts, axis=1), weights[:, :last_column])
    total[...] += part.astype(BF16).astype(F32)

    @pl.when(step == LEV // STEP - 1)
    def _():
        if last:
            grad_normed = total[...].astype(BF16)
            split(carried[...] + norm_adjoint(grad_normed, join(field), gain[...]), outs)
        else:
            split(total[...], outs)


def weights_kernel(order, mine, other, *refs):
    outs, (turned, normed, up) = refs[:8], refs[8:]
    step = pl.program_id(0)
    local = mine.shape[-1] // 6
    rows = normed.shape[0] // RING
    core = order[0] // RING

    @pl.when(step == 0)
    def _():
        for side, source in enumerate((mine, other)):
            for target, column in ((normed, 4 * local), (up, 5 * local)):
                for level in range(LEV // 2):
                    part = source[core * (LEV // 2) + level, :, column : column + local]
                    turned[level * local : (level + 1) * local] = part.T
                for place in range(RING):
                    start = pl.multiple_of((order[place] - core * RING) * rows, rows)
                    target[place * rows : (place + 1) * rows, side * SPAN : (side + 1) * SPAN] = (
                        turned[pl.ds(start, rows), :]
                    )

    def side_by_side(first, last):
        return jnp.concatenate(
            [
                jnp.concatenate([item[STEP * step + sub, :, first:last] for sub in range(STEP)], axis=1)
                for item in (mine, other)
            ]
        )

    into = dot(normed[...], side_by_side(0, 3 * local)).astype(BF16)
    outof = dot(up[...], side_by_side(3 * local, 4 * local)).astype(BF16)
    half = rows // 2
    for index, out in enumerate(outs):
        place = slice(index * half, (index + 1) * half)
        for sub in range(STEP):
            out[sub, :, : 3 * local] = into[place, sub * 3 * local : (sub + 1) * 3 * local]
            out[sub, :, 3 * local :] = outof[place, sub * local : (sub + 1) * local]


def finish_kernel(order, *refs):
    inputs, (into, outof, bias, turned) = refs[:SHARES], refs[SHARES:]
    rows = into.shape[2] // SHARES
    local = outof.shape[1]
    bias_total = jnp.zeros(bias.shape, F32)
    for source in inputs:
        bias_total += source[BLOCKS * rows :, :].astype(F32)
    bias[...] = bias_total
    for block in range(BLOCKS):
        for index, source in enumerate(inputs):
            start = pl.multiple_of(order[index] * rows, rows)
            values = source[block * rows : (block + 1) * rows, :].astype(F32)
            for part in range(3):
                into[block, part, pl.ds(start, rows), :] = values[:, part * local : (part + 1) * local]
            turned[pl.ds(start, rows), :] = values[:, 3 * local :]
        outof[block] = turned[...].T


def whole(*shape):
    return pl.BlockSpec(shape, lambda g, order: (0,) * len(shape))


def by_group(*shape):
    return pl.BlockSpec((STEP,) + shape, lambda g, order: (g,) + (0,) * len(shape))


def by_head():
    return pl.BlockSpec((2 * STEP, SPAN, SPAN), lambda g, order: (g, 0, 0))


def by_rows(base):
    start = base // STEP
    return pl.BlockSpec((2 * STEP * ROW_GROUPS, WW * WIDE), lambda g, order: (g + start, 0))


def piece_specs(rows, columns):
    pair = pl.BlockSpec((2, STEP, rows, columns), lambda g, order: (0, g, 0, 0))
    return ([pair] * (RING - 1) + [by_group(rows, columns)] * 2) * 2


def cost(flops, bytes_accessed):
    return pl.CostEstimate(flops=flops, bytes_accessed=bytes_accessed, transcendentals=0)


def run_forward(order, halves, gain, marks, bias, block, pieces):
    width = halves[0].shape[1]
    rows, columns = pieces[0].shape[2:]
    local = columns // 4
    shape = jax.ShapeDtypeStruct
    first, second, *saved = pl.pallas_call(
        forward_kernel,
        grid_spec=pltpu.PrefetchScalarGridSpec(
            num_scalar_prefetch=1,
            grid=(LEV // STEP,),
            in_specs=[
                whole(SPAN // 2, width),
                whole(SPAN // 2, width),
                whole(1, width),
                whole(2, SPAN),
                by_rows(block * LEV),
                *piece_specs(rows, columns),
            ],
            out_specs=[
                whole(SPAN // 2, width),
                whole(SPAN // 2, width),
                by_group(SPAN, 3 * local),
                by_group(SPAN, local),
                by_head(),
            ],
            scratch_shapes=[
                pltpu.VMEM((width, STEP * columns), BF16),
                pltpu.VMEM((SPAN, width), BF16),
                pltpu.VMEM((SPAN, width), F32),
                pltpu.VMEM((SPAN, SPAN), F32),
                pltpu.VMEM((2 * STEP, SPAN, SPAN), F32),
            ],
        ),
        out_shape=[
            shape((SPAN // 2, width), BF16),
            shape((SPAN // 2, width), BF16),
            shape((LEV, SPAN, 3 * local), BF16),
            shape((LEV, SPAN, local), BF16),
            shape((2 * LEV, SPAN, SPAN), F32),
        ],
        compiler_params=pltpu.CompilerParams(vmem_limit_bytes=VMEM),
        cost_estimate=cost(14 * 10**9, 2 * 10**7),
    )(order, *halves, gain, marks, bias, *pieces)
    return (first, second), saved


def run_backward(order, last, upstream, halves, gain, saved, pieces):
    width = halves[0].shape[1]
    rows, columns = pieces[0].shape[2:]
    local = columns // 4
    shape = jax.ShapeDtypeStruct
    half = whole(SPAN // 2, width)
    above = [half] * 2
    scratch = [
        pltpu.VMEM((width, STEP * columns), BF16),
        pltpu.VMEM((SPAN, width), BF16),
        pltpu.VMEM((SPAN, width), BF16),
        pltpu.VMEM((SPAN, width), F32),
    ]
    if last:
        above += [half] * 4 + [whole(1, width)]
        scratch.append(pltpu.VMEM((SPAN, width), F32))
    first, second, scores, operands = pl.pallas_call(
        functools.partial(backward_kernel, last),
        grid_spec=pltpu.PrefetchScalarGridSpec(
            num_scalar_prefetch=1,
            grid=(LEV // STEP,),
            in_specs=[
                *above,
                half,
                half,
                whole(1, width),
                by_group(SPAN, 3 * local),
                by_group(SPAN, local),
                by_head(),
                *piece_specs(rows, columns),
            ],
            out_specs=[half, half, by_rows(0), by_group(SPAN, 6 * local)],
            scratch_shapes=scratch,
        ),
        out_shape=[
            shape((SPAN // 2, width), BF16),
            shape((SPAN // 2, width), BF16),
            shape((2 * LEV * ROW_GROUPS, WW * WIDE), F32),
            shape((LEV, SPAN, 6 * local), BF16),
        ],
        compiler_params=pltpu.CompilerParams(vmem_limit_bytes=VMEM),
        cost_estimate=cost(14 * 10**9, 2 * 10**7),
    )(order, *upstream, *halves, gain, *saved, *pieces)
    return (first, second), scores, operands


def run_weights(order, mine, other, rows):
    local = mine.shape[-1] // 6
    width, columns = LEV * local, 4 * local
    return pl.pallas_call(
        weights_kernel,
        grid_spec=pltpu.PrefetchScalarGridSpec(
            num_scalar_prefetch=1,
            grid=(LEV // STEP,),
            in_specs=[whole(*mine.shape), whole(*other.shape)],
            out_specs=[by_group(rows, columns)] * 8,
            scratch_shapes=[
                pltpu.VMEM((width // 2, SPAN), BF16),
                pltpu.VMEM((width // 2, 2 * SPAN), BF16),
                pltpu.VMEM((width // 2, 2 * SPAN), BF16),
            ],
        ),
        out_shape=[jax.ShapeDtypeStruct((LEV, rows, columns), BF16)] * 8,
        compiler_params=pltpu.CompilerParams(vmem_limit_bytes=VMEM),
        cost_estimate=cost(5 * 10**9, 10**7),
    )(order, mine, other)


def run_finish(order, parts, width, local):
    shape = jax.ShapeDtypeStruct

    shapes = [
        (BLOCKS, 3, width, local),
        (BLOCKS, local, width),
        (BIAS_ROWS, 4 * local),
    ]
    return pl.pallas_call(
        finish_kernel,
        grid_spec=pltpu.PrefetchScalarGridSpec(
            num_scalar_prefetch=1,
            grid=(),
            in_specs=[whole_of(*item.shape) for item in parts],
            out_specs=[whole_of(*extent) for extent in shapes],
            scratch_shapes=[pltpu.VMEM((width, local), F32)],
        ),
        out_shape=[shape(extent, F32) for extent in shapes],
        compiler_params=pltpu.CompilerParams(vmem_limit_bytes=VMEM),
    )(order, *parts)


def bias_message(scores, by_slot, columns):
    sums = slot_sums(scores, by_slot)
    slots = sums.shape[-1]
    flat = sums.reshape(BLOCKS, LEV, 2 * slots).transpose(1, 0, 2).reshape(LEV, -1)
    flat = jnp.pad(flat, ((0, 0), (0, BIAS_ROWS * columns - flat.shape[1])))
    return flat.reshape(LEV, BIAS_ROWS, columns).astype(BF16)


def on_device(
    tokens,
    norm_gain,
    qkv_weight,
    out_weight,
    bias_table,
    rel_index,
    region_ids,
    row_valid,
    grad_out,
):
    width = tokens.shape[-1]
    local = qkv_weight.shape[-1]
    slots = bias_table.shape[-1]
    columns = 4 * local
    rows = width // SHARES
    even = lax.axis_index("lev") % 2 == 0
    order = share_order()
    gains = [norm_gain[block : block + 1] for block in range(BLOCKS)]

    own = [own_rows(qkv_weight, out_weight, b, order[0]) for b in range(BLOCKS)]
    own.append(table_rows(bias_table, columns))
    *part, tables = pack_levels(gather_levels(jnp.concatenate(own)), rows)
    tokens, grad_out = after((tokens, grad_out), tables)

    both = enter_windows(jnp.concatenate([tokens, grad_out]), even)
    start = tuple(item[0] for item in both)
    grad_start = tuple(item[1] for item in both)
    grad_shifted = wrap_left(grad_start)

    following = from_next_lon(region_ids[:, :REACH])
    shifted = jnp.concatenate([region_ids[:, REACH:], following], axis=1)
    living = by_half(jnp.broadcast_to(row_valid[:, None], (WH, WW)))
    marks = [
        jnp.concatenate([by_half(pick(even, item[:, :WW], item[:, WW:])), living])
        for item in (region_ids, shifted)
    ]

    by_slot = slot_table(rel_index, slots)
    parts = tables.reshape(LEV, -1)[:, : 3 * bias_table.size]
    parts = parts.reshape(LEV, 3, BLOCKS, 2, slots).transpose(1, 2, 0, 3, 4)
    bias = expand_bias(parts.reshape(3, BLOCKS * 2 * LEV, slots), by_slot)
    pieces_0 = second_ring(part[0], bias)

    middle, saved_0 = run_forward(order, start, gains[0], marks[0], bias, 0, pieces_0)
    second = wrap_left(middle)
    pieces_1 = second_ring(after(part[1], *pieces_0[3:5], *pieces_0[6:8]), middle[0])
    ended, saved_1 = run_forward(order, second, gains[1], marks[1], bias, 1, pieces_1)

    grad_normed, scores_1, operands_1 = run_backward(
        order, False, grad_shifted, second, gains[1], saved_1, pieces_1
    )
    later_grad = wrap_right(grad_normed)
    swapped_1 = swap_cores(operands_1)
    ended = wrap_right(ended)
    upstream = after([*grad_start, *later_grad, *middle, gains[1]], *ended)
    grad_first, scores_0, operands_0 = run_backward(
        order, True, upstream, start, gains[0], saved_0, pieces_0
    )
    swapped_0 = swap_cores(operands_0)
    operands_1, swapped_1 = after((operands_1, swapped_1), operands_0)
    grads_1 = run_weights(order, operands_1, swapped_1, rows // 2)
    begun = scatter_start(grads_1)
    operands_0, swapped_0 = after((operands_0, swapped_0), *grads_1)
    grads_0 = run_weights(order, operands_0, swapped_0, rows // 2)
    far_a, far_b, ahead_b, behind_a = after(begun, *grads_0)
    ahead_a, behind_b = scatter_middle(grads_1, far_a, far_b)
    parts_1 = (grads_1[0], ahead_a, behind_a, grads_1[1], ahead_b, behind_b)
    far_a, far_b, ahead_b, behind_a = scatter_start(grads_0)
    ahead_a, behind_b = scatter_middle(grads_0, far_a, far_b)
    parts_0 = (grads_0[0], ahead_a, behind_a, grads_0[1], ahead_b, behind_b)

    scores = after((scores_0, scores_1), *grads_0)
    message = bias_message(scores, by_slot, columns)
    total = sum_levels(parts_0 + parts_1, message)
    finished = spread_sums(total)
    grad_first, ended = after((grad_first, ended), total)
    grad_tokens = leave_windows(grad_first, even)
    output = leave_windows(ended, even)

    grad_qkv, grad_out_weight, bias_rows = run_finish(order, finished, width, local)
    grad_qkv = grad_qkv.transpose(0, 2, 1, 3)
    grad_bias = bias_rows.reshape(-1)[: BLOCKS * 2 * slots].reshape(BLOCKS, 2, slots)
    return (output[None], grad_tokens[None], grad_qkv, grad_out_weight, grad_bias)


def solution(mesh):
    placed = (
        P("lev", "lat", "lon", None),
        P(),
        P(None, None, None, "lev"),
        P(None, "lev", None),
        P(None, "lev", None),
        P(),
        P("lat", "lon"),
        P("lat"),
        P("lev", "lat", "lon", None),
    )
    return jax.shard_map(
        on_device,
        mesh=mesh,
        in_specs=placed,
        out_specs=(
            P("lev", "lat", "lon", None),
            P("lev", "lat", "lon", None),
            P(None, None, None, "lev"),
            P(None, "lev", None),
            P(None, "lev", None),
        ),
        check_vma=False,
    )
```

```python
import functools

import jax
import jax.numpy as jnp
import numpy as np
from jax import lax
from jax.experimental import pallas as pl
from jax.experimental.pallas import tpu as pltpu
from jax.sharding import PartitionSpec as P

WL = 2
WH = 6
WW = 12
SPAN = WL * WH * WW
REACH = WW // 2
BLOCKS = 2
EPSILON = 1e-05
MASKED = -1e30
F32 = jnp.float32
BF16 = jnp.bfloat16

AXES = ("lon", "lev", "lat")
LEV = 8
RING = 4
OFFSETS = (0, 1, -1, 2)
SHARES = 2 * RING
STEP = 2
BIAS_ROWS = 16
VMEM = 56 * 1024 * 1024


def decode(device):
    lat, lev, lon = device % 2, device // 2 % LEV, device // (2 * LEV)
    return (2 * lat + lon // 8, lon // 2 % 4, lon % 2, lev)


def encode(x, y, core, lev):
    x, y, lev = x % RING, y % RING, lev % LEV
    return (((x % 2) * 8 + y * 2 + core) * LEV + lev) * 2 + x // 2


def send(value, target):
    pairs = [(i, encode(*target(*decode(i)))) for i in range(2 * RING * RING * LEV)]
    return lax.ppermute(value, AXES, pairs)


def along(value, ring, step):
    def target(x, y, core, lev):
        if (core == 0) == (ring == 1):
            return (x + step, y, core, lev)
        return (x, y + step, core, lev)

    return send(value, target)


def along_levels(value, step):
    return send(value, lambda x, y, core, lev: (x, y, core, lev + step))


def swap_cores(value):
    return send(value, lambda x, y, core, lev: (x, y, 1 - core, lev))


def swap_levels(value):
    return send(value, lambda x, y, core, lev: (x, y, core, lev ^ 1))


def to_window(value, step):
    def target(x, y, core, lev):
        lon = (x % 2) * 8 + y * 2 + core
        index = (2 * lon + lev % 2 + step) % 32
        lon, side = index // 2, index % 2
        return (2 * (x // 2) + lon // 8, lon // 2 % 4, lon % 2, lev - lev % 2 + side)

    return send(value, target)


def from_next_lon(value):
    def target(x, y, core, lev):
        lon = ((x % 2) * 8 + y * 2 + core - 1) % 16
        return (2 * (x // 2) + lon // 8, lon // 2 % 4, lon % 2, lev)

    return send(value, target)


def after(values, *others):
    tied = lax.optimization_barrier((values, others))
    return tied[0]


def share_order():
    lon, lat = lax.axis_index("lon"), lax.axis_index("lat")
    x, y, core = 2 * lat + lon // 8, lon // 2 % 4, lon % 2
    which = (core + jnp.arange(2, dtype=jnp.int32)[:, None]) % 2
    place = jnp.where(which == 0, y, x) + jnp.array(OFFSETS, jnp.int32)[None]
    return (which * RING + place % RING).reshape(-1).astype(jnp.int32)


def own_rows(qkv_weight, out_weight, block, share):
    width, parts, local = qkv_weight.shape[1:]
    rows = width // SHARES
    start = share * rows
    zero = jnp.zeros_like(start)
    into = lax.dynamic_slice(
        qkv_weight, (zero + block, start, zero, zero), (1, rows, parts, local)
    )[0]
    outof = lax.dynamic_slice(out_weight, (zero + block, zero, start), (1, local, rows))[0].T
    return jnp.concatenate([into[:, part] for part in range(parts)] + [outof], axis=1)


def table_rows(bias_table, columns):
    high = lax.reduce_precision(bias_table, 8, 7)
    middle = lax.reduce_precision(bias_table - high, 8, 7)
    low = bias_table - high - middle
    flat = jnp.stack([high, middle, low]).reshape(-1)
    rows = -(-flat.shape[0] // columns // BIAS_ROWS) * BIAS_ROWS
    return jnp.pad(flat, (0, rows * columns - flat.shape[0])).reshape(rows, columns).astype(BF16)


def gather_levels(own):
    up, down = [own], [own]
    for _ in range(3):
        up.append(along_levels(up[-1], -1))
        down.append(along_levels(down[-1], 1))
    up.append(along_levels(up[-1], -1))
    return up + down[:0:-1]


def scatter_levels(messages):
    up, down = messages[LEV // 2], messages[LEV // 2 + 1]
    for step in range(LEV // 2 - 1, 0, -1):
        up = add_low(messages[step], along_levels(up, 1))
        if step > 1:
            down = add_low(messages[LEV + 1 - step], along_levels(down, -1))
    return add_low(messages[0], along_levels(up, 1), along_levels(down, -1))


def pack_kernel(*refs):
    parts, weights, tables = refs[:LEV], refs[LEV : LEV + BLOCKS], refs[LEV + BLOCKS]
    rows = weights[0].shape[2]
    for index, part in enumerate(parts):
        for block in range(BLOCKS):
            for half in range(2):
                start = (2 * block + half) * rows
                weights[block][half, index] = part[start : start + rows]
        tables[index] = part[2 * BLOCKS * rows :]


def pack_levels(parts, rows):
    height, columns = parts[0].shape
    out_shape = [jax.ShapeDtypeStruct((2, LEV, rows // 2, columns), BF16)] * BLOCKS
    out_shape.append(jax.ShapeDtypeStruct((LEV, height - BLOCKS * rows, columns), BF16))
    return pl.pallas_call(
        pack_kernel,
        out_shape=out_shape,
        compiler_params=pltpu.CompilerParams(vmem_limit_bytes=VMEM),
    )(*parts)


def second_ring(own, others=(), following=None):
    ahead, behind, swapped = along(own, 2, -1), along(own, 2, 1), swap_cores(own)
    if others:
        ahead, behind = after((ahead, behind), swapped, *others)
    halves = (ahead[0], behind[1])
    if following is not None:
        halves, following = lax.optimization_barrier((halves, following))
    far_a, far_b = along(halves[0], 2, -1), along(halves[1], 2, 1)
    rest = (ahead, behind, far_a, far_b)
    pieces = (own, *rest, swapped, *[swap_cores(item) for item in rest])
    if following is not None:
        following = after(following, pieces[6])
    return pieces, following


def add_low(*terms):
    return functools.reduce(jnp.add, [term.astype(F32) for term in terms]).astype(BF16)


def scatter_start(grads):
    return (
        along(grads[6], 2, 1),
        along(grads[7], 2, -1),
        along(grads[3], 2, 1),
        along(grads[4], 2, -1),
    )


def scatter_middle(grads, far_a, far_b):
    return (
        along(add_low(grads[2], far_a), 2, 1),
        along(add_low(grads[5], far_b), 2, -1),
    )


def levels_kernel(*refs):
    parts, bias, outs = refs[: 6 * BLOCKS], refs[6 * BLOCKS], refs[6 * BLOCKS + 1 :]
    rows = parts[0].shape[1]
    for level, out in enumerate(outs):
        for place in range(2 * BLOCKS):
            own, ahead, behind = parts[3 * place : 3 * place + 3]
            out[pl.ds(place * rows, rows), :] = own[level] + (ahead[level] + behind[level])
        out[pl.ds(2 * BLOCKS * rows, BIAS_ROWS), :] = bias[level]


def whole_of(*extent):
    return pl.BlockSpec(extent, lambda order: (0,) * len(extent))


def sum_levels(parts, bias_rows):
    rows, columns = parts[0].shape[1:]
    height = 2 * BLOCKS * rows + BIAS_ROWS
    messages = pl.pallas_call(
        levels_kernel,
        out_shape=[jax.ShapeDtypeStruct((height, columns), BF16)] * LEV,
        compiler_params=pltpu.CompilerParams(vmem_limit_bytes=VMEM),
    )(*parts, bias_rows)
    return scatter_levels(messages)


def spread_sums(total):
    total = add_low(total, along(total, 1, 1), along(total, 1, -1), along(total, 1, 2))
    mine = [total, along(total, 2, -1), along(total, 2, 1), along(total, 2, -2)]
    return mine + [swap_cores(item) for item in mine]


def pick(first, own, other):
    return jnp.where(first, own, other)


def enter_windows(field, even):
    left, right = field[..., :WW, :], field[..., WW:, :]
    keep = pick(even, left, right)
    got = swap_levels(pick(even, right, left))
    window = jnp.stack([pick(even, keep, got), pick(even, got, keep)], axis=-4)
    window = jnp.moveaxis(window, -2, -4)
    flat = window.reshape(window.shape[:-4] + (SPAN, window.shape[-1]))
    return flat[..., : SPAN // 2, :], flat[..., SPAN // 2 :, :]


def leave_windows(halves, even):
    shape = (REACH, WL, WH, halves[0].shape[-1])
    window = jnp.concatenate([item.reshape(shape) for item in halves]).transpose(1, 2, 0, 3)
    own = pick(even, window[0], window[1])
    got = swap_levels(pick(even, window[1], window[0]))
    return jnp.concatenate([pick(even, own, got), pick(even, got, own)], axis=1)


def wrap_left(halves):
    return (halves[1], to_window(halves[0], -1))


def wrap_right(halves):
    return (to_window(halves[1], 1), halves[0])


def by_half(values):
    return jnp.broadcast_to(values.T[:, None], (WW, WL, WH)).reshape(1, SPAN)


ROW_GROUPS = WL * WH
LINES = (2 * WL - 1) * (2 * WH - 1)
STEPS = 2 * WW - 1


CORNERS = [p * WH * WW + q * WW + r for p in (0, WL - 1) for q in (0, WH - 1) for r in (0, WW - 1)]


LANES = 32
WIDE = 256
REVERSED = LINES * LANES


def offset_places():
    table = np.zeros((len(CORNERS) * SPAN, REVERSED), np.float32)
    for a in range(1 - WL, WL):
        for b in range(1 - WH, WH):
            for c in range(1 - WW, WW):
                p = [(size - 1) * (step > 0) for size, step in ((WL, a), (WH, b), (WW, c))]
                k = [at - step for at, step in zip(p, (a, b, c))]
                row = CORNERS.index((p[0] * WH + p[1]) * WW + p[2])
                offset = ((WL - 1 - a) * (2 * WH - 1) + WH - 1 - b) * LANES + c + WW - 1
                table[row * SPAN + (k[0] * WH + k[1]) * WW + k[2], offset] = 1
    return table


def line_lanes(line):
    level, row = line // WH, line % WH
    for other in range(WL):
        yield other, ((WL - 1 - level + other) * (2 * WH - 1) + WH - 1 - row) * LANES


def column_table():
    table = np.zeros((ROW_GROUPS, LANES, WW, WIDE), np.float32)
    for line in range(ROW_GROUPS):
        for p in range(WW):
            for k in range(WW):
                table[line, p - k + WW - 1, p, k * ROW_GROUPS + line] = 1
    return table.reshape(ROW_GROUPS * LANES, WW * WIDE).astype(BF16)


def slot_table(rel_index, slots):
    rows = jnp.concatenate([rel_index[at : at + 1] for at in CORNERS], axis=1)
    digits = jnp.concatenate([rows // 32, rows % 32]).astype(BF16)
    places = dot(digits, offset_places().astype(BF16))
    named = np.arange(REVERSED) % LANES < STEPS
    names = jnp.where(named, places[0] * 32 + places[1], -1).astype(jnp.int32)
    return (names[:, None] == jnp.arange(slots)[None, :]).astype(BF16)


TILE = 128
BIAS_LANES = 2 * WIDE
SLOT_LANES = 4 * WIDE


def bias_kernel(steps, columns, out, rows, spread):
    count = steps.shape[0] // 3
    side = WH * LANES

    @pl.when(pl.program_id(0) == 0)
    def _():
        for line in range(ROW_GROUPS):
            for other, lane in line_lanes(line):
                value = steps[:, lane : lane + side]
                for part in range(3):
                    start = (part * ROW_GROUPS + line) * count
                    rows[start : start + count, other * side : (other + 1) * side] = value[
                        part * count : (part + 1) * count
                    ]

    values = dot(rows[...], columns[...])
    size = ROW_GROUPS * count
    values = values[:size] + values[size : 2 * size] + values[2 * size :]
    for tile in range(BIAS_LANES // TILE):
        lanes = slice(tile * TILE, (tile + 1) * TILE)
        for line in range(ROW_GROUPS):
            spread[tile, pl.ds(line, count, ROW_GROUPS), :] = values[
                line * count : (line + 1) * count, lanes
            ]
        out[:, lanes] = spread[tile]


def expand_bias(tables, by_slot):
    count = tables.shape[1]
    steps = dot_nt(tables.reshape(3 * count, -1), by_slot).astype(BF16)
    return pl.pallas_call(
        bias_kernel,
        grid=(WW * WIDE // BIAS_LANES,),
        in_specs=[
            pl.BlockSpec(steps.shape, lambda c: (0, 0)),
            pl.BlockSpec((ROW_GROUPS * LANES, BIAS_LANES), lambda c: (0, c)),
        ],
        out_specs=pl.BlockSpec((count * ROW_GROUPS, BIAS_LANES), lambda c: (0, c)),
        out_shape=jax.ShapeDtypeStruct((count * ROW_GROUPS, WW * WIDE), F32),
        scratch_shapes=[
            pltpu.VMEM((3 * ROW_GROUPS * count, ROW_GROUPS * LANES), BF16),
            pltpu.VMEM((BIAS_LANES // TILE, ROW_GROUPS * count, TILE), F32),
        ],
        compiler_params=pltpu.CompilerParams(vmem_limit_bytes=VMEM),
        cost_estimate=cost(9 * 10**9, 10**7),
    )(steps, column_table())


def slots_kernel(*refs):
    scores, columns, out, lines = refs[:BLOCKS], refs[BLOCKS], refs[BLOCKS + 1], refs[BLOCKS + 2]
    size = scores[0].shape[0]
    count = BLOCKS * size // ROW_GROUPS
    side = WH * LANES

    @pl.when(pl.program_id(0) == 0)
    def _():
        lines[...] = jnp.zeros_like(lines)

    for block in range(BLOCKS):
        part = dot_nt(scores[block][...].astype(BF16), columns[...])
        for tile in range(lines.shape[0]):
            lines[tile, pl.ds(block * size, size), :] += part[:, tile * TILE : (tile + 1) * TILE]

    @pl.when(pl.program_id(0) == WW * WIDE // SLOT_LANES - 1)
    def _():
        out[...] = jnp.zeros_like(out)
        for line in range(ROW_GROUPS):
            values = jnp.concatenate(
                [lines[tile, pl.ds(line, count, ROW_GROUPS), :] for tile in range(lines.shape[0])],
                axis=1,
            )
            for other, lane in line_lanes(line):
                out[:, lane : lane + side] += values[:, other * side : (other + 1) * side]


def slot_sums(scores, by_slot):
    size = scores[0].shape[0]
    count = BLOCKS * size // ROW_GROUPS
    wide = ROW_GROUPS * LANES
    steps = pl.pallas_call(
        slots_kernel,
        grid=(WW * WIDE // SLOT_LANES,),
        in_specs=[pl.BlockSpec((size, SLOT_LANES), lambda c: (0, c))] * BLOCKS
        + [pl.BlockSpec((wide, SLOT_LANES), lambda c: (0, c))],
        out_specs=pl.BlockSpec((count, REVERSED), lambda c: (0, 0)),
        out_shape=jax.ShapeDtypeStruct((count, REVERSED), F32),
        scratch_shapes=[pltpu.VMEM((wide // TILE, BLOCKS * size, TILE), F32)],
        compiler_params=pltpu.CompilerParams(vmem_limit_bytes=VMEM),
        cost_estimate=cost(6 * 10**9, 10**7),
    )(*scores, column_table())
    return dot(steps.astype(BF16), by_slot)


def dot(a, b):
    return jnp.dot(a, b, preferred_element_type=F32)


def dot_nt(a, b):
    return lax.dot_general(a, b, (((1,), (1,)), ((), ())), preferred_element_type=F32)


def dot_tn(a, b):
    return lax.dot_general(a, b, (((0,), (0,)), ((), ())), preferred_element_type=F32)


def standardise(field):
    values = field.astype(F32)
    centre = jnp.mean(values, axis=-1, keepdims=True)
    spread = jnp.mean((values - centre) ** 2, axis=-1, keepdims=True)
    inv_spread = lax.rsqrt(spread + EPSILON)
    return (values - centre) * inv_spread, inv_spread


def norm_adjoint(cotan, field, gain):
    normed, inv_spread = standardise(field)
    scaled = cotan.astype(F32) * gain
    first = jnp.mean(scaled, axis=-1, keepdims=True)
    second = jnp.mean(scaled * normed, axis=-1, keepdims=True)
    return inv_spread * (scaled - first - normed * second)


def piece_slots():
    for index in range(PIECES):
        side, place = index // (RING * RING), index % (RING * RING)
        yield index, side, place


def collect_rows(order, pieces, weights, sub):
    rows, local = pieces[0].shape[2], pieces[0].shape[3] // 4
    into, last = 3 * local, STEP * 3 * local
    for index in range(SHARES):
        side, place = index // RING, index % RING
        for half in range(2):
            if place < RING - 1:
                values = pieces[5 * side + place][half, sub]
            else:
                values = pieces[5 * side + RING - 1 + half][sub]
            start = pl.multiple_of((2 * order[index] + half) * rows, rows)
            weights[pl.ds(start, rows), sub * into : (sub + 1) * into] = values[:, :into]
            weights[pl.ds(start, rows), last + sub * local : last + (sub + 1) * local] = values[
                :, into:
            ]


def join(halves):
    return jnp.concatenate([item[...].astype(F32) for item in halves], axis=0)


def split(values, halves):
    halves[0][...] = values[: SPAN // 2].astype(BF16)
    halves[1][...] = values[SPAN // 2 :].astype(BF16)


def head_masks(width):
    lane = lax.broadcasted_iota(jnp.int32, (1, width), 1)
    return [(lane // (width // 2) == head).astype(F32).astype(BF16) for head in range(2)]


def forward_kernel(order, *refs):
    halves, (gain, marks, bias), pieces = refs[:2], refs[2:5], refs[5:15]
    after, (packed_out, mixed_out, probs_out) = refs[15:17], refs[17:20]
    weights, normed, total, allowed, added = refs[20:]
    group = pl.program_id(0)
    local = mixed_out.shape[-1]

    @pl.when(group == 0)
    def _():
        values, _ = standardise(join(halves))
        normed[...] = (values * gain[...]).astype(BF16)
        total[...] = jnp.zeros_like(total)
        here = lax.broadcasted_iota(jnp.int32, (SPAN, SPAN), 0)
        there = lax.broadcasted_iota(jnp.int32, (SPAN, SPAN), 1)
        labels = jnp.broadcast_to(marks[0:1].astype(F32), (SPAN, SPAN))
        living = jnp.broadcast_to(marks[1:2], (SPAN, SPAN))
        seen = (labels == labels.T) & ((living > 0) | (here == there))
        allowed[...] = jnp.where(seen, 1.0, 0.0)

    scale = (local // 2) ** (-0.5)
    for sub in range(STEP):
        collect_rows(order, pieces, weights, sub)
        for head in range(2):
            for column in range(WW):
                rows = pl.ds((2 * sub + head) * ROW_GROUPS, ROW_GROUPS)
                lanes = pl.ds(column * WIDE, SPAN)
                place = pl.ds(column * ROW_GROUPS, ROW_GROUPS)
                added[2 * sub + head, place, :] = bias[rows, lanes]
    masks = head_masks(local)
    heads = [(sub, head) for sub in range(STEP) for head in range(2)]
    queries, keys, values = [], [], []
    last = STEP * 3 * local
    side_by_side = dot(normed[...], weights[:, :last]).astype(BF16)
    for sub in range(STEP):
        packed = side_by_side[:, sub * 3 * local : (sub + 1) * 3 * local]
        packed_out[sub] = packed
        queries.append(packed[:, :local])
        keys.append(packed[:, local : 2 * local])
        values.append(packed[:, 2 * local :])
    seen = allowed[...] > 0
    scores = [dot_nt(queries[sub], keys[sub] * masks[head]) for sub, head in heads]
    scores = [
        jnp.where(seen, item * scale + added[index], MASKED) for index, item in enumerate(scores)
    ]
    tops = [jnp.max(item, axis=-1, keepdims=True) for item in scores]
    grown = [jnp.exp(item - top) for item, top in zip(scores, tops)]
    sums = [jnp.sum(item, axis=-1, keepdims=True) for item in grown]
    probs = [item / total_weight for item, total_weight in zip(grown, sums)]
    for index, item in enumerate(probs):
        probs_out[index] = item
    parts = [
        dot(item.astype(BF16), values[sub] * masks[head])
        for item, (sub, head) in zip(probs, heads)
    ]
    mixed = [(parts[2 * sub] + parts[2 * sub + 1]).astype(BF16) for sub in range(STEP)]
    for sub in range(STEP):
        mixed_out[sub] = mixed[sub]
    branch = dot_nt(jnp.concatenate(mixed, axis=1), weights[:, last:])
    total[...] += branch.astype(BF16).astype(F32)

    @pl.when(group == LEV // STEP - 1)
    def _():
        split(join(halves) + total[...].astype(BF16).astype(F32), after)


def backward_kernel(last, order, *refs):
    refs = list(refs)

    def take(count):
        taken, refs[:] = refs[:count], refs[count:]
        return taken

    grad_out = take(2)
    later_grad, later_field = (take(2), take(2)) if last else (None, None)
    later_gain = take(1)[0] if last else None
    field, (gain, packed_in, mixed_in, probs_in), pieces = take(2), take(4), take(10)
    outs, (scores_out, operands) = take(2), take(2)
    weights, normed, up, total = take(4)
    carried = take(1)[0] if last else None
    step = pl.program_id(0)
    local = mixed_in.shape[-1]

    @pl.when(step == 0)
    def _():
        values, _ = standardise(join(field))
        normed[...] = (values * gain[...]).astype(BF16)
        upstream = join(grad_out)
        if last:
            upstream = upstream + norm_adjoint(join(later_grad), join(later_field), later_gain[...])
            carried[...] = upstream
        up[...] = upstream.astype(BF16)
        total[...] = jnp.zeros_like(total)

    scores_out[...] = jnp.zeros_like(scores_out)
    scale = (local // 2) ** (-0.5)
    for sub in range(STEP):
        collect_rows(order, pieces, weights, sub)
    masks = head_masks(local)
    heads = [(sub, head) for sub in range(STEP) for head in range(2)]
    packed = [packed_in[sub] for sub in range(STEP)]
    queries, keys, values = (
        [item[:, part * local : (part + 1) * local] for item in packed] for part in range(3)
    )
    last_column = STEP * 3 * local
    cotan = dot(up[...], weights[:, last_column:]).astype(BF16)
    cotans = [cotan[:, sub * local : (sub + 1) * local] for sub in range(STEP)]
    grad_probs = [dot_nt(cotans[sub], values[sub] * masks[head]) for sub, head in heads]
    probs = [probs_in[index] for index in range(2 * STEP)]
    grad_value = [
        dot_tn(item.astype(BF16), cotans[sub] * masks[head])
        for item, (sub, head) in zip(probs, heads)
    ]
    inner = [
        jnp.sum(grad * item, axis=-1, keepdims=True) for grad, item in zip(grad_probs, probs)
    ]
    grad_scores = [
        item * (grad - dotted) for item, grad, dotted in zip(probs, grad_probs, inner)
    ]
    for index, item in enumerate(grad_scores):
        for column in range(WW):
            rows = pl.ds(index * ROW_GROUPS, ROW_GROUPS)
            lanes = pl.ds(column * WIDE, SPAN)
            scores_out[rows, lanes] = item[column * ROW_GROUPS : (column + 1) * ROW_GROUPS]
    low = [item.astype(BF16) for item in grad_scores]
    grad_query = [dot(item, keys[sub] * masks[head]) for item, (sub, head) in zip(low, heads)]
    grad_keys = [dot_tn(item, queries[sub] * masks[head]) for item, (sub, head) in zip(low, heads)]
    packed_parts = []
    for sub in range(STEP):
        first, second = 2 * sub, 2 * sub + 1
        grad_packed = jnp.concatenate(
            [
                ((grad_query[first] + grad_query[second]) * scale).astype(BF16),
                ((grad_keys[first] + grad_keys[second]) * scale).astype(BF16),
                (grad_value[first] + grad_value[second]).astype(BF16),
            ],
            axis=1,
        )
        packed_parts.append(grad_packed)
        here = pl.ds(pl.multiple_of((STEP * step + sub) * local, local), local)
        operands[sub, :, : 3 * local] = grad_packed
        operands[sub, :, 3 * local : 4 * local] = mixed_in[sub]
        operands[sub, :, 4 * local : 5 * local] = normed[:, here]
        operands[sub, :, 5 * local :] = up[:, here]
    part = dot_nt(jnp.concatenate(packed_parts, axis=1), weights[:, :last_column])
    total[...] += part.astype(BF16).astype(F32)

    @pl.when(step == LEV // STEP - 1)
    def _():
        if last:
            grad_normed = total[...].astype(BF16)
            split(carried[...] + norm_adjoint(grad_normed, join(field), gain[...]), outs)
        else:
            split(total[...], outs)


def weights_kernel(order, mine, other, *refs):
    outs, (turned, normed, up) = refs[:8], refs[8:]
    step = pl.program_id(0)
    local = mine.shape[-1] // 6
    rows = normed.shape[0] // RING
    core = order[0] // RING

    @pl.when(step == 0)
    def _():
        for side, source in enumerate((mine, other)):
            for target, column in ((normed, 4 * local), (up, 5 * local)):
                for level in range(LEV // 2):
                    part = source[core * (LEV // 2) + level, :, column : column + local]
                    turned[level * local : (level + 1) * local] = part.T
                for place in range(RING):
                    start = pl.multiple_of((order[place] - core * RING) * rows, rows)
                    target[place * rows : (place + 1) * rows, side * SPAN : (side + 1) * SPAN] = (
                        turned[pl.ds(start, rows), :]
                    )

    def side_by_side(first, last):
        return jnp.concatenate(
            [
                jnp.concatenate([item[STEP * step + sub, :, first:last] for sub in range(STEP)], axis=1)
                for item in (mine, other)
            ]
        )

    into = dot(normed[...], side_by_side(0, 3 * local)).astype(BF16)
    outof = dot(up[...], side_by_side(3 * local, 4 * local)).astype(BF16)
    half = rows // 2
    for index, out in enumerate(outs):
        place = slice(index * half, (index + 1) * half)
        for sub in range(STEP):
            out[sub, :, : 3 * local] = into[place, sub * 3 * local : (sub + 1) * 3 * local]
            out[sub, :, 3 * local :] = outof[place, sub * local : (sub + 1) * local]


def finish_kernel(order, *refs):
    inputs, (into, outof, bias, turned) = refs[:SHARES], refs[SHARES:]
    rows = into.shape[2] // SHARES
    local = outof.shape[1]
    bias_total = jnp.zeros(bias.shape, F32)
    for source in inputs:
        bias_total += source[BLOCKS * rows :, :].astype(F32)
    bias[...] = bias_total
    for block in range(BLOCKS):
        for index, source in enumerate(inputs):
            start = pl.multiple_of(order[index] * rows, rows)
            values = source[block * rows : (block + 1) * rows, :].astype(F32)
            for part in range(3):
                into[block, part, pl.ds(start, rows), :] = values[:, part * local : (part + 1) * local]
            turned[pl.ds(start, rows), :] = values[:, 3 * local :]
        outof[block] = turned[...].T


def whole(*shape):
    return pl.BlockSpec(shape, lambda g, order: (0,) * len(shape))


def by_group(*shape):
    return pl.BlockSpec((STEP,) + shape, lambda g, order: (g,) + (0,) * len(shape))


def by_head():
    return pl.BlockSpec((2 * STEP, SPAN, SPAN), lambda g, order: (g, 0, 0))


def by_rows(base):
    start = base // STEP
    return pl.BlockSpec((2 * STEP * ROW_GROUPS, WW * WIDE), lambda g, order: (g + start, 0))


def piece_specs(rows, columns):
    pair = pl.BlockSpec((2, STEP, rows, columns), lambda g, order: (0, g, 0, 0))
    return ([pair] * (RING - 1) + [by_group(rows, columns)] * 2) * 2


def cost(flops, bytes_accessed):
    return pl.CostEstimate(flops=flops, bytes_accessed=bytes_accessed, transcendentals=0)


def run_forward(order, halves, gain, marks, bias, block, pieces):
    width = halves[0].shape[1]
    rows, columns = pieces[0].shape[2:]
    local = columns // 4
    shape = jax.ShapeDtypeStruct
    first, second, *saved = pl.pallas_call(
        forward_kernel,
        grid_spec=pltpu.PrefetchScalarGridSpec(
            num_scalar_prefetch=1,
            grid=(LEV // STEP,),
            in_specs=[
                whole(SPAN // 2, width),
                whole(SPAN // 2, width),
                whole(1, width),
                whole(2, SPAN),
                by_rows(block * LEV),
                *piece_specs(rows, columns),
            ],
            out_specs=[
                whole(SPAN // 2, width),
                whole(SPAN // 2, width),
                by_group(SPAN, 3 * local),
                by_group(SPAN, local),
                by_head(),
            ],
            scratch_shapes=[
                pltpu.VMEM((width, STEP * columns), BF16),
                pltpu.VMEM((SPAN, width), BF16),
                pltpu.VMEM((SPAN, width), F32),
                pltpu.VMEM((SPAN, SPAN), F32),
                pltpu.VMEM((2 * STEP, SPAN, SPAN), F32),
            ],
        ),
        out_shape=[
            shape((SPAN // 2, width), BF16),
            shape((SPAN // 2, width), BF16),
            shape((LEV, SPAN, 3 * local), BF16),
            shape((LEV, SPAN, local), BF16),
            shape((2 * LEV, SPAN, SPAN), F32),
        ],
        compiler_params=pltpu.CompilerParams(vmem_limit_bytes=VMEM),
        cost_estimate=cost(14 * 10**9, 2 * 10**7),
    )(order, *halves, gain, marks, bias, *pieces)
    return (first, second), saved


def run_backward(order, last, upstream, halves, gain, saved, pieces):
    width = halves[0].shape[1]
    rows, columns = pieces[0].shape[2:]
    local = columns // 4
    shape = jax.ShapeDtypeStruct
    half = whole(SPAN // 2, width)
    above = [half] * 2
    scratch = [
        pltpu.VMEM((width, STEP * columns), BF16),
        pltpu.VMEM((SPAN, width), BF16),
        pltpu.VMEM((SPAN, width), BF16),
        pltpu.VMEM((SPAN, width), F32),
    ]
    if last:
        above += [half] * 4 + [whole(1, width)]
        scratch.append(pltpu.VMEM((SPAN, width), F32))
    first, second, scores, operands = pl.pallas_call(
        functools.partial(backward_kernel, last),
        grid_spec=pltpu.PrefetchScalarGridSpec(
            num_scalar_prefetch=1,
            grid=(LEV // STEP,),
            in_specs=[
                *above,
                half,
                half,
                whole(1, width),
                by_group(SPAN, 3 * local),
                by_group(SPAN, local),
                by_head(),
                *piece_specs(rows, columns),
            ],
            out_specs=[half, half, by_rows(0), by_group(SPAN, 6 * local)],
            scratch_shapes=scratch,
        ),
        out_shape=[
            shape((SPAN // 2, width), BF16),
            shape((SPAN // 2, width), BF16),
            shape((2 * LEV * ROW_GROUPS, WW * WIDE), F32),
            shape((LEV, SPAN, 6 * local), BF16),
        ],
        compiler_params=pltpu.CompilerParams(vmem_limit_bytes=VMEM),
        cost_estimate=cost(14 * 10**9, 2 * 10**7),
    )(order, *upstream, *halves, gain, *saved, *pieces)
    return (first, second), scores, operands


def run_weights(order, mine, other, rows):
    local = mine.shape[-1] // 6
    width, columns = LEV * local, 4 * local
    return pl.pallas_call(
        weights_kernel,
        grid_spec=pltpu.PrefetchScalarGridSpec(
            num_scalar_prefetch=1,
            grid=(LEV // STEP,),
            in_specs=[whole(*mine.shape), whole(*other.shape)],
            out_specs=[by_group(rows, columns)] * 8,
            scratch_shapes=[
                pltpu.VMEM((width // 2, SPAN), BF16),
                pltpu.VMEM((width // 2, 2 * SPAN), BF16),
                pltpu.VMEM((width // 2, 2 * SPAN), BF16),
            ],
        ),
        out_shape=[jax.ShapeDtypeStruct((LEV, rows, columns), BF16)] * 8,
        compiler_params=pltpu.CompilerParams(vmem_limit_bytes=VMEM),
        cost_estimate=cost(5 * 10**9, 10**7),
    )(order, mine, other)


def run_finish(order, parts, width, local):
    shape = jax.ShapeDtypeStruct

    shapes = [
        (BLOCKS, 3, width, local),
        (BLOCKS, local, width),
        (BIAS_ROWS, 4 * local),
    ]
    return pl.pallas_call(
        finish_kernel,
        grid_spec=pltpu.PrefetchScalarGridSpec(
            num_scalar_prefetch=1,
            grid=(),
            in_specs=[whole_of(*item.shape) for item in parts],
            out_specs=[whole_of(*extent) for extent in shapes],
            scratch_shapes=[pltpu.VMEM((width, local), F32)],
        ),
        out_shape=[shape(extent, F32) for extent in shapes],
        compiler_params=pltpu.CompilerParams(vmem_limit_bytes=VMEM),
    )(order, *parts)


def bias_message(scores, by_slot, columns):
    sums = slot_sums(scores, by_slot)
    slots = sums.shape[-1]
    flat = sums.reshape(BLOCKS, LEV, 2 * slots).transpose(1, 0, 2).reshape(LEV, -1)
    flat = jnp.pad(flat, ((0, 0), (0, BIAS_ROWS * columns - flat.shape[1])))
    return flat.reshape(LEV, BIAS_ROWS, columns).astype(BF16)


def on_device(
    tokens,
    norm_gain,
    qkv_weight,
    out_weight,
    bias_table,
    rel_index,
    region_ids,
    row_valid,
    grad_out,
):
    width = tokens.shape[-1]
    local = qkv_weight.shape[-1]
    slots = bias_table.shape[-1]
    columns = 4 * local
    rows = width // SHARES
    even = lax.axis_index("lev") % 2 == 0
    order = share_order()
    gains = [norm_gain[block : block + 1] for block in range(BLOCKS)]

    own = [own_rows(qkv_weight, out_weight, b, order[0]) for b in range(BLOCKS)]
    own.append(table_rows(bias_table, columns))
    *part, tables = pack_levels(gather_levels(jnp.concatenate(own)), rows)
    tokens, grad_out = after((tokens, grad_out), tables)

    both = enter_windows(jnp.concatenate([tokens, grad_out]), even)
    start = tuple(item[0] for item in both)
    grad_start = tuple(item[1] for item in both)
    grad_shifted = wrap_left(grad_start)

    following = from_next_lon(region_ids[:, :REACH])
    shifted = jnp.concatenate([region_ids[:, REACH:], following], axis=1)
    living = by_half(jnp.broadcast_to(row_valid[:, None], (WH, WW)))
    marks = [
        jnp.concatenate([by_half(pick(even, item[:, :WW], item[:, WW:])), living])
        for item in (region_ids, shifted)
    ]

    by_slot = slot_table(rel_index, slots)
    parts = tables.reshape(LEV, -1)[:, : 3 * bias_table.size]
    parts = parts.reshape(LEV, 3, BLOCKS, 2, slots).transpose(1, 2, 0, 3, 4)
    bias = expand_bias(parts.reshape(3, BLOCKS * 2 * LEV, slots), by_slot)
    pieces_0, later_part = second_ring(part[0], (bias,), part[1])
    pieces_1, _ = second_ring(later_part)

    middle, saved_0 = run_forward(order, start, gains[0], marks[0], bias, 0, pieces_0)
    second = wrap_left(middle)
    far = after(pieces_1[3:5], middle[0])
    pieces_1 = (*pieces_1[:3], *far, *pieces_1[5:8], *[swap_cores(item) for item in far])
    ended, saved_1 = run_forward(order, second, gains[1], marks[1], bias, 1, pieces_1)

    grad_normed, scores_1, operands_1 = run_backward(
        order, False, grad_shifted, second, gains[1], saved_1, pieces_1
    )
    later_grad = wrap_right(grad_normed)
    swapped_1 = swap_cores(operands_1)
    ended = wrap_right(ended)
    upstream = after([*grad_start, *later_grad, *middle, gains[1]], *ended)
    grad_first, scores_0, operands_0 = run_backward(
        order, True, upstream, start, gains[0], saved_0, pieces_0
    )
    swapped_0 = swap_cores(operands_0)
    operands_1, swapped_1 = after((operands_1, swapped_1), operands_0)
    grads_1 = run_weights(order, operands_1, swapped_1, rows // 2)
    begun = scatter_start(grads_1)
    operands_0, swapped_0 = after((operands_0, swapped_0), *grads_1)
    grads_0 = run_weights(order, operands_0, swapped_0, rows // 2)
    far_a, far_b, ahead_b, behind_a = after(begun, *grads_0)
    ahead_a, behind_b = scatter_middle(grads_1, far_a, far_b)
    parts_1 = (grads_1[0], ahead_a, behind_a, grads_1[1], ahead_b, behind_b)
    far_a, far_b, ahead_b, behind_a = scatter_start(grads_0)
    ahead_a, behind_b = scatter_middle(grads_0, far_a, far_b)
    parts_0 = (grads_0[0], ahead_a, behind_a, grads_0[1], ahead_b, behind_b)

    scores = after((scores_0, scores_1), *grads_0)
    message = bias_message(scores, by_slot, columns)
    total = sum_levels(parts_0 + parts_1, message)
    finished = spread_sums(total)
    grad_first, ended = after((grad_first, ended), total)
    grad_tokens = leave_windows(grad_first, even)
    output = leave_windows(ended, even)

    grad_qkv, grad_out_weight, bias_rows = run_finish(order, finished, width, local)
    grad_qkv = grad_qkv.transpose(0, 2, 1, 3)
    grad_bias = bias_rows.reshape(-1)[: BLOCKS * 2 * slots].reshape(BLOCKS, 2, slots)
    return (output[None], grad_tokens[None], grad_qkv, grad_out_weight, grad_bias)


def solution(mesh):
    placed = (
        P("lev", "lat", "lon", None),
        P(),
        P(None, None, None, "lev"),
        P(None, "lev", None),
        P(None, "lev", None),
        P(),
        P("lat", "lon"),
        P("lat"),
        P("lev", "lat", "lon", None),
    )
    return jax.shard_map(
        on_device,
        mesh=mesh,
        in_specs=placed,
        out_specs=(
            P("lev", "lat", "lon", None),
            P("lev", "lat", "lon", None),
            P(None, None, None, "lev"),
            P(None, "lev", None),
            P(None, "lev", None),
        ),
        check_vma=False,
    )
```

```python
import functools

import jax
import jax.numpy as jnp
import numpy as np
from jax import lax
from jax.experimental import pallas as pl
from jax.experimental.pallas import tpu as pltpu
from jax.sharding import PartitionSpec as P

WL = 2
WH = 6
WW = 12
SPAN = WL * WH * WW
REACH = WW // 2
BLOCKS = 2
EPSILON = 1e-05
MASKED = -1e30
F32 = jnp.float32
BF16 = jnp.bfloat16

AXES = ("lon", "lev", "lat")
LEV = 8
RING = 4
OFFSETS = (0, 1, -1, 2)
SHARES = 2 * RING
STEP = 2
BIAS_ROWS = 16
VMEM = 56 * 1024 * 1024


def decode(device):
    lat, lev, lon = device % 2, device // 2 % LEV, device // (2 * LEV)
    return (2 * lat + lon // 8, lon // 2 % 4, lon % 2, lev)


def encode(x, y, core, lev):
    x, y, lev = x % RING, y % RING, lev % LEV
    return (((x % 2) * 8 + y * 2 + core) * LEV + lev) * 2 + x // 2


def send(value, target):
    pairs = [(i, encode(*target(*decode(i)))) for i in range(2 * RING * RING * LEV)]
    return lax.ppermute(value, AXES, pairs)


def along(value, ring, step):
    def target(x, y, core, lev):
        if (core == 0) == (ring == 1):
            return (x + step, y, core, lev)
        return (x, y + step, core, lev)

    return send(value, target)


def along_levels(value, step):
    return send(value, lambda x, y, core, lev: (x, y, core, lev + step))


def swap_cores(value):
    return send(value, lambda x, y, core, lev: (x, y, 1 - core, lev))


def swap_levels(value):
    return send(value, lambda x, y, core, lev: (x, y, core, lev ^ 1))


def to_window(value, step):
    def target(x, y, core, lev):
        lon = (x % 2) * 8 + y * 2 + core
        index = (2 * lon + lev % 2 + step) % 32
        lon, side = index // 2, index % 2
        return (2 * (x // 2) + lon // 8, lon // 2 % 4, lon % 2, lev - lev % 2 + side)

    return send(value, target)


def from_next_lon(value):
    def target(x, y, core, lev):
        lon = ((x % 2) * 8 + y * 2 + core - 1) % 16
        return (2 * (x // 2) + lon // 8, lon // 2 % 4, lon % 2, lev)

    return send(value, target)


def after(values, *others):
    tied = lax.optimization_barrier((values, others))
    return tied[0]


def share_order():
    lon, lat = lax.axis_index("lon"), lax.axis_index("lat")
    x, y, core = 2 * lat + lon // 8, lon // 2 % 4, lon % 2
    which = (core + jnp.arange(2, dtype=jnp.int32)[:, None]) % 2
    place = jnp.where(which == 0, y, x) + jnp.array(OFFSETS, jnp.int32)[None]
    return (which * RING + place % RING).reshape(-1).astype(jnp.int32)


def own_rows(qkv_weight, out_weight, block, share):
    width, parts, local = qkv_weight.shape[1:]
    rows = width // SHARES
    start = share * rows
    zero = jnp.zeros_like(start)
    into = lax.dynamic_slice(
        qkv_weight, (zero + block, start, zero, zero), (1, rows, parts, local)
    )[0]
    outof = lax.dynamic_slice(out_weight, (zero + block, zero, start), (1, local, rows))[0].T
    return jnp.concatenate([into[:, part] for part in range(parts)] + [outof], axis=1)


def table_rows(bias_table, columns):
    high = lax.reduce_precision(bias_table, 8, 7)
    middle = lax.reduce_precision(bias_table - high, 8, 7)
    low = bias_table - high - middle
    flat = jnp.stack([high, middle, low]).reshape(-1)
    rows = -(-flat.shape[0] // columns // BIAS_ROWS) * BIAS_ROWS
    return jnp.pad(flat, (0, rows * columns - flat.shape[0])).reshape(rows, columns).astype(BF16)


def gather_levels(own):
    up, down = [own], [own]
    for _ in range(3):
        up.append(along_levels(up[-1], -1))
        down.append(along_levels(down[-1], 1))
    up.append(along_levels(up[-1], -1))
    return up + down[:0:-1]


def scatter_levels(messages):
    up, down = messages[LEV // 2], messages[LEV // 2 + 1]
    for step in range(LEV // 2 - 1, 0, -1):
        up = add_low(messages[step], along_levels(up, 1))
        if step > 1:
            down = add_low(messages[LEV + 1 - step], along_levels(down, -1))
    return add_low(messages[0], along_levels(up, 1), along_levels(down, -1))


def pack_kernel(*refs):
    parts, weights, tables = refs[:LEV], refs[LEV : LEV + BLOCKS], refs[LEV + BLOCKS]
    rows = weights[0].shape[2]
    for index, part in enumerate(parts):
        for block in range(BLOCKS):
            for half in range(2):
                start = (2 * block + half) * rows
                weights[block][half, index] = part[start : start + rows]
        tables[index] = part[2 * BLOCKS * rows :]


def pack_levels(parts, rows):
    height, columns = parts[0].shape
    out_shape = [jax.ShapeDtypeStruct((2, LEV, rows // 2, columns), BF16)] * BLOCKS
    out_shape.append(jax.ShapeDtypeStruct((LEV, height - BLOCKS * rows, columns), BF16))
    return pl.pallas_call(
        pack_kernel,
        out_shape=out_shape,
        compiler_params=pltpu.CompilerParams(vmem_limit_bytes=VMEM),
    )(*parts)


def second_ring(own, others=(), following=None):
    ahead, behind, swapped = along(own, 2, -1), along(own, 2, 1), swap_cores(own)
    if others:
        ahead, behind = after((ahead, behind), swapped, *others)
    halves = (ahead[0], behind[1])
    if following is not None:
        halves, following = lax.optimization_barrier((halves, following))
    far_a, far_b = along(halves[0], 2, -1), along(halves[1], 2, 1)
    rest = (ahead, behind, far_a, far_b)
    pieces = (own, *rest, swapped, *[swap_cores(item) for item in rest])
    if following is not None:
        following = after(following, pieces[6])
    return pieces, following


def add_low(*terms):
    return functools.reduce(jnp.add, [term.astype(F32) for term in terms]).astype(BF16)


def scatter_start(grads):
    return (
        along(grads[6], 2, 1),
        along(grads[7], 2, -1),
        along(grads[3], 2, 1),
        along(grads[4], 2, -1),
    )


def scatter_middle(grads, far_a, far_b):
    return (
        along(add_low(grads[2], far_a), 2, 1),
        along(add_low(grads[5], far_b), 2, -1),
    )


def levels_kernel(*refs):
    parts, bias, outs = refs[: 6 * BLOCKS], refs[6 * BLOCKS], refs[6 * BLOCKS + 1 :]
    rows = parts[0].shape[1]
    for level, out in enumerate(outs):
        for place in range(2 * BLOCKS):
            own, ahead, behind = parts[3 * place : 3 * place + 3]
            out[pl.ds(place * rows, rows), :] = own[level] + (ahead[level] + behind[level])
        out[pl.ds(2 * BLOCKS * rows, BIAS_ROWS), :] = bias[level]


def whole_of(*extent):
    return pl.BlockSpec(extent, lambda order: (0,) * len(extent))


def sum_levels(parts, bias_rows):
    rows, columns = parts[0].shape[1:]
    height = 2 * BLOCKS * rows + BIAS_ROWS
    messages = pl.pallas_call(
        levels_kernel,
        out_shape=[jax.ShapeDtypeStruct((height, columns), BF16)] * LEV,
        compiler_params=pltpu.CompilerParams(vmem_limit_bytes=VMEM),
    )(*parts, bias_rows)
    return scatter_levels(messages)


def spread_sums(total):
    total = add_low(total, along(total, 1, 1), along(total, 1, -1), along(total, 1, 2))
    mine = [total, along(total, 2, -1), along(total, 2, 1), along(total, 2, -2)]
    return mine + [swap_cores(item) for item in mine]


def pick(first, own, other):
    return jnp.where(first, own, other)


def enter_windows(field, even):
    left, right = field[..., :WW, :], field[..., WW:, :]
    keep = pick(even, left, right)
    got = swap_levels(pick(even, right, left))
    window = jnp.stack([pick(even, keep, got), pick(even, got, keep)], axis=-4)
    window = jnp.moveaxis(window, -2, -4)
    flat = window.reshape(window.shape[:-4] + (SPAN, window.shape[-1]))
    return flat[..., : SPAN // 2, :], flat[..., SPAN // 2 :, :]


def leave_windows(halves, even):
    shape = (REACH, WL, WH, halves[0].shape[-1])
    window = jnp.concatenate([item.reshape(shape) for item in halves]).transpose(1, 2, 0, 3)
    own = pick(even, window[0], window[1])
    got = swap_levels(pick(even, window[1], window[0]))
    return jnp.concatenate([pick(even, own, got), pick(even, got, own)], axis=1)


def wrap_left(halves):
    return (halves[1], to_window(halves[0], -1))


def wrap_right(halves):
    return (to_window(halves[1], 1), halves[0])


def by_half(values):
    return jnp.broadcast_to(values.T[:, None], (WW, WL, WH)).reshape(1, SPAN)


ROW_GROUPS = WL * WH
LINES = (2 * WL - 1) * (2 * WH - 1)
STEPS = 2 * WW - 1


CORNERS = [p * WH * WW + q * WW + r for p in (0, WL - 1) for q in (0, WH - 1) for r in (0, WW - 1)]


LANES = 32
WIDE = 256
REVERSED = LINES * LANES


def offset_places():
    table = np.zeros((len(CORNERS) * SPAN, REVERSED), np.float32)
    for a in range(1 - WL, WL):
        for b in range(1 - WH, WH):
            for c in range(1 - WW, WW):
                p = [(size - 1) * (step > 0) for size, step in ((WL, a), (WH, b), (WW, c))]
                k = [at - step for at, step in zip(p, (a, b, c))]
                row = CORNERS.index((p[0] * WH + p[1]) * WW + p[2])
                offset = ((WL - 1 - a) * (2 * WH - 1) + WH - 1 - b) * LANES + c + WW - 1
                table[row * SPAN + (k[0] * WH + k[1]) * WW + k[2], offset] = 1
    return table


def line_lanes(line):
    level, row = line // WH, line % WH
    for other in range(WL):
        yield other, ((WL - 1 - level + other) * (2 * WH - 1) + WH - 1 - row) * LANES


def column_table():
    table = np.zeros((ROW_GROUPS, LANES, WW, WIDE), np.float32)
    for line in range(ROW_GROUPS):
        for p in range(WW):
            for k in range(WW):
                table[line, p - k + WW - 1, p, k * ROW_GROUPS + line] = 1
    return table.reshape(ROW_GROUPS * LANES, WW * WIDE).astype(BF16)


def slot_table(rel_index, slots):
    rows = jnp.concatenate([rel_index[at : at + 1] for at in CORNERS], axis=1)
    digits = jnp.concatenate([rows // 32, rows % 32]).astype(BF16)
    places = dot(digits, offset_places().astype(BF16))
    named = np.arange(REVERSED) % LANES < STEPS
    names = jnp.where(named, places[0] * 32 + places[1], -1).astype(jnp.int32)
    return (names[:, None] == jnp.arange(slots)[None, :]).astype(BF16)


TILE = 128
BIAS_LANES = 2 * WIDE
SLOT_LANES = 4 * WIDE


def bias_kernel(steps, columns, out, rows, spread):
    count = steps.shape[0] // 3
    side = WH * LANES

    @pl.when(pl.program_id(0) == 0)
    def _():
        for line in range(ROW_GROUPS):
            for other, lane in line_lanes(line):
                value = steps[:, lane : lane + side]
                for part in range(3):
                    start = (part * ROW_GROUPS + line) * count
                    rows[start : start + count, other * side : (other + 1) * side] = value[
                        part * count : (part + 1) * count
                    ]

    values = dot(rows[...], columns[...])
    size = ROW_GROUPS * count
    values = values[:size] + values[size : 2 * size] + values[2 * size :]
    for tile in range(BIAS_LANES // TILE):
        lanes = slice(tile * TILE, (tile + 1) * TILE)
        for line in range(ROW_GROUPS):
            spread[tile, pl.ds(line, count, ROW_GROUPS), :] = values[
                line * count : (line + 1) * count, lanes
            ]
        out[:, lanes] = spread[tile]


def expand_bias(tables, by_slot):
    count = tables.shape[1]
    steps = dot_nt(tables.reshape(3 * count, -1), by_slot).astype(BF16)
    return pl.pallas_call(
        bias_kernel,
        grid=(WW * WIDE // BIAS_LANES,),
        in_specs=[
            pl.BlockSpec(steps.shape, lambda c: (0, 0)),
            pl.BlockSpec((ROW_GROUPS * LANES, BIAS_LANES), lambda c: (0, c)),
        ],
        out_specs=pl.BlockSpec((count * ROW_GROUPS, BIAS_LANES), lambda c: (0, c)),
        out_shape=jax.ShapeDtypeStruct((count * ROW_GROUPS, WW * WIDE), F32),
        scratch_shapes=[
            pltpu.VMEM((3 * ROW_GROUPS * count, ROW_GROUPS * LANES), BF16),
            pltpu.VMEM((BIAS_LANES // TILE, ROW_GROUPS * count, TILE), F32),
        ],
        compiler_params=pltpu.CompilerParams(vmem_limit_bytes=VMEM),
        cost_estimate=cost(9 * 10**9, 10**7),
    )(steps, column_table())


def slots_kernel(*refs):
    scores, columns, out, lines = refs[:BLOCKS], refs[BLOCKS], refs[BLOCKS + 1], refs[BLOCKS + 2]
    size = scores[0].shape[0]
    count = BLOCKS * size // ROW_GROUPS
    side = WH * LANES

    @pl.when(pl.program_id(0) == 0)
    def _():
        lines[...] = jnp.zeros_like(lines)

    for block in range(BLOCKS):
        part = dot_nt(scores[block][...].astype(BF16), columns[...])
        for tile in range(lines.shape[0]):
            lines[tile, pl.ds(block * size, size), :] += part[:, tile * TILE : (tile + 1) * TILE]

    @pl.when(pl.program_id(0) == WW * WIDE // SLOT_LANES - 1)
    def _():
        out[...] = jnp.zeros_like(out)
        for line in range(ROW_GROUPS):
            values = jnp.concatenate(
                [lines[tile, pl.ds(line, count, ROW_GROUPS), :] for tile in range(lines.shape[0])],
                axis=1,
            )
            for other, lane in line_lanes(line):
                out[:, lane : lane + side] += values[:, other * side : (other + 1) * side]


def slot_sums(scores, by_slot):
    size = scores[0].shape[0]
    count = BLOCKS * size // ROW_GROUPS
    wide = ROW_GROUPS * LANES
    steps = pl.pallas_call(
        slots_kernel,
        grid=(WW * WIDE // SLOT_LANES,),
        in_specs=[pl.BlockSpec((size, SLOT_LANES), lambda c: (0, c))] * BLOCKS
        + [pl.BlockSpec((wide, SLOT_LANES), lambda c: (0, c))],
        out_specs=pl.BlockSpec((count, REVERSED), lambda c: (0, 0)),
        out_shape=jax.ShapeDtypeStruct((count, REVERSED), F32),
        scratch_shapes=[pltpu.VMEM((wide // TILE, BLOCKS * size, TILE), F32)],
        compiler_params=pltpu.CompilerParams(vmem_limit_bytes=VMEM),
        cost_estimate=cost(6 * 10**9, 10**7),
    )(*scores, column_table())
    return dot(steps.astype(BF16), by_slot)


def dot(a, b):
    return jnp.dot(a, b, preferred_element_type=F32)


def dot_nt(a, b):
    return lax.dot_general(a, b, (((1,), (1,)), ((), ())), preferred_element_type=F32)


def dot_tn(a, b):
    return lax.dot_general(a, b, (((0,), (0,)), ((), ())), preferred_element_type=F32)


def standardise(field):
    values = field.astype(F32)
    centre = jnp.mean(values, axis=-1, keepdims=True)
    spread = jnp.mean((values - centre) ** 2, axis=-1, keepdims=True)
    inv_spread = lax.rsqrt(spread + EPSILON)
    return (values - centre) * inv_spread, inv_spread


def norm_adjoint(cotan, field, gain):
    normed, inv_spread = standardise(field)
    scaled = cotan.astype(F32) * gain
    first = jnp.mean(scaled, axis=-1, keepdims=True)
    second = jnp.mean(scaled * normed, axis=-1, keepdims=True)
    return inv_spread * (scaled - first - normed * second)


def piece_slots():
    for index in range(PIECES):
        side, place = index // (RING * RING), index % (RING * RING)
        yield index, side, place


def collect_rows(order, pieces, weights, sub):
    rows, local = pieces[0].shape[2], pieces[0].shape[3] // 4
    into, last = 3 * local, STEP * 3 * local
    for index in range(SHARES):
        side, place = index // RING, index % RING
        for half in range(2):
            if place < RING - 1:
                values = pieces[5 * side + place][half, sub]
            else:
                values = pieces[5 * side + RING - 1 + half][sub]
            start = pl.multiple_of((2 * order[index] + half) * rows, rows)
            weights[pl.ds(start, rows), sub * into : (sub + 1) * into] = values[:, :into]
            weights[pl.ds(start, rows), last + sub * local : last + (sub + 1) * local] = values[
                :, into:
            ]


def join(halves):
    return jnp.concatenate([item[...].astype(F32) for item in halves], axis=0)


def split(values, halves):
    halves[0][...] = values[: SPAN // 2].astype(BF16)
    halves[1][...] = values[SPAN // 2 :].astype(BF16)


def head_masks(width):
    lane = lax.broadcasted_iota(jnp.int32, (1, width), 1)
    return [(lane // (width // 2) == head).astype(F32).astype(BF16) for head in range(2)]


def forward_kernel(order, *refs):
    halves, (gain, marks, bias), pieces = refs[:2], refs[2:5], refs[5:15]
    after, (packed_out, mixed_out, probs_out) = refs[15:17], refs[17:20]
    weights, normed, total, allowed, added = refs[20:]
    group = pl.program_id(0)
    local = mixed_out.shape[-1]

    @pl.when(group == 0)
    def _():
        values, _ = standardise(join(halves))
        normed[...] = (values * gain[...]).astype(BF16)
        total[...] = jnp.zeros_like(total)
        here = lax.broadcasted_iota(jnp.int32, (SPAN, SPAN), 0)
        there = lax.broadcasted_iota(jnp.int32, (SPAN, SPAN), 1)
        labels = jnp.broadcast_to(marks[0:1].astype(F32), (SPAN, SPAN))
        living = jnp.broadcast_to(marks[1:2], (SPAN, SPAN))
        seen = (labels == labels.T) & ((living > 0) | (here == there))
        allowed[...] = jnp.where(seen, 1.0, 0.0)

    scale = (local // 2) ** (-0.5)
    for sub in range(STEP):
        collect_rows(order, pieces, weights, sub)
        for head in range(2):
            for column in range(WW):
                rows = pl.ds((2 * sub + head) * ROW_GROUPS, ROW_GROUPS)
                lanes = pl.ds(column * WIDE, SPAN)
                place = pl.ds(column * ROW_GROUPS, ROW_GROUPS)
                added[2 * sub + head, place, :] = bias[rows, lanes]
    masks = head_masks(local)
    heads = [(sub, head) for sub in range(STEP) for head in range(2)]
    queries, keys, values = [], [], []
    last = STEP * 3 * local
    side_by_side = dot(normed[...], weights[:, :last]).astype(BF16)
    for sub in range(STEP):
        packed = side_by_side[:, sub * 3 * local : (sub + 1) * 3 * local]
        packed_out[sub] = packed
        queries.append(packed[:, :local])
        keys.append(packed[:, local : 2 * local])
        values.append(packed[:, 2 * local :])
    seen = allowed[...] > 0
    scores = [dot_nt(queries[sub], keys[sub] * masks[head]) for sub, head in heads]
    scores = [
        jnp.where(seen, item * scale + added[index], MASKED) for index, item in enumerate(scores)
    ]
    tops = [jnp.max(item, axis=-1, keepdims=True) for item in scores]
    grown = [jnp.exp(item - top) for item, top in zip(scores, tops)]
    sums = [jnp.sum(item, axis=-1, keepdims=True) for item in grown]
    probs = [item / total_weight for item, total_weight in zip(grown, sums)]
    for index, item in enumerate(probs):
        probs_out[index] = item
    parts = [
        dot(item.astype(BF16), values[sub] * masks[head])
        for item, (sub, head) in zip(probs, heads)
    ]
    mixed = [(parts[2 * sub] + parts[2 * sub + 1]).astype(BF16) for sub in range(STEP)]
    for sub in range(STEP):
        mixed_out[sub] = mixed[sub]
    branch = dot_nt(jnp.concatenate(mixed, axis=1), weights[:, last:])
    total[...] += branch.astype(BF16).astype(F32)

    @pl.when(group == LEV // STEP - 1)
    def _():
        split(join(halves) + total[...].astype(BF16).astype(F32), after)


def backward_kernel(last, order, *refs):
    refs = list(refs)

    def take(count):
        taken, refs[:] = refs[:count], refs[count:]
        return taken

    grad_out = take(2)
    later_grad, later_field = (take(2), take(2)) if last else (None, None)
    later_gain = take(1)[0] if last else None
    field, (gain, packed_in, mixed_in, probs_in), pieces = take(2), take(4), take(10)
    outs, (scores_out, operands) = take(2), take(2)
    weights, normed, up, total = take(4)
    carried = take(1)[0] if last else None
    step = pl.program_id(0)
    local = mixed_in.shape[-1]

    @pl.when(step == 0)
    def _():
        values, _ = standardise(join(field))
        normed[...] = (values * gain[...]).astype(BF16)
        upstream = join(grad_out)
        if last:
            upstream = upstream + norm_adjoint(join(later_grad), join(later_field), later_gain[...])
            carried[...] = upstream
        up[...] = upstream.astype(BF16)
        total[...] = jnp.zeros_like(total)

    scores_out[...] = jnp.zeros_like(scores_out)
    scale = (local // 2) ** (-0.5)
    for sub in range(STEP):
        collect_rows(order, pieces, weights, sub)
    masks = head_masks(local)
    heads = [(sub, head) for sub in range(STEP) for head in range(2)]
    packed = [packed_in[sub] for sub in range(STEP)]
    queries, keys, values = (
        [item[:, part * local : (part + 1) * local] for item in packed] for part in range(3)
    )
    last_column = STEP * 3 * local
    cotan = dot(up[...], weights[:, last_column:]).astype(BF16)
    cotans = [cotan[:, sub * local : (sub + 1) * local] for sub in range(STEP)]
    grad_probs = [dot_nt(cotans[sub], values[sub] * masks[head]) for sub, head in heads]
    probs = [probs_in[index] for index in range(2 * STEP)]
    grad_value = [
        dot_tn(item.astype(BF16), cotans[sub] * masks[head])
        for item, (sub, head) in zip(probs, heads)
    ]
    inner = [
        jnp.sum(grad * item, axis=-1, keepdims=True) for grad, item in zip(grad_probs, probs)
    ]
    grad_scores = [
        item * (grad - dotted) for item, grad, dotted in zip(probs, grad_probs, inner)
    ]
    for index, item in enumerate(grad_scores):
        for column in range(WW):
            rows = pl.ds(index * ROW_GROUPS, ROW_GROUPS)
            lanes = pl.ds(column * WIDE, SPAN)
            scores_out[rows, lanes] = item[column * ROW_GROUPS : (column + 1) * ROW_GROUPS]
    low = [item.astype(BF16) for item in grad_scores]
    grad_query = [dot(item, keys[sub] * masks[head]) for item, (sub, head) in zip(low, heads)]
    grad_keys = [dot_tn(item, queries[sub] * masks[head]) for item, (sub, head) in zip(low, heads)]
    packed_parts = []
    for sub in range(STEP):
        first, second = 2 * sub, 2 * sub + 1
        grad_packed = jnp.concatenate(
            [
                ((grad_query[first] + grad_query[second]) * scale).astype(BF16),
                ((grad_keys[first] + grad_keys[second]) * scale).astype(BF16),
                (grad_value[first] + grad_value[second]).astype(BF16),
            ],
            axis=1,
        )
        packed_parts.append(grad_packed)
        here = pl.ds(pl.multiple_of((STEP * step + sub) * local, local), local)
        operands[sub, :, : 3 * local] = grad_packed
        operands[sub, :, 3 * local : 4 * local] = mixed_in[sub]
        operands[sub, :, 4 * local : 5 * local] = normed[:, here]
        operands[sub, :, 5 * local :] = up[:, here]
    part = dot_nt(jnp.concatenate(packed_parts, axis=1), weights[:, :last_column])
    total[...] += part.astype(BF16).astype(F32)

    @pl.when(step == LEV // STEP - 1)
    def _():
        if last:
            grad_normed = total[...].astype(BF16)
            split(carried[...] + norm_adjoint(grad_normed, join(field), gain[...]), outs)
        else:
            split(total[...], outs)


def weights_kernel(order, mine, other, *refs):
    outs, (turned, normed, up) = refs[:8], refs[8:]
    step = pl.program_id(0)
    local = mine.shape[-1] // 6
    rows = normed.shape[0] // RING
    core = order[0] // RING

    @pl.when(step == 0)
    def _():
        for side, source in enumerate((mine, other)):
            for target, column in ((normed, 4 * local), (up, 5 * local)):
                for level in range(LEV // 2):
                    part = source[core * (LEV // 2) + level, :, column : column + local]
                    turned[level * local : (level + 1) * local] = part.T
                for place in range(RING):
                    start = pl.multiple_of((order[place] - core * RING) * rows, rows)
                    target[place * rows : (place + 1) * rows, side * SPAN : (side + 1) * SPAN] = (
                        turned[pl.ds(start, rows), :]
                    )

    def side_by_side(first, last):
        return jnp.concatenate(
            [
                jnp.concatenate([item[STEP * step + sub, :, first:last] for sub in range(STEP)], axis=1)
                for item in (mine, other)
            ]
        )

    into = dot(normed[...], side_by_side(0, 3 * local)).astype(BF16)
    outof = dot(up[...], side_by_side(3 * local, 4 * local)).astype(BF16)
    half = rows // 2
    for index, out in enumerate(outs):
        place = slice(index * half, (index + 1) * half)
        for sub in range(STEP):
            out[sub, :, : 3 * local] = into[place, sub * 3 * local : (sub + 1) * 3 * local]
            out[sub, :, 3 * local :] = outof[place, sub * local : (sub + 1) * local]


def finish_kernel(order, *refs):
    inputs, (into, outof, bias, turned) = refs[:SHARES], refs[SHARES:]
    rows = into.shape[2] // SHARES
    local = outof.shape[1]
    bias_total = jnp.zeros(bias.shape, F32)
    for source in inputs:
        bias_total += source[BLOCKS * rows :, :].astype(F32)
    bias[...] = bias_total
    for block in range(BLOCKS):
        for index, source in enumerate(inputs):
            start = pl.multiple_of(order[index] * rows, rows)
            values = source[block * rows : (block + 1) * rows, :].astype(F32)
            for part in range(3):
                into[block, part, pl.ds(start, rows), :] = values[:, part * local : (part + 1) * local]
            turned[pl.ds(start, rows), :] = values[:, 3 * local :]
        outof[block] = turned[...].T


def whole(*shape):
    return pl.BlockSpec(shape, lambda g, order: (0,) * len(shape))


def by_group(*shape):
    return pl.BlockSpec((STEP,) + shape, lambda g, order: (g,) + (0,) * len(shape))


def by_head():
    return pl.BlockSpec((2 * STEP, SPAN, SPAN), lambda g, order: (g, 0, 0))


def by_rows(base):
    start = base // STEP
    return pl.BlockSpec((2 * STEP * ROW_GROUPS, WW * WIDE), lambda g, order: (g + start, 0))


def piece_specs(rows, columns):
    pair = pl.BlockSpec((2, STEP, rows, columns), lambda g, order: (0, g, 0, 0))
    return ([pair] * (RING - 1) + [by_group(rows, columns)] * 2) * 2


def cost(flops, bytes_accessed):
    return pl.CostEstimate(flops=flops, bytes_accessed=bytes_accessed, transcendentals=0)


def run_forward(order, halves, gain, marks, bias, block, pieces):
    width = halves[0].shape[1]
    rows, columns = pieces[0].shape[2:]
    local = columns // 4
    shape = jax.ShapeDtypeStruct
    first, second, *saved = pl.pallas_call(
        forward_kernel,
        grid_spec=pltpu.PrefetchScalarGridSpec(
            num_scalar_prefetch=1,
            grid=(LEV // STEP,),
            in_specs=[
                whole(SPAN // 2, width),
                whole(SPAN // 2, width),
                whole(1, width),
                whole(2, SPAN),
                by_rows(block * LEV),
                *piece_specs(rows, columns),
            ],
            out_specs=[
                whole(SPAN // 2, width),
                whole(SPAN // 2, width),
                by_group(SPAN, 3 * local),
                by_group(SPAN, local),
                by_head(),
            ],
            scratch_shapes=[
                pltpu.VMEM((width, STEP * columns), BF16),
                pltpu.VMEM((SPAN, width), BF16),
                pltpu.VMEM((SPAN, width), F32),
                pltpu.VMEM((SPAN, SPAN), F32),
                pltpu.VMEM((2 * STEP, SPAN, SPAN), F32),
            ],
        ),
        out_shape=[
            shape((SPAN // 2, width), BF16),
            shape((SPAN // 2, width), BF16),
            shape((LEV, SPAN, 3 * local), BF16),
            shape((LEV, SPAN, local), BF16),
            shape((2 * LEV, SPAN, SPAN), F32),
        ],
        compiler_params=pltpu.CompilerParams(vmem_limit_bytes=VMEM),
        cost_estimate=cost(14 * 10**9, 2 * 10**7),
    )(order, *halves, gain, marks, bias, *pieces)
    return (first, second), saved


def run_backward(order, last, upstream, halves, gain, saved, pieces):
    width = halves[0].shape[1]
    rows, columns = pieces[0].shape[2:]
    local = columns // 4
    shape = jax.ShapeDtypeStruct
    half = whole(SPAN // 2, width)
    above = [half] * 2
    scratch = [
        pltpu.VMEM((width, STEP * columns), BF16),
        pltpu.VMEM((SPAN, width), BF16),
        pltpu.VMEM((SPAN, width), BF16),
        pltpu.VMEM((SPAN, width), F32),
    ]
    if last:
        above += [half] * 4 + [whole(1, width)]
        scratch.append(pltpu.VMEM((SPAN, width), F32))
    first, second, scores, operands = pl.pallas_call(
        functools.partial(backward_kernel, last),
        grid_spec=pltpu.PrefetchScalarGridSpec(
            num_scalar_prefetch=1,
            grid=(LEV // STEP,),
            in_specs=[
                *above,
                half,
                half,
                whole(1, width),
                by_group(SPAN, 3 * local),
                by_group(SPAN, local),
                by_head(),
                *piece_specs(rows, columns),
            ],
            out_specs=[half, half, by_rows(0), by_group(SPAN, 6 * local)],
            scratch_shapes=scratch,
        ),
        out_shape=[
            shape((SPAN // 2, width), BF16),
            shape((SPAN // 2, width), BF16),
            shape((2 * LEV * ROW_GROUPS, WW * WIDE), F32),
            shape((LEV, SPAN, 6 * local), BF16),
        ],
        compiler_params=pltpu.CompilerParams(vmem_limit_bytes=VMEM),
        cost_estimate=cost(14 * 10**9, 2 * 10**7),
    )(order, *upstream, *halves, gain, *saved, *pieces)
    return (first, second), scores, operands


def run_weights(order, mine, other, rows):
    local = mine.shape[-1] // 6
    width, columns = LEV * local, 4 * local
    return pl.pallas_call(
        weights_kernel,
        grid_spec=pltpu.PrefetchScalarGridSpec(
            num_scalar_prefetch=1,
            grid=(LEV // STEP,),
            in_specs=[whole(*mine.shape), whole(*other.shape)],
            out_specs=[by_group(rows, columns)] * 8,
            scratch_shapes=[
                pltpu.VMEM((width // 2, SPAN), BF16),
                pltpu.VMEM((width // 2, 2 * SPAN), BF16),
                pltpu.VMEM((width // 2, 2 * SPAN), BF16),
            ],
        ),
        out_shape=[jax.ShapeDtypeStruct((LEV, rows, columns), BF16)] * 8,
        compiler_params=pltpu.CompilerParams(vmem_limit_bytes=VMEM),
        cost_estimate=cost(5 * 10**9, 10**7),
    )(order, mine, other)


def run_finish(order, parts, width, local):
    shape = jax.ShapeDtypeStruct

    shapes = [
        (BLOCKS, 3, width, local),
        (BLOCKS, local, width),
        (BIAS_ROWS, 4 * local),
    ]
    return pl.pallas_call(
        finish_kernel,
        grid_spec=pltpu.PrefetchScalarGridSpec(
            num_scalar_prefetch=1,
            grid=(),
            in_specs=[whole_of(*item.shape) for item in parts],
            out_specs=[whole_of(*extent) for extent in shapes],
            scratch_shapes=[pltpu.VMEM((width, local), F32)],
        ),
        out_shape=[shape(extent, F32) for extent in shapes],
        compiler_params=pltpu.CompilerParams(vmem_limit_bytes=VMEM),
    )(order, *parts)


def bias_message(scores, by_slot, columns):
    sums = slot_sums(scores, by_slot)
    slots = sums.shape[-1]
    flat = sums.reshape(BLOCKS, LEV, 2 * slots).transpose(1, 0, 2).reshape(LEV, -1)
    flat = jnp.pad(flat, ((0, 0), (0, BIAS_ROWS * columns - flat.shape[1])))
    return flat.reshape(LEV, BIAS_ROWS, columns).astype(BF16)


def on_device(
    tokens,
    norm_gain,
    qkv_weight,
    out_weight,
    bias_table,
    rel_index,
    region_ids,
    row_valid,
    grad_out,
):
    width = tokens.shape[-1]
    local = qkv_weight.shape[-1]
    slots = bias_table.shape[-1]
    columns = 4 * local
    rows = width // SHARES
    even = lax.axis_index("lev") % 2 == 0
    order = share_order()
    gains = [norm_gain[block : block + 1] for block in range(BLOCKS)]

    own = [own_rows(qkv_weight, out_weight, b, order[0]) for b in range(BLOCKS)]
    own.append(table_rows(bias_table, columns))
    *part, tables = pack_levels(gather_levels(jnp.concatenate(own)), rows)
    tokens, grad_out = after((tokens, grad_out), tables)

    both = enter_windows(jnp.concatenate([tokens, grad_out]), even)
    start = tuple(item[0] for item in both)
    grad_start = tuple(item[1] for item in both)
    grad_shifted = wrap_left(grad_start)

    following = from_next_lon(region_ids[:, :REACH])
    shifted = jnp.concatenate([region_ids[:, REACH:], following], axis=1)
    living = by_half(jnp.broadcast_to(row_valid[:, None], (WH, WW)))
    marks = [
        jnp.concatenate([by_half(pick(even, item[:, :WW], item[:, WW:])), living])
        for item in (region_ids, shifted)
    ]

    by_slot = slot_table(rel_index, slots)
    parts = tables.reshape(LEV, -1)[:, : 3 * bias_table.size]
    parts = parts.reshape(LEV, 3, BLOCKS, 2, slots).transpose(1, 2, 0, 3, 4)
    bias = expand_bias(parts.reshape(3, BLOCKS * 2 * LEV, slots), by_slot)
    pieces_0, later_part = second_ring(part[0], (bias, *start), part[1])
    pieces_1, _ = second_ring(later_part)

    middle, saved_0 = run_forward(order, start, gains[0], marks[0], bias, 0, pieces_0)
    second = wrap_left(middle)
    far = after(pieces_1[3:5], middle[0])
    pieces_1 = (*pieces_1[:3], *far, *pieces_1[5:8], *[swap_cores(item) for item in far])
    ended, saved_1 = run_forward(order, second, gains[1], marks[1], bias, 1, pieces_1)

    grad_normed, scores_1, operands_1 = run_backward(
        order, False, grad_shifted, second, gains[1], saved_1, pieces_1
    )
    later_grad = wrap_right(grad_normed)
    swapped_1 = swap_cores(operands_1)
    ended = wrap_right(ended)
    upstream = after([*grad_start, *later_grad, *middle, gains[1]], *ended)
    grad_first, scores_0, operands_0 = run_backward(
        order, True, upstream, start, gains[0], saved_0, pieces_0
    )
    swapped_0 = swap_cores(operands_0)
    operands_1, swapped_1 = after((operands_1, swapped_1), operands_0)
    grads_1 = run_weights(order, operands_1, swapped_1, rows // 2)
    begun = scatter_start(grads_1)
    operands_0, swapped_0 = after((operands_0, swapped_0), *grads_1)
    grads_0 = run_weights(order, operands_0, swapped_0, rows // 2)
    far_a, far_b, ahead_b, behind_a = after(begun, *grads_0)
    ahead_a, behind_b = scatter_middle(grads_1, far_a, far_b)
    parts_1 = (grads_1[0], ahead_a, behind_a, grads_1[1], ahead_b, behind_b)
    far_a, far_b, ahead_b, behind_a = scatter_start(grads_0)
    ahead_a, behind_b = scatter_middle(grads_0, far_a, far_b)
    parts_0 = (grads_0[0], ahead_a, behind_a, grads_0[1], ahead_b, behind_b)

    scores = after((scores_0, scores_1), *grads_0)
    message = bias_message(scores, by_slot, columns)
    total = sum_levels(parts_0 + parts_1, message)
    finished = spread_sums(total)
    grad_first, ended = after((grad_first, ended), total)
    grad_tokens = leave_windows(grad_first, even)
    output = leave_windows(ended, even)

    grad_qkv, grad_out_weight, bias_rows = run_finish(order, finished, width, local)
    grad_qkv = grad_qkv.transpose(0, 2, 1, 3)
    grad_bias = bias_rows.reshape(-1)[: BLOCKS * 2 * slots].reshape(BLOCKS, 2, slots)
    return (output[None], grad_tokens[None], grad_qkv, grad_out_weight, grad_bias)


def solution(mesh):
    placed = (
        P("lev", "lat", "lon", None),
        P(),
        P(None, None, None, "lev"),
        P(None, "lev", None),
        P(None, "lev", None),
        P(),
        P("lat", "lon"),
        P("lat"),
        P("lev", "lat", "lon", None),
    )
    return jax.shard_map(
        on_device,
        mesh=mesh,
        in_specs=placed,
        out_specs=(
            P("lev", "lat", "lon", None),
            P("lev", "lat", "lon", None),
            P(None, None, None, "lev"),
            P(None, "lev", None),
            P(None, "lev", None),
        ),
        check_vma=False,
    )
```
